32 devices in a mesh: seq: 8 (over z, x), fsdp: 4 (over y, core).
Axes of the slice: x: 2, y: 2, z: 4, core: 2. Of those that a mesh axis runs over, the one named last changes fastest.
Arguments:
- tokens: bfloat16 [8, 1024, 1024], P('fsdp', 'seq'), may hold values from -6 to 6
- resets: int32 [8, 1024], P('fsdp', 'seq'), may hold values 0 or 1
- pre_gain: float32 [1024], replicated, may hold values from 0.5 to 1.5
- query_weight: bfloat16 [1024, 1024], P('fsdp'), may hold values from -0.1875 to 0.1875
- key_weight: bfloat16 [1024, 1024], P('fsdp'), may hold values from -0.1875 to 0.1875
- value_weight: bfloat16 [1024, 1024], P('fsdp'), may hold values from -0.1875 to 0.1875
- forget_weight: bfloat16 [1024, 256], P('fsdp'), may hold values from -0.1875 to 0.1875
- forget_bias: float32 [256], replicated, may hold values from -1 to 9
- outgate_weight: bfloat16 [1024, 1024], P('fsdp'), may hold values from -0.1875 to 0.1875
- output_weight: bfloat16 [1024, 1024], P('fsdp'), may hold values from -0.1875 to 0.1875
- head_gain: float32 [256], replicated, may hold values from 0.5 to 1.5
- post_gain: float32 [1024], replicated, may hold values from 0.5 to 1.5
- gate_weight: bfloat16 [1024, 2816], P('fsdp'), may hold values from -0.1875 to 0.1875
- up_weight: bfloat16 [1024, 2816], P('fsdp'), may hold values from -0.1875 to 0.1875
- down_weight: bfloat16 [2816, 1024], P('fsdp'), may hold values from -0.109375 to 0.109375
- cotangent: bfloat16 [8, 1024, 1024], P('fsdp', 'seq'), may hold values from -6 to 6
Outputs:
- block_output: bfloat16 [8, 1024, 1024], P('fsdp', 'seq')
- input_grad: bfloat16 [8, 1024, 1024], P('fsdp', 'seq')
- pregain_grad: float32 [1024], replicated
- query_grad: float32 [1024, 1024], P(('seq', 'fsdp'))
- key_grad: float32 [1024, 1024], P(('seq', 'fsdp'))
- value_grad: float32 [1024, 1024], P(('seq', 'fsdp'))
- forget_grad: float32 [1024, 256], P(('seq', 'fsdp'))
- bias_grad: float32 [256], replicated
- outgate_grad: float32 [1024, 1024], P(('seq', 'fsdp'))
- output_grad: float32 [1024, 1024], P(('seq', 'fsdp'))
- headgain_grad: float32 [256], replicated
- postgain_grad: float32 [1024], replicated
- gate_grad: float32 [1024, 2816], P(('seq', 'fsdp'))
- up_grad: float32 [1024, 2816], P(('seq', 'fsdp'))
- down_grad: float32 [2816, 1024], P(('seq', 'fsdp'))
The draws below stay inside these ranges and needn't reach their ends.
Inputs may be any that keep to these rules, and one draw needn't show every extreme that they name: `resets`: 1 marks the first position of a document; documents may cross devices and span many of them.
All inputs are finite; a program needn't handle non-finite values.
Results may differ from the reference program's by a relative error of at most 0.015.
Values may be sent and summed in bfloat16 or wider, within the bound.
A program may use at most 120 MiB of HBM per device.

```python
import jax
import jax.numpy as jnp
from jax import lax

D = 1024
HEADS = 4
HEAD = 256
SLOTS = 64
FF = 2816
GROUP = 64
TOK_DEV = 128
LENGTH = 1024
STREAMS = 8


def place_ends(entries, own_key, low, largest):
    place = [jax.random.randint(jax.random.fold_in(own_key, axis), (), 0, length) for axis, length in enumerate(entries.shape)]
    widest = entries.shape.index(max(entries.shape))
    neighbour = place[:widest] + [(place[widest] + 1) % entries.shape[widest]] + place[widest + 1:]
    return entries.at[tuple(place)].set(low).at[tuple(neighbour)].set(largest)


def block_scale(key, extent, split, low, top_value):
    def one(position, parts):
        steps = jax.random.uniform(jax.random.fold_in(jax.random.fold_in(key, 6), position), (parts,), jnp.float32, low / len(split), top_value / len(split))
        return jnp.repeat(jnp.exp(steps), extent[position] // parts).reshape((-1,) + (1,) * (len(extent) - position - 1))

    level = one(*split[0])
    for cut in split[1:]:
        level = level * one(*cut)
    return level


def noise(own_key, shape, width, limit, pieces=(), kind=jnp.bfloat16):
    entries = jax.random.normal(own_key, shape, jnp.float32) * width
    if len(pieces) > 0:
        entries = block_scale(own_key, shape, pieces, -0.22, 0.18) * entries
    return jnp.clip(entries, min=-limit, max=limit).astype(kind)


def setup_inputs(seed: int = 0) -> dict:
    seeds = jax.random.split(jax.random.key(seed), 17)
    return {
        "tokens": noise(seeds[0], (STREAMS, LENGTH, D), 1.0, 6.0, ((0, 4), (1, 8))),
        "resets": place_ends((jax.random.randint(seeds[1], (STREAMS, LENGTH), 0, 4 * TOK_DEV) < 1).astype(jnp.int32), jax.random.fold_in(seeds[1], 1), 0, 1),
        "pre_gain": jnp.clip(1.0 + 0.1 * jax.random.normal(seeds[2], (D,), jnp.float32), 0.5, 1.5),
        "query_weight": noise(seeds[3], (D, D), D ** -0.5, 0.1875, ((0, 4),)),
        "key_weight": noise(seeds[4], (D, D), D ** -0.5, 0.1875, ((0, 4),)),
        "value_weight": noise(seeds[5], (D, D), D ** -0.5, 0.1875, ((0, 4),)),
        "forget_weight": noise(seeds[6], (D, HEADS * SLOTS), D ** -0.5, 0.1875, ((0, 4),)),
        "forget_bias": jnp.clip(jax.random.uniform(seeds[7], (HEADS * SLOTS,), jnp.float32, -1.0, 9.0), -1.0, 9.0),
        "outgate_weight": noise(seeds[8], (D, D), D ** -0.5, 0.1875, ((0, 4),)),
        "output_weight": noise(seeds[9], (D, D), D ** -0.5, 0.1875, ((0, 4),)),
        "head_gain": jnp.clip(1.0 + 0.1 * jax.random.normal(seeds[10], (HEAD,), jnp.float32), 0.5, 1.5),
        "post_gain": jnp.clip(1.0 + 0.1 * jax.random.normal(seeds[11], (D,), jnp.float32), 0.5, 1.5),
        "gate_weight": noise(seeds[12], (D, FF), D ** -0.5, 0.1875, ((0, 4),)),
        "up_weight": noise(seeds[13], (D, FF), D ** -0.5, 0.1875, ((0, 4),)),
        "down_weight": noise(seeds[14], (FF, D), FF ** -0.5, 0.109375, ((0, 4),)),
        "cotangent": noise(seeds[15], (STREAMS, LENGTH, D), 1.0, 6.0, ((0, 4), (1, 8))),
    }


highest = lax.Precision.HIGHEST
norm_eps = 1e-06
gate_scale = 8.0

@jax.custom_vjp
def low(v):
    return lax.optimization_barrier(v.astype(jnp.bfloat16)).astype(jnp.float32)

@jax.custom_vjp
def low_back(v):
    return v

def low_keep(v):
    return (low(v), None)

def low_pass(kept, grad):
    return (grad,)

def back_keep(v):
    return (v, None)

def back_low(kept, grad):
    return (low(grad),)
low.defvjp(low_keep, low_pass)
low_back.defvjp(back_keep, back_low)

def rms_norm(values, gain):
    return values * lax.rsqrt(lax.optimization_barrier(jnp.mean(values * values, axis=-1, keepdims=True)) + norm_eps) * gain

def slot_block(carry, block):
    key_state, value_state = carry
    queries, keys_in, values_in, log_gates, flags = block
    scale = queries.shape[-1] ** (-0.5)
    length = queries.shape[0]
    decay_sum = jnp.cumsum(log_gates, axis=0)
    resets_seen = jnp.cumsum(flags)
    places = jnp.arange(length)
    linked = ((resets_seen[:, None] == resets_seen[None, :]) & (places[:, None] >= places[None, :])).astype(jnp.float32)
    fresh = (resets_seen == 0).astype(jnp.float32)
    ending = (resets_seen == resets_seen[-1]).astype(jnp.float32)
    growth = jnp.exp(decay_sum)
    shrink = jnp.exp(-decay_sum) * -jnp.expm1(log_gates)
    affinity = jnp.einsum('thd,shd->hts', queries, keys_in, precision=highest) * (scale * linked)[None]
    inner = jnp.einsum('hts,shi->thi', affinity, shrink, precision=highest)
    carried = jnp.einsum('thd,hid->thi', queries, key_state, precision=highest) * (scale * fresh)[:, None, None]
    scores = growth * (inner + carried)
    weights = jax.nn.softmax(scores, axis=-1)
    lifted = weights * growth
    mixing = jnp.einsum('thi,shi->hts', lifted, shrink, precision=highest) * linked[None]
    outputs = jnp.einsum('hts,shd->thd', mixing, values_in, precision=highest)
    outputs = outputs + jnp.einsum('thi,hid->thd', lifted, value_state, precision=highest) * fresh[:, None, None]
    last_growth = growth[-1][:, :, None]
    kept = shrink * ending[:, None, None]
    key_next = last_growth * (fresh[-1] * key_state + jnp.einsum('shi,shd->hid', kept, keys_in, precision=highest))
    value_next = last_growth * (fresh[-1] * value_state + jnp.einsum('shi,shd->hid', kept, values_in, precision=highest))
    return ((key_next, value_next), outputs)

def split_blocks(array):
    count = array.shape[0] // GROUP
    return array.reshape((count, GROUP) + array.shape[1:])

def slot_attention(queries, keys_in, values_in, log_gates, flags, key_state, value_state):
    blocks = (split_blocks(queries), split_blocks(keys_in), split_blocks(values_in), split_blocks(log_gates), split_blocks(flags))
    final, outputs = lax.scan(jax.checkpoint(slot_block), (key_state, value_state), blocks)
    return (outputs.reshape(queries.shape), final)

def forward(params, inputs, flags):
    pre_gain, query_weight, key_weight, value_weight, forget_weight, forget_bias, outgate_weight, output_weight, head_gain, post_gain, gate_weight, up_weight, down_weight = params
    length = inputs.shape[0]
    heads = D // HEAD
    normed = low(rms_norm(inputs, pre_gain))

    def project(weight):
        return jnp.dot(normed, weight, precision=highest)
    queries = low(low_back(project(query_weight))).reshape(length, heads, HEAD)
    keys_in = low(low_back(project(key_weight))).reshape(length, heads, HEAD)
    values_in = low(low_back(project(value_weight))).reshape(length, heads, HEAD)
    log_gates = (jax.nn.log_sigmoid(low_back(project(forget_weight)) + forget_bias) / gate_scale).reshape(length, heads, SLOTS)
    gate_logits = low_back(project(outgate_weight))
    zeros = jnp.zeros((heads, SLOTS, HEAD), jnp.float32)
    mixed, final = slot_attention(queries, keys_in, values_in, log_gates, flags, zeros, zeros)
    merged = low(rms_norm(mixed, head_gain).reshape(length, D) * jax.nn.silu(gate_logits))
    hidden_one = inputs + low_back(jnp.dot(merged, output_weight, precision=highest))
    normed_two = low(rms_norm(hidden_one, post_gain))
    gate_vals = low_back(jnp.dot(normed_two, gate_weight, precision=highest))
    up_vals = low_back(jnp.dot(normed_two, up_weight, precision=highest))
    hidden = low(jax.nn.silu(gate_vals) * up_vals)
    return hidden_one + low_back(jnp.dot(hidden, down_weight, precision=highest))

def reference(tokens, resets, pre_gain, query_weight, key_weight, value_weight, forget_weight, forget_bias, outgate_weight, output_weight, head_gain, post_gain, gate_weight, up_weight, down_weight, cotangent):
    params = tuple((member.astype(jnp.float32) for member in (pre_gain, query_weight, key_weight, value_weight, forget_weight, forget_bias, outgate_weight, output_weight, head_gain, post_gain, gate_weight, up_weight, down_weight)))
    zero_grads = jax.tree.map(jnp.zeros_like, params)

    def one_stream(totals, items):
        stream_tokens, stream_flags, stream_cot = items

        def inner(weights, values):
            return forward(weights, values, stream_flags)
        outputs, pullback = jax.vjp(inner, params, stream_tokens.astype(jnp.float32))
        weight_grads, token_grads = pullback(stream_cot.astype(jnp.float32))
        totals = jax.tree.map(jnp.add, totals, weight_grads)
        return (totals, (outputs.astype(jnp.bfloat16), token_grads.astype(jnp.bfloat16)))
    totals, (block_output, input_grad) = lax.scan(one_stream, zero_grads, (tokens, resets, cotangent))
    return (block_output, input_grad, totals[0], totals[1], totals[2], totals[3], totals[4], totals[5], totals[6], totals[7], totals[8], totals[9], totals[10], totals[11], totals[12])
```

```python
import functools

import jax
import jax.numpy as jnp
from jax import lax
from jax.experimental import pallas as pl
from jax.experimental.pallas import tpu as pltpu
from jax.sharding import PartitionSpec as P

BLOCK = 64
norm_eps = 1e-06
f32, bf16 = jnp.float32, jnp.bfloat16
MESH = pl.DeviceIdType.MESH
VMEM = pltpu.VMEM
ANY = pl.ANY
LIMIT = 60 * 2**20


def in_vmem():
    return pl.BlockSpec(memory_space=VMEM)


def in_place():
    return pl.BlockSpec(memory_space=ANY)


def greet(partners):
    barrier = pltpu.get_barrier_semaphore()
    for partner in partners:
        pl.semaphore_signal(barrier, inc=1, device_id=partner, device_id_type=MESH)
    pl.semaphore_wait(barrier, len(partners))


def remote(src, dst, sems, index, partner):
    return pltpu.make_async_remote_copy(
        src_ref=src,
        dst_ref=dst,
        send_sem=sems[0].at[index],
        recv_sem=sems[1].at[index],
        device_id=partner,
        device_id_type=MESH,
    )


def gather_kernel(count, *refs):
    shards, wholes = refs[:count], refs[count : 2 * count]
    local, *sems = refs[2 * count :]
    s, f = lax.axis_index("seq"), lax.axis_index("fsdp")
    q = lax.rem(s, 4)
    sib, far, nx, nz = (s, f ^ 1), (s, f ^ 2), (s ^ 1, f), (s ^ 2, f)
    fy = f ^ 2
    greet((sib, far, nx, nz))
    started = []

    def go(copy):
        copy.start()
        started.append(copy)

    def piece(m, owner, which, half=None):
        rows = shards[m].shape[0]
        quarter = rows // 4
        first = (quarter // 2 + 15) // 16 * 16
        start, size = (0, quarter) if half is None else ((0, first), (first, quarter - first))[half]
        return wholes[m].at[owner, pl.ds(pl.multiple_of(which * quarter + start, 16), size)]

    def send(kind, m, part, partner):
        go(remote(part, part, sems, (kind, m), partner))

    def arrived(kind, m, part):
        remote(part, part, sems, (kind, m), sib).wait_recv()

    for m in range(count):
        rows = shards[m].shape[0]
        quarter = rows // 4
        src = shards[m].at[pl.ds(pl.multiple_of(q * quarter, 16), quarter)]
        go(remote(src, piece(m, f, q), sems, (1, m), far))
    own = []
    for m in range(count):
        go(remote(shards[m], wholes[m].at[f], sems, (0, m), sib))
        copy = pltpu.make_async_copy(shards[m], wholes[m].at[f], local.at[m])
        copy.start()
        own.append(copy)
    for step in range(count + 2):
        if step < count:
            m = step
            mine = piece(m, fy, q)
            arrived(1, m, mine)
            send(2, m, mine, nx)
            send(3, m, mine, nz)
            send(6, m, mine, sib)
        if 0 <= step - 1 < count:
            m = step - 1
            from_x, from_z = piece(m, fy, q ^ 1), piece(m, fy, q ^ 2)
            arrived(2, m, from_x)
            send(4, m, piece(m, fy, q ^ 1, 0), nz)
            send(7, m, from_x, sib)
            arrived(3, m, from_z)
            send(5, m, piece(m, fy, q ^ 2, 1), nx)
            send(8, m, from_z, sib)
        if 0 <= step - 2 < count:
            m = step - 2
            for kind, half in ((4, 0), (5, 1)):
                part = piece(m, fy, q ^ 3, half)
                arrived(kind, m, part)
                send(kind + 5, m, part, sib)
    fs = fy ^ 1
    for m in range(count):
        arrived(0, m, wholes[m].at[f ^ 1])
        arrived(6, m, piece(m, fs, q))
        arrived(7, m, piece(m, fs, q ^ 1))
        arrived(8, m, piece(m, fs, q ^ 2))
        arrived(9, m, piece(m, fs, q ^ 3, 0))
        arrived(10, m, piece(m, fs, q ^ 3, 1))
        own[m].wait()
    for copy in started:
        copy.wait_send()


def gather(shards):
    count = len(shards)
    wholes = pl.pallas_call(
        functools.partial(gather_kernel, count),
        name="gather",
        out_shape=[jax.ShapeDtypeStruct((4,) + w.shape, w.dtype) for w in shards],
        in_specs=[in_place()] * count,
        out_specs=[in_place()] * count,
        scratch_shapes=[
            pltpu.SemaphoreType.DMA((count,)),
            pltpu.SemaphoreType.DMA((11, count)),
            pltpu.SemaphoreType.DMA((11, count)),
        ],
        compiler_params=pltpu.CompilerParams(collective_id=1, has_side_effects=True),
    )(*shards)
    return [w.reshape((-1, w.shape[-1])) for w in wholes]


def parts_of(a, count):
    if a.dtype == bf16:
        return [a]
    out = []
    for i in range(count):
        part = a.astype(bf16)
        out.append(part)
        if i + 1 < count:
            a = a - part.astype(f32)
    return out


def dot(a, b, ca=1, cb=0, count=1):
    total = None
    for right in reversed(parts_of(b, count)):
        term = lax.dot_general(
            a.astype(bf16), right, (((ca,), (cb,)), ((), ())), preferred_element_type=f32
        )
        total = term if total is None else total + term
    return total


def to_col(row):
    n = row.shape[1]
    i = lax.broadcasted_iota(jnp.int32, (n, n), 0)
    j = lax.broadcasted_iota(jnp.int32, (n, n), 1)
    return jnp.sum(jnp.where(i == j, jnp.broadcast_to(row, (n, n)), 0.0), axis=1, keepdims=True)


def mask_set(flags_col, flags_row):
    n = flags_col.shape[0]
    i = lax.broadcasted_iota(jnp.int32, (n, n), 0)
    j = lax.broadcasted_iota(jnp.int32, (n, n), 1)
    same = (i // BLOCK) == (j // BLOCK)
    lower = jnp.where(same & (i >= j), 1.0, 0.0)
    block = jnp.where(same, 1.0, 0.0)
    seen_col = dot(lower, flags_col)[:, :1]
    all_col = dot(block, flags_col)[:, :1]
    seen_row = dot(flags_row, lower, 1, 1)[:1, :]
    linked = jnp.where(seen_col == seen_row, lower, 0.0)
    fresh = jnp.where(seen_col == 0.0, 1.0, 0.0)
    ending = jnp.where(seen_col == all_col, 1.0, 0.0)
    unbroken = jnp.where(all_col == 0.0, 1.0, 0.0)
    return lower, linked, fresh, ending, unbroken


def gate_set(pre, bias, lower, ending):
    z = pre + bias
    u = jnp.exp(-jnp.abs(z))
    lp = jnp.where(
        u < 0.02, u * (1.0 - u * (0.5 - u * (1.0 / 3.0 - 0.25 * u))), jnp.log(1.0 + u)
    )
    g = (jnp.minimum(z, 0.0) - lp) * 0.125
    series = 1.0 + g * (1.0 / 7.0)
    for order in (6, 5, 4, 3, 2):
        series = 1.0 + g * (1.0 / order) * series
    oma = jnp.where(g > -0.35, -g * series, 1.0 - jnp.exp(g))
    a = dot(lower, g, count=3)
    n, lanes = a.shape
    last = jnp.concatenate(
        [
            jnp.broadcast_to(a[b * BLOCK + BLOCK - 1 : b * BLOCK + BLOCK], (BLOCK, lanes))
            for b in range(n // BLOCK)
        ],
        axis=0,
    )
    tail = jnp.exp(last - a) * ending
    return z, u, oma, jnp.exp(a), jnp.exp(-a), tail


def rows_of(b):
    return slice(b * BLOCK, (b + 1) * BLOCK)


def passing(growth, unbroken, b, hs):
    last = b * BLOCK + BLOCK - 1
    return to_col(growth[last : last + 1, hs] * unbroken[last : last + 1])


def attend_kernel(
    size, heads, q_ref, k_ref, v_ref, pre_ref, bias_ref, fcol_ref, frow_ref, logit_ref, gain_ref,
    merged_ref, mixed_ref, aff_ref, mixing_ref, weight_ref, inner_ref, state_ref, pass_ref,
    ends, came, going, send_sem, recv_sem,
):
    s, f = lax.axis_index("seq"), lax.axis_index("fsdp")
    right, left = (lax.rem(s + 1, size), f), (lax.rem(s + size - 1, size), f)
    greet((left, right))
    n, width = q_ref.shape
    head = width // heads
    slots = pre_ref.shape[1] // heads
    blocks = n // BLOCK
    streams = 2
    per = blocks // streams
    scale = head ** (-0.5)
    lower, linked, fresh, ending, unbroken = mask_set(fcol_ref[...], frow_ref[...])
    z, u, oma, growth, inverse, tail = gate_set(pre_ref[...], bias_ref[...], lower, ending)
    shrink, kept = inverse * oma, tail * oma

    @pl.when(s == 0)
    def _():
        came[...] = jnp.zeros_like(came)

    for h in range(heads):
        hs, hd = slice(h * slots, (h + 1) * slots), slice(h * head, (h + 1) * head)
        for b in range(blocks):
            part = kept[rows_of(b), hs]
            at = (h * streams + b // per) * per + b % per
            ends[at, :, :head] = dot(part, k_ref[rows_of(b), hd], 0, 0)
            ends[at, :, head:] = dot(part, v_ref[rows_of(b), hd], 0, 0)
            pass_ref[at] = jnp.broadcast_to(passing(growth, unbroken, b, hs), pass_ref.shape[1:])
    sends = []
    for pair in range(heads * streams):
        copy = remote(going.at[pair], came.at[pair], (send_sem, recv_sem), pair, right)

        @pl.when(s > 0)
        def _(copy=copy):
            copy.wait_recv()

        state = came[pair].astype(f32)
        for b in range(per):
            at = pair * per + b
            state_ref[pair, b] = state.astype(bf16)
            state = pass_ref[at][:, :1] * state + ends[at]
        state_ref[pair, per] = state.astype(bf16)
        going[pair] = state.astype(bf16)

        @pl.when(s < size - 1)
        def _(copy=copy):
            copy.start()

        sends.append(copy)
    for h in range(heads):
        hs, hd = slice(h * slots, (h + 1) * slots), slice(h * head, (h + 1) * head)
        gr, sh = growth[:, hs], shrink[:, hs]
        qh, vh = q_ref[:, hd], v_ref[:, hd]
        aff = (dot(qh, k_ref[:, hd], 1, 1) * (linked * scale)).astype(bf16)
        aff_ref[h] = aff
        carried = jnp.concatenate(
            [
                dot(qh[rows_of(b)], state_ref[h * streams + b // per, b % per, :, :head], 1, 1)
                for b in range(blocks)
            ],
            axis=0,
        )
        inner = dot(aff, sh) + carried * (scale * fresh)
        scores = gr * inner
        e = jnp.exp(scores - jnp.max(scores, axis=1, keepdims=True))
        weights = e / jnp.sum(e, axis=1, keepdims=True)
        weight_ref[:, hs] = weights
        inner_ref[:, hs] = inner
        lifted = weights * gr
        mixing = (dot(lifted, sh.astype(bf16), 1, 1) * linked).astype(bf16)
        mixing_ref[h] = mixing
        brought = jnp.concatenate(
            [
                dot(lifted[rows_of(b)], state_ref[h * streams + b // per, b % per, :, head:])
                for b in range(blocks)
            ],
            axis=0,
        )
        mixed = dot(mixing, vh) + brought * fresh
        mixed_ref[:, hd] = mixed
        r = lax.rsqrt(jnp.mean(mixed * mixed, axis=1, keepdims=True) + norm_eps)
        logits = logit_ref[:, hd]
        merged_ref[:, hd] = (
            mixed * r * gain_ref[...] * (logits / (1.0 + jnp.exp(-logits)))
        ).astype(bf16)
    for copy in sends:

        @pl.when(s < size - 1)
        def _(copy=copy):
            copy.wait_send()


def attend(size, heads, q, k, v, pre, bias, fcol, frow, logits, gain):
    n, width = q.shape
    head, slots = width // heads, pre.shape[1] // heads
    pairs, per = heads * 2, n // BLOCK // 2
    return pl.pallas_call(
        functools.partial(attend_kernel, size, heads),
        name="attend",
        out_shape=[
            jax.ShapeDtypeStruct((n, width), bf16),
            jax.ShapeDtypeStruct((n, width), f32),
            jax.ShapeDtypeStruct((heads, n, n), bf16),
            jax.ShapeDtypeStruct((heads, n, n), bf16),
            jax.ShapeDtypeStruct(pre.shape, f32),
            jax.ShapeDtypeStruct(pre.shape, f32),
            jax.ShapeDtypeStruct((pairs, per + 1, slots, 2 * head), bf16),
            jax.ShapeDtypeStruct((pairs * per, slots, 128), f32),
        ],
        in_specs=[in_vmem()] * 9,
        out_specs=[in_vmem()] * 8,
        scratch_shapes=[
            VMEM((pairs * per, slots, 2 * head), f32),
            VMEM((pairs, slots, 2 * head), bf16),
            VMEM((pairs, slots, 2 * head), bf16),
            pltpu.SemaphoreType.DMA((pairs,)),
            pltpu.SemaphoreType.DMA((pairs,)),
        ],
        compiler_params=pltpu.CompilerParams(
            collective_id=2, has_side_effects=True, vmem_limit_bytes=LIMIT
        ),
    )(q, k, v, pre, bias, fcol, frow, logits, gain)


def return_kernel(
    size, heads, q_ref, k_ref, v_ref, pre_ref, bias_ref, fcol_ref, frow_ref, logit_ref, gain_ref,
    mixed_ref, aff_ref, mixing_ref, weight_ref, inner_ref, state_ref, pass_ref, delta_ref,
    q_low, k_low, v_low, forget_low, logit_low, bias_grad, gain_grad,
    owed, came, going, k_acc, v_acc, dmix, da_acc, doma_acc, send_sem, recv_sem,
):
    s, f = lax.axis_index("seq"), lax.axis_index("fsdp")
    right, left = (lax.rem(s + 1, size), f), (lax.rem(s + size - 1, size), f)
    greet((left, right))
    n, width = q_ref.shape
    head = width // heads
    slots = pre_ref.shape[1] // heads
    blocks = n // BLOCK
    streams = 2
    per = blocks // streams
    scale = head ** (-0.5)
    lower, linked, fresh, ending, unbroken = mask_set(fcol_ref[...], frow_ref[...])
    z, u, oma, growth, inverse, tail = gate_set(pre_ref[...], bias_ref[...], lower, ending)
    shrink, kept = inverse * oma, tail * oma

    @pl.when(s == size - 1)
    def _():
        came[...] = jnp.zeros_like(came)

    gain_total = jnp.zeros((1, head), f32)
    for h in range(heads):
        hs, hd = slice(h * slots, (h + 1) * slots), slice(h * head, (h + 1) * head)
        mixed, logits, delta = mixed_ref[:, hd], logit_ref[:, hd], delta_ref[:, hd]
        r = lax.rsqrt(jnp.mean(mixed * mixed, axis=1, keepdims=True) + norm_eps)
        sig = 1.0 / (1.0 + jnp.exp(-logits))
        silu = logits * sig
        unit = mixed * r
        dy = delta * silu
        logit_low[:, hd] = (delta * unit * gain_ref[...] * (sig + silu * (1.0 - sig))).astype(bf16)
        gain_total = gain_total + jnp.sum(dy * unit, axis=0, keepdims=True)
        dy = dy * gain_ref[...]
        dmixed = r * (dy - unit * jnp.mean(unit * dy, axis=1, keepdims=True))
        gr, sh = growth[:, hs], shrink[:, hs].astype(bf16)
        weights, inner = weight_ref[:, hs], inner_ref[:, hs]
        aff, mixing = aff_ref[h], mixing_ref[h]
        qh, kh, vh = q_ref[:, hd], k_ref[:, hd], v_ref[:, hd]
        do = dmixed.astype(bf16)
        lifted = (weights * gr).astype(bf16)
        dm = (dot(do, vh, 1, 1) * linked).astype(bf16)
        v_acc[:, hd] = dot(mixing, do, 0, 0)
        fdo = (dmixed * fresh).astype(bf16)

        def states(b, h=h):
            return state_ref.at[h * streams + b // per, b % per]

        dlift = dot(dm, sh) + jnp.concatenate(
            [dot(fdo[rows_of(b)], states(b)[:, head:], 1, 1) for b in range(blocks)], axis=0
        )
        dsh = dot(dm, lifted, 0, 0)
        dw = dlift * gr
        dsc = weights * (dw - jnp.sum(weights * dw, axis=1, keepdims=True))
        du = dsc * gr
        du_low = du.astype(bf16)
        da = (dot(du_low, sh, 1, 1) * (linked * scale)).astype(bf16)
        dsh = dsh + dot(aff, du_low, 0, 0)
        fdu = (du * (fresh * scale)).astype(bf16)
        q_low[:, hd] = (
            dot(da, kh)
            + jnp.concatenate(
                [dot(fdu[rows_of(b)], states(b)[:, :head]) for b in range(blocks)], axis=0
            )
        ).astype(bf16)
        k_acc[:, hd] = dot(da, qh, 0, 0)
        for b in range(blocks):
            at = (h * streams + b // per) * per + b % per
            owed[at, :, :head] = dot(fdu[rows_of(b)], qh[rows_of(b)], 0, 0)
            owed[at, :, head:] = dot(lifted[rows_of(b)], fdo[rows_of(b)], 0, 0)
        da_acc[:, hs] = lifted.astype(f32) * dlift + du_low.astype(f32) * inner - dsh * sh.astype(f32)
        doma_acc[:, hs] = dsh * inverse[:, hs]
    gain_grad[...] = gain_total
    sends = []
    for pair in range(heads * streams):
        copy = remote(going.at[pair], came.at[pair], (send_sem, recv_sem), pair, left)

        @pl.when(s < size - 1)
        def _(copy=copy):
            copy.wait_recv()

        state = came[pair].astype(f32)
        for b in reversed(range(per)):
            at = pair * per + b
            before = owed[at] + pass_ref[at][:, :1] * state
            owed[at] = state
            state = before
        going[pair] = state.astype(bf16)

        @pl.when(s > 0)
        def _(copy=copy):
            copy.start()

        sends.append(copy)
    row = lax.broadcasted_iota(jnp.int32, (BLOCK, 1), 0)
    for h in range(heads):
        hs, hd = slice(h * slots, (h + 1) * slots), slice(h * head, (h + 1) * head)
        for b in range(blocks):
            rb = rows_of(b)
            pair = h * streams + b // per
            at = pair * per + b % per
            leaving = owed[at]
            low = leaving.astype(bf16)
            part = kept[rb, hs].astype(bf16)
            dkept = dot(k_ref[rb, hd], low[:, :head], 1, 1) + dot(v_ref[rb, hd], low[:, head:], 1, 1)
            k_low[rb, hd] = (k_acc[rb, hd] + dot(part, low[:, :head])).astype(bf16)
            v_low[rb, hd] = (v_acc[rb, hd] + dot(part, low[:, head:])).astype(bf16)
            held = jnp.sum(low.astype(f32) * state_ref[pair, b % per + 1].astype(f32), axis=1, keepdims=True)
            held_row = to_row(held)
            da_acc[rb, hs] = (
                da_acc[rb, hs] - dkept * part.astype(f32) + jnp.where(row == BLOCK - 1, held_row, 0.0)
            )
            doma_acc[rb, hs] = doma_acc[rb, hs] + dkept * tail[rb, hs]
    dg = dot(lower, da_acc[...], 0, 0, count=3) - doma_acc[...] * (1.0 - oma)
    sig = jnp.where(z >= 0.0, u / (1.0 + u), 1.0 / (1.0 + u))
    dpre = dg * sig * 0.125
    forget_low[...] = dpre.astype(bf16)
    bias_grad[...] = jnp.sum(dpre, axis=0, keepdims=True)
    for copy in sends:

        @pl.when(s > 0)
        def _(copy=copy):
            copy.wait_send()


def to_row(col):
    n = col.shape[0]
    i = lax.broadcasted_iota(jnp.int32, (n, n), 0)
    j = lax.broadcasted_iota(jnp.int32, (n, n), 1)
    return jnp.sum(jnp.where(i == j, jnp.broadcast_to(col, (n, n)), 0.0), axis=0, keepdims=True)


def go_back(size, heads, q, k, v, pre, bias, fcol, frow, logits, gain, kept, delta):
    n, width = q.shape
    head, slots = width // heads, pre.shape[1] // heads
    pairs, per = heads * 2, n // BLOCK // 2
    return pl.pallas_call(
        functools.partial(return_kernel, size, heads),
        name="go_back",
        out_shape=[
            jax.ShapeDtypeStruct((n, width), bf16),
            jax.ShapeDtypeStruct((n, width), bf16),
            jax.ShapeDtypeStruct((n, width), bf16),
            jax.ShapeDtypeStruct(pre.shape, bf16),
            jax.ShapeDtypeStruct((n, width), bf16),
            jax.ShapeDtypeStruct((1, pre.shape[1]), f32),
            jax.ShapeDtypeStruct((1, head), f32),
        ],
        in_specs=[in_vmem()] * 17,
        out_specs=[in_vmem()] * 7,
        scratch_shapes=[
            VMEM((pairs * per, slots, 2 * head), f32),
            VMEM((pairs, slots, 2 * head), bf16),
            VMEM((pairs, slots, 2 * head), bf16),
            VMEM((n, width), f32),
            VMEM((n, width), f32),
            VMEM((8, 128), f32),
            VMEM(pre.shape, f32),
            VMEM(pre.shape, f32),
            pltpu.SemaphoreType.DMA((pairs,)),
            pltpu.SemaphoreType.DMA((pairs,)),
        ],
        compiler_params=pltpu.CompilerParams(
            collective_id=3, has_side_effects=True, vmem_limit_bytes=LIMIT
        ),
    )(q, k, v, pre, bias, fcol, frow, logits, gain, *kept, delta)


TILE = 256


def cut(columns, flip):
    tiles = columns // TILE
    if tiles <= 1:
        half = columns // 2
        return [(0, half, flip), (half, half, 1 - flip)]
    pieces = 2 if tiles <= 4 else 4
    out, start = [], 0
    for i in range(pieces):
        count = tiles // pieces + (1 if i < tiles % pieces else 0)
        out.append((start, count * TILE, (i + flip) % 2))
        start += count * TILE
    return out


def sum_kernel(lo, plan, n_left, n_right, *refs):
    zs = lo // 2
    lefts, refs = refs[:n_left], refs[n_left:]
    rights, refs = refs[:n_right], refs[n_right:]
    vec_in, refs = refs[0], refs[1:]
    outs, refs = refs[: len(plan)], refs[len(plan) :]
    vec_out, refs = refs[0], refs[1:]
    left_all, refs = refs[:n_left], refs[n_left:]
    right_all, refs = refs[:n_right], refs[n_right:]
    chunks = [(g,) + c for g, p in enumerate(plan) for c in p[5]]
    nc = len(chunks)
    sums, refs = refs[:nc], refs[nc:]
    first, refs = refs[:nc], refs[nc:]
    second, refs = refs[:nc], refs[nc:]
    third, refs = refs[:nc], refs[nc:]
    vec_acc, vec_got, local, in_send, in_recv, st_send, st_recv, z_send, z_recv, v_send, v_recv = refs
    s, f = lax.axis_index("seq"), lax.axis_index("fsdp")
    core, y = lax.rem(f, 2), f // 2
    low = lax.rem(s, lo)
    base = s - low
    x, z = lax.rem(low, 2), low // 2
    sib, far, nx = (s, f ^ 1), (s, f ^ 2), (s ^ 1, f)
    nz = [(base + lax.rem(z + d, zs) * 2 + x, f) for d in range(1, zs)]
    greet([sib, far, nx] + nz)
    started, own = [], []

    def go(copy):
        copy.start()
        started.append(copy)

    tokens = rights[0].shape[0]
    waiting = {}

    def exchange(kind, i):
        index = i if kind == 0 else n_left + i
        if (kind, i) in waiting:
            return
        if kind == 0:
            src_own, src_far = lefts[i].at[core], lefts[i].at[1 - core]
            dst_own, dst_far = left_all[i].at[:, pl.ds(0, tokens)], left_all[i].at[:, pl.ds(tokens, tokens)]
        else:
            src_own = src_far = rights[i]
            dst_own, dst_far = right_all[i].at[pl.ds(0, tokens)], right_all[i].at[pl.ds(tokens, tokens)]
        keep = pltpu.make_async_copy(src_own, dst_own, local.at[index])
        keep.start()
        copy = remote(src_far, dst_far, (in_send, in_recv), index, sib)
        go(copy)
        waiting[kind, i] = [keep, copy]

    def have(kind, i):
        pair = waiting[kind, i]
        if pair:
            pair[0].wait()
            pair[1].wait_recv()
            waiting[kind, i] = None

    for left, right, *_ in plan:
        exchange(0, left)
        exchange(1, right)

    def stage_copy(c, stage):
        order = chunks[c][3]
        ours, theirs = (y, 1 - y), (x, 1 - x)
        if stage == 0:
            other = (theirs if order else ours)[1]
            return remote(sums[c].at[other], first[c], (st_send, st_recv), (0, c), nx if order else far)
        if order:
            src = sums[c].at[x, 1 - y]
        else:
            src = sums[c].at[y, 1 - x]
        return remote(src, second[c], (st_send, st_recv), (1, c), far if order else nx)

    def z_copy(c, d):
        order = chunks[c][3]
        a, b = (x, y) if order else (y, x)
        src = sums[c].at[a, b, lax.rem(z + d, zs)]
        return remote(src, third[c].at[d - 1], (z_send, z_recv), (d - 1, c), nz[d - 1])

    def produce(c):
        g, start, width, order = chunks[c]
        left, right, columns, rows, kept, _ = plan[g]
        have(0, left)
        have(1, right)
        tile = min(TILE, width)

        def body(i, carry):
            at = pl.multiple_of(start + i * tile, 128)
            to = pl.multiple_of(i * tile, 128)
            got = jnp.dot(
                left_all[left][...], right_all[right][:, pl.ds(at, tile)], preferred_element_type=f32
            ).astype(bf16)
            for zz in range(zs):
                for xx in range(2):
                    for yy in range(2):
                        group = (zz * 2 + xx) * 2 + yy
                        a, b = (xx, yy) if order else (yy, xx)
                        sums[c][a, b, zz, :, pl.ds(to, tile)] = got[group * rows : (group + 1) * rows]
            return carry

        lax.fori_loop(0, width // tile, body, 0)
        go(stage_copy(c, 0))

    def after_first(c):
        order = chunks[c][3]
        stage_copy(c, 0).wait_recv()
        a = x if order else y
        for b in range(2):
            for zz in range(zs):
                sums[c][a, b, zz] = (
                    sums[c][a, b, zz].astype(f32) + first[c][b, zz].astype(f32)
                ).astype(bf16)
        go(stage_copy(c, 1))

    def after_second(c):
        order = chunks[c][3]
        stage_copy(c, 1).wait_recv()
        a, b = (x, y) if order else (y, x)
        for zz in range(zs):
            sums[c][a, b, zz] = (
                sums[c][a, b, zz].astype(f32) + second[c][zz].astype(f32)
            ).astype(bf16)
        for d in range(1, zs):
            go(z_copy(c, d))

    def after_third(c):
        g, start, width, order = chunks[c]
        kept = plan[g][4]
        a, b = (x, y) if order else (y, x)
        total = sums[c][a, b, z].astype(f32)
        for d in range(1, zs):
            z_copy(c, d).wait_recv()
            total = total + third[c][d - 1].astype(f32)
        outs[g][:, start : start + width] = total[:kept]

    def vector(step):
        if step == 0:
            vec_acc[0] = vec_in[...]
        elif step <= 3:
            v_copy(step - 1).wait_recv()
            vec_acc[step] = vec_acc[step - 1] + vec_got[step - 1]
        else:
            total = vec_acc[3]
            for d in range(1, zs):
                v_copy(2 + d).wait_recv()
                total = total + vec_got[2 + d]
            vec_out[...] = total
        if step < 3:
            go(v_copy(step))
        elif step == 3:
            for d in range(1, zs):
                go(v_copy(2 + d))

    def v_copy(i):
        partner = (sib, far, nx)[i] if i < 3 else nz[i - 3]
        return remote(vec_acc.at[min(i, 3)], vec_got.at[i], (v_send, v_recv), i, partner)

    lag = 2
    steps = nc + 3 * lag
    for t in range(steps):
        if t < nc:
            produce(t)
        if 0 <= t - lag < nc:
            after_first(t - lag)
        if 0 <= t - 2 * lag < nc:
            after_second(t - 2 * lag)
        if 0 <= t - 3 * lag < nc:
            after_third(t - 3 * lag)
        if steps - 7 <= t < steps - 2:
            vector(t - (steps - 7))
    for copy in started:
        copy.wait_send()


def sum_grads(lo, plan, lefts, rights, vectors):
    zs = lo // 2
    tokens = rights[0].shape[0]
    chunks = [(p[3],) + c for p in plan for c in p[5]]
    nc = len(chunks)
    dma = pltpu.SemaphoreType.DMA
    n_in = len(lefts) + len(rights)
    scratch = [VMEM((a.shape[1], 2 * tokens), bf16) for a in lefts]
    scratch += [VMEM((2 * tokens, b.shape[1]), bf16) for b in rights]
    scratch += [VMEM((2, 2, zs, r, w), bf16) for r, _, w, _ in chunks]
    scratch += [VMEM((2, zs, r, w), bf16) for r, _, w, _ in chunks]
    scratch += [VMEM((zs, r, w), bf16) for r, _, w, _ in chunks]
    scratch += [VMEM((zs - 1, r, w), bf16) for r, _, w, _ in chunks]
    scratch += [
        VMEM((4,) + vectors.shape, f32),
        VMEM((2 + zs,) + vectors.shape, f32),
        dma((n_in,)),
        dma((n_in,)),
        dma((n_in,)),
        dma((2, nc)),
        dma((2, nc)),
        dma((zs - 1, nc)),
        dma((zs - 1, nc)),
        dma((2 + zs,)),
        dma((2 + zs,)),
    ]
    out = pl.pallas_call(
        functools.partial(sum_kernel, lo, plan, len(lefts), len(rights)),
        name="sum_grads",
        out_shape=[jax.ShapeDtypeStruct((p[4], p[2]), f32) for p in plan]
        + [jax.ShapeDtypeStruct(vectors.shape, f32)],
        in_specs=[in_place()] * n_in + [in_vmem()],
        out_specs=[in_vmem()] * (len(plan) + 1),
        scratch_shapes=scratch,
        compiler_params=pltpu.CompilerParams(
            collective_id=4, has_side_effects=True, vmem_limit_bytes=LIMIT
        ),
    )(*lefts, *rights, vectors)
    return out[:-1], out[-1]


def rms_norm(values, gain):
    return values * lax.rsqrt(jnp.mean(values * values, axis=-1, keepdims=True) + norm_eps) * gain


def fore_dot(left, right):
    return jnp.dot(left, right, preferred_element_type=f32)


def back_dot(left, right):
    return lax.dot_general(left, right, (((1,), (1,)), ((), ())), preferred_element_type=f32)


def gated_unit(gate_vals, up_vals):
    return jax.nn.silu(gate_vals) * up_vals


def by_owner(a, hi, lo):
    tokens, features = a.shape
    r = features // (hi * lo * 4)
    t = a.reshape(tokens, hi, lo, 2, 2, r).transpose(4, 2, 3, 1, 5, 0).reshape(2, lo * 2, hi * r, tokens)
    pad = -(hi * r) % 16
    if pad:
        t = jnp.pad(t, ((0, 0), (0, 0), (0, pad), (0, 0)))
    return t.reshape(2, -1, tokens)


def body(
    size, tokens, resets, pre_gain, query_weight, key_weight, value_weight, forget_weight, forget_bias,
    outgate_weight, output_weight, head_gain, post_gain, gate_weight, up_weight, down_weight, cotangent,
):
    lo = 8 if size % 8 == 0 else size
    hi = size // lo
    streams, length, width = tokens.shape
    n = streams * length
    head = head_gain.shape[0]
    heads = width // head
    (wq, wk, wv, wf, wg, wo, w_gate, w_up, w_down) = gather(
        (
            query_weight, key_weight, value_weight, forget_weight, outgate_weight, output_weight,
            gate_weight, up_weight, down_weight,
        )
    )
    inputs = tokens.reshape(n, width).astype(f32)
    cotan = cotangent.reshape(n, width)
    flags = resets.reshape(n).astype(f32)
    fcol = jnp.broadcast_to(flags[:, None], (n, 128))
    frow = jnp.broadcast_to(flags[None], (8, n))
    bias, gain = forget_bias[None], head_gain[None]
    normed_full, norm_back = jax.vjp(rms_norm, inputs, pre_gain)
    normed = normed_full.astype(bf16)
    q = fore_dot(normed, wq).astype(bf16)
    k = fore_dot(normed, wk).astype(bf16)
    v = fore_dot(normed, wv).astype(bf16)
    pre = fore_dot(normed, wf)
    logits = fore_dot(normed, wg)
    merged, *kept = attend(size, heads, q, k, v, pre, bias, fcol, frow, logits, gain)
    hidden_one = inputs + fore_dot(merged, wo)
    normed_second, second_back = jax.vjp(rms_norm, hidden_one, post_gain)
    normed_two = normed_second.astype(bf16)
    gate_vals = fore_dot(normed_two, w_gate)
    up_vals = fore_dot(normed_two, w_up)
    hidden_full, unit_back = jax.vjp(gated_unit, gate_vals, up_vals)
    hidden = hidden_full.astype(bf16)
    block_output = (hidden_one + fore_dot(hidden, w_down)).astype(bf16)
    hidden_delta = back_dot(cotan, w_down)
    gate_full, up_full = unit_back(hidden_delta)
    gate_delta = gate_full.astype(bf16)
    up_delta = up_full.astype(bf16)
    second_delta = back_dot(gate_delta, w_gate) + back_dot(up_delta, w_up)
    through_norm, postgain_grad = second_back(second_delta)
    first_delta = cotan.astype(f32) + through_norm
    attn_delta = first_delta.astype(bf16)
    merged_delta = back_dot(attn_delta, wo)
    q_low, k_low, v_low, forget_low, logit_low, bias_grad, headgain_grad = go_back(
        size, heads, q, k, v, pre, bias, fcol, frow, logits, gain, kept, merged_delta
    )
    normed_delta = (
        back_dot(q_low, wq)
        + back_dot(k_low, wk)
        + back_dot(v_low, wv)
        + back_dot(forget_low, wf)
        + back_dot(logit_low, wg)
    )
    input_delta, pregain_grad = norm_back(normed_delta)
    input_grad = (first_delta + input_delta).astype(bf16)

    order = functools.partial(by_owner, hi=hi, lo=lo)
    lefts = [order(hidden), order(normed_two), order(merged), order(normed)]
    rights = [cotan, gate_delta, up_delta, attn_delta, logit_low, q_low, k_low, v_low, forget_low]
    which = (0, 1, 1, 2, 3, 3, 3, 3, 3)
    features = (hidden.shape[1],) + (width,) * 8
    plan = []
    for i, (left, right) in enumerate(zip(which, rights)):
        kept_rows = features[i] // (lo * 4)
        columns = right.shape[1]
        plan.append((left, i, columns, -(-kept_rows // 16) * 16, kept_rows, tuple(cut(columns, i % 2))))
    sizes = (width, bias.shape[1], head, width)
    vectors = jnp.concatenate([pregain_grad, bias_grad[0], headgain_grad[0], postgain_grad])
    total = vectors.shape[0]
    vectors = jnp.pad(vectors, (0, -total % 1024)).reshape(8, -1)
    grads, vectors = sum_grads(lo, tuple(plan), lefts, rights, vectors)
    if hi > 1:
        alike = [[a * lo + b for a in range(hi)] for b in range(lo)]
        grads = [
            lax.psum_scatter(g, "seq", scatter_dimension=0, axis_index_groups=alike, tiled=True)
            for g in grads
        ]
        vectors = lax.psum(vectors, "seq", axis_index_groups=alike)
    down_grad, gate_grad, up_grad, output_grad, outgate_grad, query_grad, key_grad, value_grad, forget_grad = grads
    vectors = vectors.reshape(-1)
    ends = [sum(sizes[: i + 1]) for i in range(4)]
    pregain, bias_total, headgain, postgain = [vectors[e - w : e] for e, w in zip(ends, sizes)]
    shape = tokens.shape
    return (
        block_output.reshape(shape), input_grad.reshape(shape), pregain, query_grad, key_grad, value_grad,
        forget_grad, bias_total, outgate_grad, output_grad, headgain, postgain, gate_grad, up_grad, down_grad,
    )


def solution(mesh):
    rows, whole, both = P("fsdp", None), P(), P(("seq", "fsdp"), None)
    return jax.shard_map(
        functools.partial(body, mesh.shape["seq"]),
        mesh=mesh,
        in_specs=(
            P("fsdp", "seq", None), P("fsdp", "seq"), whole, rows, rows, rows, rows, whole, rows, rows,
            whole, whole, rows, rows, rows, P("fsdp", "seq", None),
        ),
        out_specs=(
            P("fsdp", "seq", None), P("fsdp", "seq", None), whole, both, both, both, both, whole, both,
            both, whole, whole, both, both, both,
        ),
        check_vma=False,
    )
```

```python
import functools

import jax
import jax.numpy as jnp
from jax import lax
from jax.experimental import pallas as pl
from jax.experimental.pallas import tpu as pltpu
from jax.sharding import PartitionSpec as P

BLOCK = 64
norm_eps = 1e-06
f32, bf16 = jnp.float32, jnp.bfloat16
MESH = pl.DeviceIdType.MESH
VMEM = pltpu.VMEM
ANY = pl.ANY
LIMIT = 60 * 2**20


def in_vmem():
    return pl.BlockSpec(memory_space=VMEM)


def in_place():
    return pl.BlockSpec(memory_space=ANY)


def greet(partners):
    barrier = pltpu.get_barrier_semaphore()
    for partner in partners:
        pl.semaphore_signal(barrier, inc=1, device_id=partner, device_id_type=MESH)
    pl.semaphore_wait(barrier, len(partners))


def remote(src, dst, sems, index, partner):
    return pltpu.make_async_remote_copy(
        src_ref=src,
        dst_ref=dst,
        send_sem=sems[0].at[index],
        recv_sem=sems[1].at[index],
        device_id=partner,
        device_id_type=MESH,
    )


def gather_kernel(count, *refs):
    shards, wholes, held = refs[:count], refs[count : 2 * count], refs[2 * count : 3 * count]
    local, *sems = refs[3 * count :]
    s, f = lax.axis_index("seq"), lax.axis_index("fsdp")
    q = lax.rem(s, 4)
    sib, far, nx, nz = (s, f ^ 1), (s, f ^ 2), (s ^ 1, f), (s ^ 2, f)
    fy = f ^ 2
    greet((sib, far, nx, nz))
    started = []

    def go(copy):
        copy.start()
        started.append(copy)

    def piece(m, owner, which, half=None):
        rows = shards[m].shape[0]
        quarter = rows // 4
        first = (quarter // 2 + 15) // 16 * 16
        start, size = (0, quarter) if half is None else ((0, first), (first, quarter - first))[half]
        return wholes[m].at[owner, pl.ds(pl.multiple_of(which * quarter + start, 16), size)]

    def send(kind, m, part, partner):
        go(remote(part, part, sems, (kind, m), partner))

    def arrived(kind, m, part):
        remote(part, part, sems, (kind, m), sib).wait_recv()

    for m in range(count):
        rows = shards[m].shape[0]
        quarter = rows // 4
        src = shards[m].at[pl.ds(pl.multiple_of(q * quarter, 16), quarter)]
        go(remote(src, piece(m, f, q), sems, (1, m), far))
    own = []
    for m in range(count):
        go(remote(shards[m], wholes[m].at[f], sems, (0, m), sib))
        copy = pltpu.make_async_copy(shards[m], held[m], local.at[0, m])
        copy.start()
        own.append(copy)
    for m in range(count):
        own[m].wait()
        own[m] = pltpu.make_async_copy(held[m], wholes[m].at[f], local.at[1, m])
        own[m].start()
    for step in range(count + 2):
        if step < count:
            m = step
            mine = piece(m, fy, q)
            arrived(1, m, mine)
            send(2, m, mine, nx)
            send(3, m, mine, nz)
            send(6, m, mine, sib)
        if 0 <= step - 1 < count:
            m = step - 1
            from_x, from_z = piece(m, fy, q ^ 1), piece(m, fy, q ^ 2)
            arrived(2, m, from_x)
            send(4, m, piece(m, fy, q ^ 1, 0), nz)
            send(7, m, from_x, sib)
            arrived(3, m, from_z)
            send(5, m, piece(m, fy, q ^ 2, 1), nx)
            send(8, m, from_z, sib)
        if 0 <= step - 2 < count:
            m = step - 2
            for kind, half in ((4, 0), (5, 1)):
                part = piece(m, fy, q ^ 3, half)
                arrived(kind, m, part)
                send(kind + 5, m, part, sib)
    fs = fy ^ 1
    for m in range(count):
        arrived(0, m, wholes[m].at[f ^ 1])
        arrived(6, m, piece(m, fs, q))
        arrived(7, m, piece(m, fs, q ^ 1))
        arrived(8, m, piece(m, fs, q ^ 2))
        arrived(9, m, piece(m, fs, q ^ 3, 0))
        arrived(10, m, piece(m, fs, q ^ 3, 1))
        own[m].wait()
    for copy in started:
        copy.wait_send()


def gather(shards):
    count = len(shards)
    wholes = pl.pallas_call(
        functools.partial(gather_kernel, count),
        name="gather",
        out_shape=[jax.ShapeDtypeStruct((4,) + w.shape, w.dtype) for w in shards],
        in_specs=[in_place()] * count,
        out_specs=[in_place()] * count,
        scratch_shapes=[VMEM(w.shape, w.dtype) for w in shards]
        + [
            pltpu.SemaphoreType.DMA((2, count)),
            pltpu.SemaphoreType.DMA((11, count)),
            pltpu.SemaphoreType.DMA((11, count)),
        ],
        compiler_params=pltpu.CompilerParams(
            collective_id=1, has_side_effects=True, vmem_limit_bytes=LIMIT
        ),
    )(*shards)
    return [w.reshape((-1, w.shape[-1])) for w in wholes]


def parts_of(a, count):
    if a.dtype == bf16:
        return [a]
    out = []
    for i in range(count):
        part = a.astype(bf16)
        out.append(part)
        if i + 1 < count:
            a = a - part.astype(f32)
    return out


def dot(a, b, ca=1, cb=0, count=1):
    total = None
    for right in reversed(parts_of(b, count)):
        term = lax.dot_general(
            a.astype(bf16), right, (((ca,), (cb,)), ((), ())), preferred_element_type=f32
        )
        total = term if total is None else total + term
    return total


def to_col(row):
    n = row.shape[1]
    i = lax.broadcasted_iota(jnp.int32, (n, n), 0)
    j = lax.broadcasted_iota(jnp.int32, (n, n), 1)
    return jnp.sum(jnp.where(i == j, jnp.broadcast_to(row, (n, n)), 0.0), axis=1, keepdims=True)


def mask_set(flags_col, flags_row):
    n = flags_col.shape[0]
    i = lax.broadcasted_iota(jnp.int32, (n, n), 0)
    j = lax.broadcasted_iota(jnp.int32, (n, n), 1)
    same = (i // BLOCK) == (j // BLOCK)
    lower = jnp.where(same & (i >= j), 1.0, 0.0)
    block = jnp.where(same, 1.0, 0.0)
    seen_col = dot(lower, flags_col)[:, :1]
    all_col = dot(block, flags_col)[:, :1]
    seen_row = dot(flags_row, lower, 1, 1)[:1, :]
    linked = jnp.where(seen_col == seen_row, lower, 0.0)
    fresh = jnp.where(seen_col == 0.0, 1.0, 0.0)
    ending = jnp.where(seen_col == all_col, 1.0, 0.0)
    unbroken = jnp.where(all_col == 0.0, 1.0, 0.0)
    return lower, linked, fresh, ending, unbroken


def gate_set(pre, bias, lower, ending):
    z = pre + bias
    u = jnp.exp(-jnp.abs(z))
    lp = jnp.where(
        u < 0.02, u * (1.0 - u * (0.5 - u * (1.0 / 3.0 - 0.25 * u))), jnp.log(1.0 + u)
    )
    g = (jnp.minimum(z, 0.0) - lp) * 0.125
    series = 1.0 + g * (1.0 / 7.0)
    for order in (6, 5, 4, 3, 2):
        series = 1.0 + g * (1.0 / order) * series
    oma = jnp.where(g > -0.35, -g * series, 1.0 - jnp.exp(g))
    a = dot(lower, g, count=3)
    n, lanes = a.shape
    last = jnp.concatenate(
        [
            jnp.broadcast_to(a[b * BLOCK + BLOCK - 1 : b * BLOCK + BLOCK], (BLOCK, lanes))
            for b in range(n // BLOCK)
        ],
        axis=0,
    )
    tail = jnp.exp(last - a) * ending
    return z, u, oma, jnp.exp(a), jnp.exp(-a), tail


def rows_of(b):
    return slice(b * BLOCK, (b + 1) * BLOCK)


def passing(growth, unbroken, b, hs):
    last = b * BLOCK + BLOCK - 1
    return to_col(growth[last : last + 1, hs] * unbroken[last : last + 1])


def attend_kernel(
    size, heads, q_ref, k_ref, v_ref, pre_ref, bias_ref, fcol_ref, frow_ref, logit_ref, gain_ref,
    merged_ref, mixed_ref, aff_ref, mixing_ref, weight_ref, inner_ref, state_ref, pass_ref,
    ends, came, going, send_sem, recv_sem,
):
    s, f = lax.axis_index("seq"), lax.axis_index("fsdp")
    right, left = (lax.rem(s + 1, size), f), (lax.rem(s + size - 1, size), f)
    greet((left, right))
    n, width = q_ref.shape
    head = width // heads
    slots = pre_ref.shape[1] // heads
    blocks = n // BLOCK
    streams = 2
    per = blocks // streams
    scale = head ** (-0.5)
    lower, linked, fresh, ending, unbroken = mask_set(fcol_ref[...], frow_ref[...])
    z, u, oma, growth, inverse, tail = gate_set(pre_ref[...], bias_ref[...], lower, ending)
    shrink, kept = inverse * oma, tail * oma

    @pl.when(s == 0)
    def _():
        came[...] = jnp.zeros_like(came)

    for h in range(heads):
        hs, hd = slice(h * slots, (h + 1) * slots), slice(h * head, (h + 1) * head)
        for b in range(blocks):
            part = kept[rows_of(b), hs]
            at = (h * streams + b // per) * per + b % per
            ends[at, :, :head] = dot(part, k_ref[rows_of(b), hd], 0, 0)
            ends[at, :, head:] = dot(part, v_ref[rows_of(b), hd], 0, 0)
            pass_ref[at] = jnp.broadcast_to(passing(growth, unbroken, b, hs), pass_ref.shape[1:])
    sends = []
    for pair in range(heads * streams):
        copy = remote(going.at[pair], came.at[pair], (send_sem, recv_sem), pair, right)

        @pl.when(s > 0)
        def _(copy=copy):
            copy.wait_recv()

        state = came[pair].astype(f32)
        for b in range(per):
            at = pair * per + b
            state_ref[pair, b] = state.astype(bf16)
            state = pass_ref[at][:, :1] * state + ends[at]
        state_ref[pair, per] = state.astype(bf16)
        going[pair] = state.astype(bf16)

        @pl.when(s < size - 1)
        def _(copy=copy):
            copy.start()

        sends.append(copy)
    for h in range(heads):
        hs, hd = slice(h * slots, (h + 1) * slots), slice(h * head, (h + 1) * head)
        gr, sh = growth[:, hs], shrink[:, hs]
        qh, vh = q_ref[:, hd], v_ref[:, hd]
        aff = (dot(qh, k_ref[:, hd], 1, 1) * (linked * scale)).astype(bf16)
        aff_ref[h] = aff
        carried = jnp.concatenate(
            [
                dot(qh[rows_of(b)], state_ref[h * streams + b // per, b % per, :, :head], 1, 1)
                for b in range(blocks)
            ],
            axis=0,
        )
        inner = dot(aff, sh) + carried * (scale * fresh)
        scores = gr * inner
        e = jnp.exp(scores - jnp.max(scores, axis=1, keepdims=True))
        weights = e / jnp.sum(e, axis=1, keepdims=True)
        weight_ref[:, hs] = weights
        inner_ref[:, hs] = inner
        lifted = weights * gr
        mixing = (dot(lifted, sh.astype(bf16), 1, 1) * linked).astype(bf16)
        mixing_ref[h] = mixing
        brought = jnp.concatenate(
            [
                dot(lifted[rows_of(b)], state_ref[h * streams + b // per, b % per, :, head:])
                for b in range(blocks)
            ],
            axis=0,
        )
        mixed = dot(mixing, vh) + brought * fresh
        mixed_ref[:, hd] = mixed
        r = lax.rsqrt(jnp.mean(mixed * mixed, axis=1, keepdims=True) + norm_eps)
        logits = logit_ref[:, hd]
        merged_ref[:, hd] = (
            mixed * r * gain_ref[...] * (logits / (1.0 + jnp.exp(-logits)))
        ).astype(bf16)
    for copy in sends:

        @pl.when(s < size - 1)
        def _(copy=copy):
            copy.wait_send()


def attend(size, heads, q, k, v, pre, bias, fcol, frow, logits, gain):
    n, width = q.shape
    head, slots = width // heads, pre.shape[1] // heads
    pairs, per = heads * 2, n // BLOCK // 2
    return pl.pallas_call(
        functools.partial(attend_kernel, size, heads),
        name="attend",
        out_shape=[
            jax.ShapeDtypeStruct((n, width), bf16),
            jax.ShapeDtypeStruct((n, width), f32),
            jax.ShapeDtypeStruct((heads, n, n), bf16),
            jax.ShapeDtypeStruct((heads, n, n), bf16),
            jax.ShapeDtypeStruct(pre.shape, f32),
            jax.ShapeDtypeStruct(pre.shape, f32),
            jax.ShapeDtypeStruct((pairs, per + 1, slots, 2 * head), bf16),
            jax.ShapeDtypeStruct((pairs * per, slots, 128), f32),
        ],
        in_specs=[in_vmem()] * 9,
        out_specs=[in_vmem()] * 8,
        scratch_shapes=[
            VMEM((pairs * per, slots, 2 * head), f32),
            VMEM((pairs, slots, 2 * head), bf16),
            VMEM((pairs, slots, 2 * head), bf16),
            pltpu.SemaphoreType.DMA((pairs,)),
            pltpu.SemaphoreType.DMA((pairs,)),
        ],
        compiler_params=pltpu.CompilerParams(
            collective_id=2, has_side_effects=True, vmem_limit_bytes=LIMIT
        ),
    )(q, k, v, pre, bias, fcol, frow, logits, gain)


def return_kernel(
    size, heads, q_ref, k_ref, v_ref, pre_ref, bias_ref, fcol_ref, frow_ref, logit_ref, gain_ref,
    mixed_ref, aff_ref, mixing_ref, weight_ref, inner_ref, state_ref, pass_ref, delta_ref,
    q_low, k_low, v_low, forget_low, logit_low, bias_grad, gain_grad,
    owed, came, going, k_acc, v_acc, dmix, da_acc, doma_acc, send_sem, recv_sem,
):
    s, f = lax.axis_index("seq"), lax.axis_index("fsdp")
    right, left = (lax.rem(s + 1, size), f), (lax.rem(s + size - 1, size), f)
    greet((left, right))
    n, width = q_ref.shape
    head = width // heads
    slots = pre_ref.shape[1] // heads
    blocks = n // BLOCK
    streams = 2
    per = blocks // streams
    scale = head ** (-0.5)
    lower, linked, fresh, ending, unbroken = mask_set(fcol_ref[...], frow_ref[...])
    z, u, oma, growth, inverse, tail = gate_set(pre_ref[...], bias_ref[...], lower, ending)
    shrink, kept = inverse * oma, tail * oma

    @pl.when(s == size - 1)
    def _():
        came[...] = jnp.zeros_like(came)

    gain_total = jnp.zeros((1, head), f32)
    for h in range(heads):
        hs, hd = slice(h * slots, (h + 1) * slots), slice(h * head, (h + 1) * head)
        mixed, logits, delta = mixed_ref[:, hd], logit_ref[:, hd], delta_ref[:, hd]
        r = lax.rsqrt(jnp.mean(mixed * mixed, axis=1, keepdims=True) + norm_eps)
        sig = 1.0 / (1.0 + jnp.exp(-logits))
        silu = logits * sig
        unit = mixed * r
        dy = delta * silu
        logit_low[:, hd] = (delta * unit * gain_ref[...] * (sig + silu * (1.0 - sig))).astype(bf16)
        gain_total = gain_total + jnp.sum(dy * unit, axis=0, keepdims=True)
        dy = dy * gain_ref[...]
        dmixed = r * (dy - unit * jnp.mean(unit * dy, axis=1, keepdims=True))
        gr, sh = growth[:, hs], shrink[:, hs].astype(bf16)
        weights, inner = weight_ref[:, hs], inner_ref[:, hs]
        aff, mixing = aff_ref[h], mixing_ref[h]
        qh, kh, vh = q_ref[:, hd], k_ref[:, hd], v_ref[:, hd]
        do = dmixed.astype(bf16)
        lifted = (weights * gr).astype(bf16)
        dm = (dot(do, vh, 1, 1) * linked).astype(bf16)
        v_acc[:, hd] = dot(mixing, do, 0, 0)
        fdo = (dmixed * fresh).astype(bf16)

        def states(b, h=h):
            return state_ref.at[h * streams + b // per, b % per]

        dlift = dot(dm, sh) + jnp.concatenate(
            [dot(fdo[rows_of(b)], states(b)[:, head:], 1, 1) for b in range(blocks)], axis=0
        )
        dsh = dot(dm, lifted, 0, 0)
        dw = dlift * gr
        dsc = weights * (dw - jnp.sum(weights * dw, axis=1, keepdims=True))
        du = dsc * gr
        du_low = du.astype(bf16)
        da = (dot(du_low, sh, 1, 1) * (linked * scale)).astype(bf16)
        dsh = dsh + dot(aff, du_low, 0, 0)
        fdu = (du * (fresh * scale)).astype(bf16)
        q_low[:, hd] = (
            dot(da, kh)
            + jnp.concatenate(
                [dot(fdu[rows_of(b)], states(b)[:, :head]) for b in range(blocks)], axis=0
            )
        ).astype(bf16)
        k_acc[:, hd] = dot(da, qh, 0, 0)
        for b in range(blocks):
            at = (h * streams + b // per) * per + b % per
            owed[at, :, :head] = dot(fdu[rows_of(b)], qh[rows_of(b)], 0, 0)
            owed[at, :, head:] = dot(lifted[rows_of(b)], fdo[rows_of(b)], 0, 0)
        da_acc[:, hs] = lifted.astype(f32) * dlift + du_low.astype(f32) * inner - dsh * sh.astype(f32)
        doma_acc[:, hs] = dsh * inverse[:, hs]
    gain_grad[...] = gain_total
    sends = []
    for pair in range(heads * streams):
        copy = remote(going.at[pair], came.at[pair], (send_sem, recv_sem), pair, left)

        @pl.when(s < size - 1)
        def _(copy=copy):
            copy.wait_recv()

        state = came[pair].astype(f32)
        for b in reversed(range(per)):
            at = pair * per + b
            before = owed[at] + pass_ref[at][:, :1] * state
            owed[at] = state
            state = before
        going[pair] = state.astype(bf16)

        @pl.when(s > 0)
        def _(copy=copy):
            copy.start()

        sends.append(copy)
    row = lax.broadcasted_iota(jnp.int32, (BLOCK, 1), 0)
    for h in range(heads):
        hs, hd = slice(h * slots, (h + 1) * slots), slice(h * head, (h + 1) * head)
        for b in range(blocks):
            rb = rows_of(b)
            pair = h * streams + b // per
            at = pair * per + b % per
            leaving = owed[at]
            low = leaving.astype(bf16)
            part = kept[rb, hs].astype(bf16)
            dkept = dot(k_ref[rb, hd], low[:, :head], 1, 1) + dot(v_ref[rb, hd], low[:, head:], 1, 1)
            k_low[rb, hd] = (k_acc[rb, hd] + dot(part, low[:, :head])).astype(bf16)
            v_low[rb, hd] = (v_acc[rb, hd] + dot(part, low[:, head:])).astype(bf16)
            held = jnp.sum(low.astype(f32) * state_ref[pair, b % per + 1].astype(f32), axis=1, keepdims=True)
            held_row = to_row(held)
            da_acc[rb, hs] = (
                da_acc[rb, hs] - dkept * part.astype(f32) + jnp.where(row == BLOCK - 1, held_row, 0.0)
            )
            doma_acc[rb, hs] = doma_acc[rb, hs] + dkept * tail[rb, hs]
    dg = dot(lower, da_acc[...], 0, 0, count=3) - doma_acc[...] * (1.0 - oma)
    sig = jnp.where(z >= 0.0, u / (1.0 + u), 1.0 / (1.0 + u))
    dpre = dg * sig * 0.125
    forget_low[...] = dpre.astype(bf16)
    bias_grad[...] = jnp.sum(dpre, axis=0, keepdims=True)
    for copy in sends:

        @pl.when(s > 0)
        def _(copy=copy):
            copy.wait_send()


def to_row(col):
    n = col.shape[0]
    i = lax.broadcasted_iota(jnp.int32, (n, n), 0)
    j = lax.broadcasted_iota(jnp.int32, (n, n), 1)
    return jnp.sum(jnp.where(i == j, jnp.broadcast_to(col, (n, n)), 0.0), axis=0, keepdims=True)


def go_back(size, heads, q, k, v, pre, bias, fcol, frow, logits, gain, kept, delta):
    n, width = q.shape
    head, slots = width // heads, pre.shape[1] // heads
    pairs, per = heads * 2, n // BLOCK // 2
    return pl.pallas_call(
        functools.partial(return_kernel, size, heads),
        name="go_back",
        out_shape=[
            jax.ShapeDtypeStruct((n, width), bf16),
            jax.ShapeDtypeStruct((n, width), bf16),
            jax.ShapeDtypeStruct((n, width), bf16),
            jax.ShapeDtypeStruct(pre.shape, bf16),
            jax.ShapeDtypeStruct((n, width), bf16),
            jax.ShapeDtypeStruct((1, pre.shape[1]), f32),
            jax.ShapeDtypeStruct((1, head), f32),
        ],
        in_specs=[in_vmem()] * 17,
        out_specs=[in_vmem()] * 7,
        scratch_shapes=[
            VMEM((pairs * per, slots, 2 * head), f32),
            VMEM((pairs, slots, 2 * head), bf16),
            VMEM((pairs, slots, 2 * head), bf16),
            VMEM((n, width), f32),
            VMEM((n, width), f32),
            VMEM((8, 128), f32),
            VMEM(pre.shape, f32),
            VMEM(pre.shape, f32),
            pltpu.SemaphoreType.DMA((pairs,)),
            pltpu.SemaphoreType.DMA((pairs,)),
        ],
        compiler_params=pltpu.CompilerParams(
            collective_id=3, has_side_effects=True, vmem_limit_bytes=LIMIT
        ),
    )(q, k, v, pre, bias, fcol, frow, logits, gain, *kept, delta)


TILE = 256


def cut(columns, flip):
    tiles = columns // TILE
    if tiles <= 1:
        half = columns // 2
        return [(0, half, flip), (half, half, 1 - flip)]
    pieces = 2 if tiles <= 4 else 4
    out, start = [], 0
    for i in range(pieces):
        count = tiles // pieces + (1 if i < tiles % pieces else 0)
        out.append((start, count * TILE, (i + flip) % 2))
        start += count * TILE
    return out


def sum_kernel(lo, plan, n_left, n_right, *refs):
    zs = lo // 2
    lefts, refs = refs[:n_left], refs[n_left:]
    rights, refs = refs[:n_right], refs[n_right:]
    vec_in, refs = refs[0], refs[1:]
    outs, refs = refs[: len(plan)], refs[len(plan) :]
    vec_out, refs = refs[0], refs[1:]
    left_all, refs = refs[:n_left], refs[n_left:]
    right_all, refs = refs[:n_right], refs[n_right:]
    chunks = [(g,) + c for g, p in enumerate(plan) for c in p[5]]
    nc = len(chunks)
    sums, refs = refs[:nc], refs[nc:]
    first, refs = refs[:nc], refs[nc:]
    second, refs = refs[:nc], refs[nc:]
    third, refs = refs[:nc], refs[nc:]
    vec_acc, vec_got, local, in_send, in_recv, st_send, st_recv, z_send, z_recv, v_send, v_recv = refs
    s, f = lax.axis_index("seq"), lax.axis_index("fsdp")
    core, y = lax.rem(f, 2), f // 2
    low = lax.rem(s, lo)
    base = s - low
    x, z = lax.rem(low, 2), low // 2
    sib, far, nx = (s, f ^ 1), (s, f ^ 2), (s ^ 1, f)
    nz = [(base + lax.rem(z + d, zs) * 2 + x, f) for d in range(1, zs)]
    greet([sib, far, nx] + nz)
    started, own = [], []

    def go(copy):
        copy.start()
        started.append(copy)

    tokens = rights[0].shape[0]
    waiting = {}

    def exchange(kind, i):
        index = i if kind == 0 else n_left + i
        if (kind, i) in waiting:
            return
        if kind == 0:
            src_own, src_far = lefts[i].at[core], lefts[i].at[1 - core]
            dst_own, dst_far = left_all[i].at[:, pl.ds(0, tokens)], left_all[i].at[:, pl.ds(tokens, tokens)]
        else:
            src_own = src_far = rights[i]
            dst_own, dst_far = right_all[i].at[pl.ds(0, tokens)], right_all[i].at[pl.ds(tokens, tokens)]
        keep = pltpu.make_async_copy(src_own, dst_own, local.at[index])
        keep.start()
        copy = remote(src_far, dst_far, (in_send, in_recv), index, sib)
        go(copy)
        waiting[kind, i] = [keep, copy]

    def have(kind, i):
        pair = waiting[kind, i]
        if pair:
            pair[0].wait()
            pair[1].wait_recv()
            waiting[kind, i] = None

    for left, right, *_ in plan:
        exchange(0, left)
        exchange(1, right)

    def stage_copy(c, stage):
        order = chunks[c][3]
        ours, theirs = (y, 1 - y), (x, 1 - x)
        if stage == 0:
            other = (theirs if order else ours)[1]
            return remote(sums[c].at[other], first[c], (st_send, st_recv), (0, c), nx if order else far)
        if order:
            src = sums[c].at[x, 1 - y]
        else:
            src = sums[c].at[y, 1 - x]
        return remote(src, second[c], (st_send, st_recv), (1, c), far if order else nx)

    def z_copy(c, d):
        order = chunks[c][3]
        a, b = (x, y) if order else (y, x)
        src = sums[c].at[a, b, lax.rem(z + d, zs)]
        return remote(src, third[c].at[d - 1], (z_send, z_recv), (d - 1, c), nz[d - 1])

    def produce(c):
        g, start, width, order = chunks[c]
        left, right, columns, rows, kept, _ = plan[g]
        have(0, left)
        have(1, right)
        tile = min(TILE, width)

        def body(i, carry):
            at = pl.multiple_of(start + i * tile, 128)
            to = pl.multiple_of(i * tile, 128)
            got = jnp.dot(
                left_all[left][...], right_all[right][:, pl.ds(at, tile)], preferred_element_type=f32
            ).astype(bf16)
            for zz in range(zs):
                for xx in range(2):
                    for yy in range(2):
                        group = (zz * 2 + xx) * 2 + yy
                        a, b = (xx, yy) if order else (yy, xx)
                        sums[c][a, b, zz, :, pl.ds(to, tile)] = got[group * rows : (group + 1) * rows]
            return carry

        lax.fori_loop(0, width // tile, body, 0)
        go(stage_copy(c, 0))

    def after_first(c):
        order = chunks[c][3]
        stage_copy(c, 0).wait_recv()
        a = x if order else y
        for b in range(2):
            for zz in range(zs):
                sums[c][a, b, zz] = (
                    sums[c][a, b, zz].astype(f32) + first[c][b, zz].astype(f32)
                ).astype(bf16)
        go(stage_copy(c, 1))

    def after_second(c):
        order = chunks[c][3]
        stage_copy(c, 1).wait_recv()
        a, b = (x, y) if order else (y, x)
        for zz in range(zs):
            sums[c][a, b, zz] = (
                sums[c][a, b, zz].astype(f32) + second[c][zz].astype(f32)
            ).astype(bf16)
        for d in range(1, zs):
            go(z_copy(c, d))

    def after_third(c):
        g, start, width, order = chunks[c]
        kept = plan[g][4]
        a, b = (x, y) if order else (y, x)
        total = sums[c][a, b, z].astype(f32)
        for d in range(1, zs):
            z_copy(c, d).wait_recv()
            total = total + third[c][d - 1].astype(f32)
        outs[g][:, start : start + width] = total[:kept]

    def vector(step):
        if step == 0:
            vec_acc[0] = vec_in[...]
        elif step <= 3:
            v_copy(step - 1).wait_recv()
            vec_acc[step] = vec_acc[step - 1] + vec_got[step - 1]
        else:
            total = vec_acc[3]
            for d in range(1, zs):
                v_copy(2 + d).wait_recv()
                total = total + vec_got[2 + d]
            vec_out[...] = total
        if step < 3:
            go(v_copy(step))
        elif step == 3:
            for d in range(1, zs):
                go(v_copy(2 + d))

    def v_copy(i):
        partner = (sib, far, nx)[i] if i < 3 else nz[i - 3]
        return remote(vec_acc.at[min(i, 3)], vec_got.at[i], (v_send, v_recv), i, partner)

    lag = 2
    steps = nc + 3 * lag
    for t in range(steps):
        if t < nc:
            produce(t)
        if 0 <= t - lag < nc:
            after_first(t - lag)
        if 0 <= t - 2 * lag < nc:
            after_second(t - 2 * lag)
        if 0 <= t - 3 * lag < nc:
            after_third(t - 3 * lag)
        if steps - 7 <= t < steps - 2:
            vector(t - (steps - 7))
    for copy in started:
        copy.wait_send()


def sum_grads(lo, plan, lefts, rights, vectors):
    zs = lo // 2
    tokens = rights[0].shape[0]
    chunks = [(p[3],) + c for p in plan for c in p[5]]
    nc = len(chunks)
    dma = pltpu.SemaphoreType.DMA
    n_in = len(lefts) + len(rights)
    scratch = [VMEM((a.shape[1], 2 * tokens), bf16) for a in lefts]
    scratch += [VMEM((2 * tokens, b.shape[1]), bf16) for b in rights]
    scratch += [VMEM((2, 2, zs, r, w), bf16) for r, _, w, _ in chunks]
    scratch += [VMEM((2, zs, r, w), bf16) for r, _, w, _ in chunks]
    scratch += [VMEM((zs, r, w), bf16) for r, _, w, _ in chunks]
    scratch += [VMEM((zs - 1, r, w), bf16) for r, _, w, _ in chunks]
    scratch += [
        VMEM((4,) + vectors.shape, f32),
        VMEM((2 + zs,) + vectors.shape, f32),
        dma((n_in,)),
        dma((n_in,)),
        dma((n_in,)),
        dma((2, nc)),
        dma((2, nc)),
        dma((zs - 1, nc)),
        dma((zs - 1, nc)),
        dma((2 + zs,)),
        dma((2 + zs,)),
    ]
    out = pl.pallas_call(
        functools.partial(sum_kernel, lo, plan, len(lefts), len(rights)),
        name="sum_grads",
        out_shape=[jax.ShapeDtypeStruct((p[4], p[2]), f32) for p in plan]
        + [jax.ShapeDtypeStruct(vectors.shape, f32)],
        in_specs=[in_place()] * n_in + [in_vmem()],
        out_specs=[in_vmem()] * (len(plan) + 1),
        scratch_shapes=scratch,
        compiler_params=pltpu.CompilerParams(
            collective_id=4, has_side_effects=True, vmem_limit_bytes=LIMIT
        ),
    )(*lefts, *rights, vectors)
    return out[:-1], out[-1]


def rms_norm(values, gain):
    return values * lax.rsqrt(jnp.mean(values * values, axis=-1, keepdims=True) + norm_eps) * gain


def fore_dot(left, right):
    return jnp.dot(left, right, preferred_element_type=f32)


def back_dot(left, right):
    return lax.dot_general(left, right, (((1,), (1,)), ((), ())), preferred_element_type=f32)


def gated_unit(gate_vals, up_vals):
    return jax.nn.silu(gate_vals) * up_vals


def by_owner(a, hi, lo):
    tokens, features = a.shape
    r = features // (hi * lo * 4)
    t = a.reshape(tokens, hi, lo, 2, 2, r).transpose(4, 2, 3, 1, 5, 0).reshape(2, lo * 2, hi * r, tokens)
    pad = -(hi * r) % 16
    if pad:
        t = jnp.pad(t, ((0, 0), (0, 0), (0, pad), (0, 0)))
    return t.reshape(2, -1, tokens)


def body(
    size, tokens, resets, pre_gain, query_weight, key_weight, value_weight, forget_weight, forget_bias,
    outgate_weight, output_weight, head_gain, post_gain, gate_weight, up_weight, down_weight, cotangent,
):
    lo = 8 if size % 8 == 0 else size
    hi = size // lo
    streams, length, width = tokens.shape
    n = streams * length
    head = head_gain.shape[0]
    heads = width // head
    (wq, wk, wv, wf, wg, wo, w_gate, w_up, w_down) = gather(
        (
            query_weight, key_weight, value_weight, forget_weight, outgate_weight, output_weight,
            gate_weight, up_weight, down_weight,
        )
    )
    inputs = tokens.reshape(n, width).astype(f32)
    cotan = cotangent.reshape(n, width)
    flags = resets.reshape(n).astype(f32)
    fcol = jnp.broadcast_to(flags[:, None], (n, 128))
    frow = jnp.broadcast_to(flags[None], (8, n))
    bias, gain = forget_bias[None], head_gain[None]
    normed_full, norm_back = jax.vjp(rms_norm, inputs, pre_gain)
    normed = normed_full.astype(bf16)
    q = fore_dot(normed, wq).astype(bf16)
    k = fore_dot(normed, wk).astype(bf16)
    v = fore_dot(normed, wv).astype(bf16)
    pre = fore_dot(normed, wf)
    logits = fore_dot(normed, wg)
    merged, *kept = attend(size, heads, q, k, v, pre, bias, fcol, frow, logits, gain)
    hidden_one = inputs + fore_dot(merged, wo)
    normed_second, second_back = jax.vjp(rms_norm, hidden_one, post_gain)
    normed_two = normed_second.astype(bf16)
    gate_vals = fore_dot(normed_two, w_gate)
    up_vals = fore_dot(normed_two, w_up)
    hidden_full, unit_back = jax.vjp(gated_unit, gate_vals, up_vals)
    hidden = hidden_full.astype(bf16)
    block_output = (hidden_one + fore_dot(hidden, w_down)).astype(bf16)
    hidden_delta = back_dot(cotan, w_down)
    gate_full, up_full = unit_back(hidden_delta)
    gate_delta = gate_full.astype(bf16)
    up_delta = up_full.astype(bf16)
    second_delta = back_dot(gate_delta, w_gate) + back_dot(up_delta, w_up)
    through_norm, postgain_grad = second_back(second_delta)
    first_delta = cotan.astype(f32) + through_norm
    attn_delta = first_delta.astype(bf16)
    merged_delta = back_dot(attn_delta, wo)
    q_low, k_low, v_low, forget_low, logit_low, bias_grad, headgain_grad = go_back(
        size, heads, q, k, v, pre, bias, fcol, frow, logits, gain, kept, merged_delta
    )
    normed_delta = (
        back_dot(q_low, wq)
        + back_dot(k_low, wk)
        + back_dot(v_low, wv)
        + back_dot(forget_low, wf)
        + back_dot(logit_low, wg)
    )
    input_delta, pregain_grad = norm_back(normed_delta)
    input_grad = (first_delta + input_delta).astype(bf16)

    order = functools.partial(by_owner, hi=hi, lo=lo)
    lefts = [order(hidden), order(normed_two), order(merged), order(normed)]
    rights = [cotan, gate_delta, up_delta, attn_delta, logit_low, q_low, k_low, v_low, forget_low]
    which = (0, 1, 1, 2, 3, 3, 3, 3, 3)
    features = (hidden.shape[1],) + (width,) * 8
    plan = []
    for i, (left, right) in enumerate(zip(which, rights)):
        kept_rows = features[i] // (lo * 4)
        columns = right.shape[1]
        plan.append((left, i, columns, -(-kept_rows // 16) * 16, kept_rows, tuple(cut(columns, i % 2))))
    sizes = (width, bias.shape[1], head, width)
    vectors = jnp.concatenate([pregain_grad, bias_grad[0], headgain_grad[0], postgain_grad])
    total = vectors.shape[0]
    vectors = jnp.pad(vectors, (0, -total % 1024)).reshape(8, -1)
    grads, vectors = sum_grads(lo, tuple(plan), lefts, rights, vectors)
    if hi > 1:
        alike = [[a * lo + b for a in range(hi)] for b in range(lo)]
        grads = [
            lax.psum_scatter(g, "seq", scatter_dimension=0, axis_index_groups=alike, tiled=True)
            for g in grads
        ]
        vectors = lax.psum(vectors, "seq", axis_index_groups=alike)
    down_grad, gate_grad, up_grad, output_grad, outgate_grad, query_grad, key_grad, value_grad, forget_grad = grads
    vectors = vectors.reshape(-1)
    ends = [sum(sizes[: i + 1]) for i in range(4)]
    pregain, bias_total, headgain, postgain = [vectors[e - w : e] for e, w in zip(ends, sizes)]
    shape = tokens.shape
    return (
        block_output.reshape(shape), input_grad.reshape(shape), pregain, query_grad, key_grad, value_grad,
        forget_grad, bias_total, outgate_grad, output_grad, headgain, postgain, gate_grad, up_grad, down_grad,
    )


def solution(mesh):
    rows, whole, both = P("fsdp", None), P(), P(("seq", "fsdp"), None)
    return jax.shard_map(
        functools.partial(body, mesh.shape["seq"]),
        mesh=mesh,
        in_specs=(
            P("fsdp", "seq", None), P("fsdp", "seq"), whole, rows, rows, rows, rows, whole, rows, rows,
            whole, whole, rows, rows, rows, P("fsdp", "seq", None),
        ),
        out_specs=(
            P("fsdp", "seq", None), P("fsdp", "seq", None), whole, both, both, both, both, whole, both,
            both, whole, whole, both, both, both,
        ),
        check_vma=False,
    )
```

```python
import functools

import jax
import jax.numpy as jnp
from jax import lax
from jax.experimental import pallas as pl
from jax.experimental.pallas import tpu as pltpu
from jax.sharding import PartitionSpec as P

BLOCK = 64
TILE = 256
norm_eps = 1e-06
f32, bf16 = jnp.float32, jnp.bfloat16
MESH = pl.DeviceIdType.MESH
VMEM = pltpu.VMEM
ANY = pl.ANY
LIMIT = 60 * 2**20


def in_vmem():
    return pl.BlockSpec(memory_space=VMEM)


def in_place():
    return pl.BlockSpec(memory_space=ANY)


def greet(partners):
    barrier = pltpu.get_barrier_semaphore()
    for partner in partners:
        pl.semaphore_signal(barrier, inc=1, device_id=partner, device_id_type=MESH)
    pl.semaphore_wait(barrier, len(partners))


def remote(src, dst, sems, index, partner):
    return pltpu.make_async_remote_copy(
        src_ref=src,
        dst_ref=dst,
        send_sem=sems[0].at[index],
        recv_sem=sems[1].at[index],
        device_id=partner,
        device_id_type=MESH,
    )


def parts_of(a, count):
    if a.dtype == bf16:
        return [a]
    out = []
    for i in range(count):
        part = a.astype(bf16)
        out.append(part)
        if i + 1 < count:
            a = a - part.astype(f32)
    return out


def dot(a, b, ca=1, cb=0, count=1):
    total = None
    for right in reversed(parts_of(b, count)):
        term = lax.dot_general(
            a.astype(bf16), right, (((ca,), (cb,)), ((), ())), preferred_element_type=f32
        )
        total = term if total is None else total + term
    return total


def to_col(row):
    n = row.shape[1]
    i = lax.broadcasted_iota(jnp.int32, (n, n), 0)
    j = lax.broadcasted_iota(jnp.int32, (n, n), 1)
    return jnp.sum(jnp.where(i == j, jnp.broadcast_to(row, (n, n)), 0.0), axis=1, keepdims=True)


def mask_set(flags_col, flags_row):
    n = flags_col.shape[0]
    i = lax.broadcasted_iota(jnp.int32, (n, n), 0)
    j = lax.broadcasted_iota(jnp.int32, (n, n), 1)
    same = (i // BLOCK) == (j // BLOCK)
    lower = jnp.where(same & (i >= j), 1.0, 0.0)
    block = jnp.where(same, 1.0, 0.0)
    seen_col = dot(lower, flags_col)[:, :1]
    all_col = dot(block, flags_col)[:, :1]
    seen_row = dot(flags_row, lower, 1, 1)[:1, :]
    linked = jnp.where(seen_col == seen_row, lower, 0.0)
    fresh = jnp.where(seen_col == 0.0, 1.0, 0.0)
    ending = jnp.where(seen_col == all_col, 1.0, 0.0)
    unbroken = jnp.where(all_col == 0.0, 1.0, 0.0)
    return lower, linked, fresh, ending, unbroken


def gate_set(pre, bias, lower, ending):
    z = pre + bias
    u = jnp.exp(-jnp.abs(z))
    lp = jnp.where(
        u < 0.02, u * (1.0 - u * (0.5 - u * (1.0 / 3.0 - 0.25 * u))), jnp.log(1.0 + u)
    )
    g = (jnp.minimum(z, 0.0) - lp) * 0.125
    series = 1.0 + g * (1.0 / 7.0)
    for order in (6, 5, 4, 3, 2):
        series = 1.0 + g * (1.0 / order) * series
    oma = jnp.where(g > -0.35, -g * series, 1.0 - jnp.exp(g))
    a = dot(lower, g, count=3)
    n, lanes = a.shape
    last = jnp.concatenate(
        [
            jnp.broadcast_to(a[b * BLOCK + BLOCK - 1 : b * BLOCK + BLOCK], (BLOCK, lanes))
            for b in range(n // BLOCK)
        ],
        axis=0,
    )
    tail = jnp.exp(last - a) * ending
    return z, u, oma, jnp.exp(a), jnp.exp(-a), tail


def rows_of(b):
    return slice(b * BLOCK, (b + 1) * BLOCK)


def passing(growth, unbroken, b, hs):
    last = b * BLOCK + BLOCK - 1
    return to_col(growth[last : last + 1, hs] * unbroken[last : last + 1])


def sigmoid(v):
    return 1.0 / (1.0 + jnp.exp(-v))


WEIGHTS = ("key", "value", "forget", "query", "outgate", "output", "gate", "up", "down")
TWICE = ("gate", "up")


def front_kernel(size, heads, grouped, *refs):
    count = len(WEIGHTS)
    shards, refs = dict(zip(WEIGHTS, refs[:count])), refs[count:]
    (tok_ref, cot_ref, pre_gain, post_gain, head_gain, bias_ref, fcol_ref, frow_ref), refs = refs[:8], refs[8:]
    (
        out_ref, first_ref, attn_ref, mdelta_ref, postgain_grad,
        normed_t, merged_t, second_t, hidden_t, gate_delta, up_delta,
        q_ref, k_ref, v_ref, pre_ref, logit_ref,
        mixed_ref, aff_ref, mixing_ref, weight_ref, inner_ref, state_ref, pass_ref,
    ), refs = refs[:23], refs[23:]
    passed, refs = dict(zip(WEIGHTS[:5], refs[:5])), refs[5:]
    whole, refs = dict(zip(WEIGHTS, refs[:count])), refs[count:]
    (
        normed, merged, one_ref, second, block_acc, delta_acc, flat_t,
        ends, going, gathered, prefix, came,
        local, send_sem, recv_sem, away, st_send, st_recv,
    ) = refs
    sems = (send_sem, recv_sem)
    s, f = lax.axis_index("seq"), lax.axis_index("fsdp")
    q = lax.rem(s, 4)
    kind_bit = lax.rem(q + q // 2, 2)
    sib, far, nx, nz = (s, f ^ 1), (s, f ^ 2), (s ^ 1, f), (s ^ 2, f)
    fy, fs = f ^ 2, f ^ 3
    others = [(lax.rem(s + d, size), f) for d in range(1, size)]
    greet([sib, far] + others)
    started = []

    def go(copy):
        copy.start()
        started.append(copy)

    def piece(m, owner, start, length):
        rows = shards[m].shape[0]
        return whole[m].at[pl.ds(pl.multiple_of(owner * rows + start, 16), length)]

    def quarter(m, owner, which, half=None):
        rows = shards[m].shape[0] // 4
        first = (rows // 2 + 15) // 16 * 16
        start, length = (0, rows) if half is None else ((0, first), (first, rows - first))[half]
        return piece(m, owner, which * rows + start, length)

    def eighth(m, owner, bit, half):
        rows = shards[m].shape[0] // 2
        return piece(m, owner, bit * rows + half * (rows // 2), rows // 2)

    def mine(m, owner):
        if m in TWICE:
            rows = shards[m].shape[0] // 2
            return piece(m, owner, kind_bit * rows, rows)
        return quarter(m, owner, q)

    def from_x(m, owner):
        return eighth(m, owner, 1 - kind_bit, 0) if m in TWICE else quarter(m, owner, q ^ 1)

    def from_z(m, owner):
        return eighth(m, owner, 1 - kind_bit, 1) if m in TWICE else quarter(m, owner, q ^ 2)

    def send(kind, m, part, partner):
        go(remote(part, part, sems, (kind, WEIGHTS.index(m)), partner))

    def arrived(kind, m, part):
        remote(part, part, sems, (kind, WEIGHTS.index(m)), sib).wait_recv()

    own = {}
    for i, m in enumerate(WEIGHTS):
        rows = shards[m].shape[0]
        if m in TWICE:
            src = shards[m].at[pl.ds(pl.multiple_of(kind_bit * (rows // 2), 16), rows // 2)]
        else:
            src = shards[m].at[pl.ds(pl.multiple_of(q * (rows // 4), 16), rows // 4)]
        go(remote(src, mine(m, f), sems, (1, i), far))
    for i, m in enumerate(WEIGHTS):
        rows = shards[m].shape[0]
        go(remote(shards[m], piece(m, f, 0, rows), sems, (0, i), sib))
        own[m] = pltpu.make_async_copy(shards[m], piece(m, f, 0, rows), local.at[i])
        own[m].start()

    def pump(step):
        if step < count:
            m = WEIGHTS[step]
            part = mine(m, fy)
            arrived(1, m, part)
            if m in TWICE:
                send(2, m, eighth(m, fy, kind_bit, 0), nx)
                send(3, m, eighth(m, fy, kind_bit, 1), nz)
            else:
                send(2, m, part, nx)
                send(3, m, part, nz)
            send(6, m, part, sib)
        if 0 <= step - 1 < count:
            m = WEIGHTS[step - 1]
            arrived(2, m, from_x(m, fy))
            if m not in TWICE:
                send(4, m, quarter(m, fy, q ^ 1, 0), nz)
            send(7, m, from_x(m, fy), sib)
            arrived(3, m, from_z(m, fy))
            if m not in TWICE:
                send(5, m, quarter(m, fy, q ^ 2, 1), nx)
            send(8, m, from_z(m, fy), sib)
        if 0 <= step - 2 < count:
            m = WEIGHTS[step - 2]
            if m not in TWICE:
                for kind in (4, 5):
                    part = quarter(m, fy, q ^ 3, kind - 4)
                    arrived(kind, m, part)
                    send(kind + 5, m, part, sib)

    def ready(m):
        own[m].wait()
        arrived(0, m, piece(m, f ^ 1, 0, shards[m].shape[0]))
        arrived(6, m, mine(m, fs))
        arrived(7, m, from_x(m, fs))
        arrived(8, m, from_z(m, fs))
        if m not in TWICE:
            arrived(9, m, quarter(m, fs, q ^ 3, 0))
            arrived(10, m, quarter(m, fs, q ^ 3, 1))

    n, width = tok_ref.shape
    head = width // heads
    slots = bias_ref.shape[1] // heads
    blocks = n // BLOCK
    streams = 2
    per = blocks // streams
    pairs = heads * streams
    scale = head ** (-0.5)

    def across(columns, step):
        def turn(i, carry):
            step(pl.ds(pl.multiple_of(i * TILE, TILE), TILE))
            return carry

        lax.fori_loop(0, columns // TILE, turn, 0)

    def project(m, to_ref):
        def step(at):
            to_ref[:, at] = dot(normed[...], whole[m][:, at]).astype(to_ref.dtype)

        across(whole[m].shape[1], step)

    def turn_over(source, to_ref, rows, padded):
        if not grouped:
            to_ref[...] = source[...].astype(bf16)
            return
        for group in range(16):
            for core in range(2):
                at = (group * 2 + core) * rows
                to_ref[core, group * padded : group * padded + rows] = source[at : at + rows].astype(bf16)

    inputs = tok_ref[...].astype(f32)
    unit = inputs * lax.rsqrt(jnp.mean(inputs * inputs, axis=1, keepdims=True) + norm_eps)
    scaled = unit * pre_gain[...]
    normed[...] = scaled.astype(bf16)
    turn_over(scaled.T, normed_t, width // 32, width // 32)
    for step in range(5):
        pump(step)
    for m, to_ref in (("key", k_ref), ("value", v_ref), ("forget", pre_ref)):
        ready(m)
        project(m, to_ref)
    lower, linked, fresh, ending, unbroken = mask_set(fcol_ref[...], frow_ref[...])
    z, u, oma, growth, inverse, tail = gate_set(pre_ref[...], bias_ref[...], lower, ending)
    shrink, kept = inverse * oma, tail * oma
    for h in range(heads):
        hs, hd = slice(h * slots, (h + 1) * slots), slice(h * head, (h + 1) * head)
        for stream in range(streams):
            pair = h * streams + stream
            total, through = None, None
            for b in range(stream * per, (stream + 1) * per):
                part = kept[rows_of(b), hs].astype(bf16)
                at = pair * per + b % per
                end_k = dot(part, k_ref[rows_of(b), hd], 0, 0)
                end_v = dot(part, v_ref[rows_of(b), hd], 0, 0)
                ends[at, :, :head] = end_k
                ends[at, :, head:] = end_v
                factor = passing(growth, unbroken, b, hs)
                pass_ref[at] = jnp.broadcast_to(factor, pass_ref.shape[1:])
                if total is None:
                    total, through = (end_k, end_v), factor
                else:
                    total = (factor * total[0] + end_k, factor * total[1] + end_v)
                    through = through * factor
            at = slice(pair * slots, (pair + 1) * slots)
            going[at, :head] = total[0].astype(bf16)
            going[at, head : 2 * head] = total[1].astype(bf16)
            going[at, 2 * head :] = jnp.broadcast_to(through, (slots, going.shape[1] - 2 * head)).astype(bf16)

    share = pairs * slots // size

    def rows_for(place):
        return pl.ds(pl.multiple_of(place * share, 16), share)

    first_hop, second_hop = [], []
    for d in range(1, size):
        to = others[d - 1]
        copy = remote(going.at[rows_for(to[0])], gathered.at[s], (st_send, st_recv), (0, d - 1), to)
        go(copy)
        first_hop.append(lax.rem(s + size - d, size))
    gathered[s] = going[rows_for(s)]
    pump(5)
    pump(6)
    for m, to_ref in (("query", q_ref), ("outgate", logit_ref)):
        ready(m)
        project(m, to_ref)
    for i, m in enumerate(WEIGHTS[:5]):
        copy = pltpu.make_async_copy(whole[m], passed[m], away.at[i])
        copy.start()
        own[m] = copy
    for d in range(1, size):
        source = first_hop[d - 1]
        remote(gathered.at[source], gathered.at[source], (st_send, st_recv), (0, d - 1), sib).wait_recv()
    state = jnp.zeros((share, 2 * head), f32)
    for place in range(size):
        prefix[place] = state.astype(bf16)
        entry = gathered[place].astype(f32)
        state = entry[:, 2 * head : 2 * head + 1] * state + entry[:, : 2 * head]
    for d in range(1, size):
        to = others[d - 1]
        go(remote(prefix.at[to[0]], came.at[rows_for(s)], (st_send, st_recv), (1, d - 1), to))
    came[rows_for(s)] = prefix[s]
    pump(7)
    for h in range(heads):
        hd = slice(h * head, (h + 1) * head)
        aff_ref[h] = (dot(q_ref[:, hd], k_ref[:, hd], 1, 1) * (linked * scale)).astype(bf16)
    for d in range(1, size):
        part = came.at[rows_for(first_hop[d - 1])]
        remote(part, part, (st_send, st_recv), (1, d - 1), sib).wait_recv()
    pump(8)
    for h in range(heads):
        hs, hd = slice(h * slots, (h + 1) * slots), slice(h * head, (h + 1) * head)
        for stream in range(streams):
            pair = h * streams + stream
            state = came[pair * slots : (pair + 1) * slots].astype(f32)
            for b in range(per):
                at = pair * per + b
                state_ref[pair, b] = state.astype(bf16)
                state = pass_ref[at][:, :1] * state + ends[at]
            state_ref[pair, per] = state.astype(bf16)
        gr, sh = growth[:, hs], shrink[:, hs]
        qh, vh = q_ref[:, hd], v_ref[:, hd]
        carried = jnp.concatenate(
            [
                dot(qh[rows_of(b)], state_ref[h * streams + b // per, b % per, :, :head], 1, 1)
                for b in range(blocks)
            ],
            axis=0,
        )
        inner = dot(aff_ref[h], sh) + carried * (scale * fresh)
        scores = gr * inner
        e = jnp.exp(scores - jnp.max(scores, axis=1, keepdims=True))
        weights = e / jnp.sum(e, axis=1, keepdims=True)
        weight_ref[:, hs] = weights
        inner_ref[:, hs] = inner
        lifted = weights * gr
        mixing = (dot(lifted, sh.astype(bf16), 1, 1) * linked).astype(bf16)
        mixing_ref[h] = mixing
        brought = jnp.concatenate(
            [
                dot(lifted[rows_of(b)], state_ref[h * streams + b // per, b % per, :, head:])
                for b in range(blocks)
            ],
            axis=0,
        )
        mixed = dot(mixing, vh) + brought * fresh
        mixed_ref[:, hd] = mixed
        r = lax.rsqrt(jnp.mean(mixed * mixed, axis=1, keepdims=True) + norm_eps)
        logits = logit_ref[:, hd]
        delta_acc[:, hd] = mixed * r * head_gain[...] * (logits * sigmoid(logits))
        merged[:, hd] = delta_acc[:, hd].astype(bf16)
    ready("output")

    def join(at):
        one_ref[:, at] = tok_ref[:, at].astype(f32) + dot(merged[...], whole["output"][:, at])

    across(width, join)
    turn_over(delta_acc[...].T, merged_t, width // 32, width // 32)
    one = one_ref[...]
    scaled = one * lax.rsqrt(jnp.mean(one * one, axis=1, keepdims=True) + norm_eps) * post_gain[...]
    second[...] = scaled.astype(bf16)
    turn_over(scaled.T, second_t, width // 32, width // 32)
    pump(9)
    pump(10)
    ready("gate")
    ready("up")
    ready("down")
    block_acc[...] = one
    delta_acc[...] = jnp.zeros_like(delta_acc)

    def unit_tile(i, carry):
        at = pl.ds(pl.multiple_of(i * TILE, TILE), TILE)
        w_gate, w_up, w_down = whole["gate"][:, at], whole["up"][:, at], whole["down"][at]
        gate_vals, up_vals = dot(second[...], w_gate), dot(second[...], w_up)
        sig = sigmoid(gate_vals)
        silu = gate_vals * sig
        full = silu * up_vals
        flat_t[at] = full.T
        hidden_delta = dot(cot_ref[...], w_down, 1, 1)
        d_up = (hidden_delta * silu).astype(bf16)
        d_gate = (hidden_delta * up_vals * (sig + silu * (1.0 - sig))).astype(bf16)
        gate_delta[:, at] = d_gate
        up_delta[:, at] = d_up
        block_acc[...] += dot(full, w_down)
        delta_acc[...] += dot(d_gate, w_gate, 1, 1) + dot(d_up, w_up, 1, 1)
        return carry

    ff = whole["down"].shape[0]
    lax.fori_loop(0, ff // TILE, unit_tile, 0)
    out_ref[...] = block_acc[...].astype(bf16)
    turn_over(flat_t, hidden_t, ff // 32, -(-(ff // 32) // 16) * 16)
    one = one_ref[...]
    r = lax.rsqrt(jnp.mean(one * one, axis=1, keepdims=True) + norm_eps)
    unit = one * r
    delta = delta_acc[...]
    postgain_grad[...] = jnp.sum(delta * unit, axis=0, keepdims=True)
    delta = delta * post_gain[...]
    first = cot_ref[...].astype(f32) + r * (delta - unit * jnp.mean(unit * delta, axis=1, keepdims=True))
    first_ref[...] = first
    attn_ref[...] = first.astype(bf16)

    def split(at):
        mdelta_ref[:, at] = dot(attn_ref[...], whole["output"][at], 1, 1)

    across(width, split)
    for m in WEIGHTS[:5]:
        own[m].wait()
    for copy in started:
        copy.wait_send()


def front(size, heads, grouped, shards, tokens, cotan, pre_gain, post_gain, head_gain, bias, fcol, frow):
    n, width = tokens.shape
    head, slots = width // heads, bias.shape[1] // heads
    pairs, per = heads * 2, n // BLOCK // 2
    ff = shards["gate"].shape[1]
    shards = [shards[m] for m in WEIGHTS]
    count = len(shards)
    padded = -(-(ff // 32) // 16) * 512

    def turned(rows, grouped_rows):
        shape = (2, grouped_rows // 2, n) if grouped else (rows, n)
        return jax.ShapeDtypeStruct(shape, bf16)

    def low(*shape):
        return jax.ShapeDtypeStruct(shape, bf16)

    def full(*shape):
        return jax.ShapeDtypeStruct(shape, f32)

    outs = [
        low(n, width), full(n, width), low(n, width), full(n, width), full(1, width),
        turned(width, width), turned(width, width), turned(width, width), turned(ff, padded),
        low(n, ff), low(n, ff),
        low(n, width), low(n, width), low(n, width), full(n, heads * slots), full(n, width),
        full(n, width), low(heads, n, n), low(heads, n, n), full(n, heads * slots), full(n, heads * slots),
        low(pairs, per + 1, slots, 2 * head), full(pairs * per, slots, 128),
    ]
    wholes = [low(4 * w.shape[0], w.shape[1]) for w in shards]
    share = pairs * slots // size
    dma = pltpu.SemaphoreType.DMA
    got = pl.pallas_call(
        functools.partial(front_kernel, size, heads, grouped),
        name="front",
        out_shape=outs + wholes[:5],
        in_specs=[in_place()] * count + [in_vmem()] * 8,
        out_specs=[in_vmem()] * len(outs) + [in_place()] * 5,
        scratch_shapes=[VMEM(w.shape, bf16) for w in wholes]
        + [
            VMEM((n, width), bf16),
            VMEM((n, width), bf16),
            VMEM((n, width), f32),
            VMEM((n, width), bf16),
            VMEM((n, width), f32),
            VMEM((n, width), f32),
            VMEM((ff, n), f32),
            VMEM((pairs * per, slots, 2 * head), f32),
            VMEM((pairs * slots, 2 * head + 128), bf16),
            VMEM((size, share, 2 * head + 128), bf16),
            VMEM((size, share, 2 * head), bf16),
            VMEM((pairs * slots, 2 * head), bf16),
            dma((count,)),
            dma((11, count)),
            dma((11, count)),
            dma((5,)),
            dma((2, size - 1)),
            dma((2, size - 1)),
        ],
        compiler_params=pltpu.CompilerParams(
            collective_id=1, has_side_effects=True, vmem_limit_bytes=LIMIT
        ),
    )(*shards, tokens, cotan, pre_gain, post_gain, head_gain, bias, fcol, frow)
    return got


def return_kernel(
    size, heads, q_ref, k_ref, v_ref, pre_ref, bias_ref, fcol_ref, frow_ref, logit_ref, gain_ref,
    mixed_ref, aff_ref, mixing_ref, weight_ref, inner_ref, state_ref, pass_ref, delta_ref,
    q_low, k_low, v_low, forget_low, logit_low, bias_grad, gain_grad,
    owed, came, going, k_acc, v_acc, dmix, da_acc, doma_acc, send_sem, recv_sem,
):
    s, f = lax.axis_index("seq"), lax.axis_index("fsdp")
    right, left = (lax.rem(s + 1, size), f), (lax.rem(s + size - 1, size), f)
    greet((left, right))
    n, width = q_ref.shape
    head = width // heads
    slots = pre_ref.shape[1] // heads
    blocks = n // BLOCK
    streams = 2
    per = blocks // streams
    scale = head ** (-0.5)
    lower, linked, fresh, ending, unbroken = mask_set(fcol_ref[...], frow_ref[...])
    z, u, oma, growth, inverse, tail = gate_set(pre_ref[...], bias_ref[...], lower, ending)
    shrink, kept = inverse * oma, tail * oma

    @pl.when(s == size - 1)
    def _():
        came[...] = jnp.zeros_like(came)

    gain_total = jnp.zeros((1, head), f32)
    for h in range(heads):
        hs, hd = slice(h * slots, (h + 1) * slots), slice(h * head, (h + 1) * head)
        mixed, logits, delta = mixed_ref[:, hd], logit_ref[:, hd], delta_ref[:, hd]
        r = lax.rsqrt(jnp.mean(mixed * mixed, axis=1, keepdims=True) + norm_eps)
        sig = 1.0 / (1.0 + jnp.exp(-logits))
        silu = logits * sig
        unit = mixed * r
        dy = delta * silu
        logit_low[:, hd] = (delta * unit * gain_ref[...] * (sig + silu * (1.0 - sig))).astype(bf16)
        gain_total = gain_total + jnp.sum(dy * unit, axis=0, keepdims=True)
        dy = dy * gain_ref[...]
        dmixed = r * (dy - unit * jnp.mean(unit * dy, axis=1, keepdims=True))
        gr, sh = growth[:, hs], shrink[:, hs].astype(bf16)
        weights, inner = weight_ref[:, hs], inner_ref[:, hs]
        aff, mixing = aff_ref[h], mixing_ref[h]
        qh, kh, vh = q_ref[:, hd], k_ref[:, hd], v_ref[:, hd]
        do = dmixed.astype(bf16)
        lifted = (weights * gr).astype(bf16)
        dm = (dot(do, vh, 1, 1) * linked).astype(bf16)
        v_acc[:, hd] = dot(mixing, do, 0, 0)
        fdo = (dmixed * fresh).astype(bf16)

        def states(b, h=h):
            return state_ref.at[h * streams + b // per, b % per]

        dlift = dot(dm, sh) + jnp.concatenate(
            [dot(fdo[rows_of(b)], states(b)[:, head:], 1, 1) for b in range(blocks)], axis=0
        )
        dsh = dot(dm, lifted, 0, 0)
        dw = dlift * gr
        dsc = weights * (dw - jnp.sum(weights * dw, axis=1, keepdims=True))
        du = dsc * gr
        du_low = du.astype(bf16)
        da = (dot(du_low, sh, 1, 1) * (linked * scale)).astype(bf16)
        dsh = dsh + dot(aff, du_low, 0, 0)
        fdu = (du * (fresh * scale)).astype(bf16)
        q_low[:, hd] = (
            dot(da, kh)
            + jnp.concatenate(
                [dot(fdu[rows_of(b)], states(b)[:, :head]) for b in range(blocks)], axis=0
            )
        ).astype(bf16)
        k_acc[:, hd] = dot(da, qh, 0, 0)
        for b in range(blocks):
            at = (h * streams + b // per) * per + b % per
            owed[at, :, :head] = dot(fdu[rows_of(b)], qh[rows_of(b)], 0, 0)
            owed[at, :, head:] = dot(lifted[rows_of(b)], fdo[rows_of(b)], 0, 0)
        da_acc[:, hs] = lifted.astype(f32) * dlift + du_low.astype(f32) * inner - dsh * sh.astype(f32)
        doma_acc[:, hs] = dsh * inverse[:, hs]
    gain_grad[...] = gain_total
    sends = []
    for pair in range(heads * streams):
        copy = remote(going.at[pair], came.at[pair], (send_sem, recv_sem), pair, left)

        @pl.when(s < size - 1)
        def _(copy=copy):
            copy.wait_recv()

        state = came[pair].astype(f32)
        for b in reversed(range(per)):
            at = pair * per + b
            before = owed[at] + pass_ref[at][:, :1] * state
            owed[at] = state
            state = before
        going[pair] = state.astype(bf16)

        @pl.when(s > 0)
        def _(copy=copy):
            copy.start()

        sends.append(copy)
    row = lax.broadcasted_iota(jnp.int32, (BLOCK, 1), 0)
    for h in range(heads):
        hs, hd = slice(h * slots, (h + 1) * slots), slice(h * head, (h + 1) * head)
        for b in range(blocks):
            rb = rows_of(b)
            pair = h * streams + b // per
            at = pair * per + b % per
            leaving = owed[at]
            low = leaving.astype(bf16)
            part = kept[rb, hs].astype(bf16)
            dkept = dot(k_ref[rb, hd], low[:, :head], 1, 1) + dot(v_ref[rb, hd], low[:, head:], 1, 1)
            k_low[rb, hd] = (k_acc[rb, hd] + dot(part, low[:, :head])).astype(bf16)
            v_low[rb, hd] = (v_acc[rb, hd] + dot(part, low[:, head:])).astype(bf16)
            held = jnp.sum(low.astype(f32) * state_ref[pair, b % per + 1].astype(f32), axis=1, keepdims=True)
            held_row = to_row(held)
            da_acc[rb, hs] = (
                da_acc[rb, hs] - dkept * part.astype(f32) + jnp.where(row == BLOCK - 1, held_row, 0.0)
            )
            doma_acc[rb, hs] = doma_acc[rb, hs] + dkept * tail[rb, hs]
    dg = dot(lower, da_acc[...], 0, 0, count=3) - doma_acc[...] * (1.0 - oma)
    sig = jnp.where(z >= 0.0, u / (1.0 + u), 1.0 / (1.0 + u))
    dpre = dg * sig * 0.125
    forget_low[...] = dpre.astype(bf16)
    bias_grad[...] = jnp.sum(dpre, axis=0, keepdims=True)
    for copy in sends:

        @pl.when(s > 0)
        def _(copy=copy):
            copy.wait_send()


def to_row(col):
    n = col.shape[0]
    i = lax.broadcasted_iota(jnp.int32, (n, n), 0)
    j = lax.broadcasted_iota(jnp.int32, (n, n), 1)
    return jnp.sum(jnp.where(i == j, jnp.broadcast_to(col, (n, n)), 0.0), axis=0, keepdims=True)


def go_back(size, heads, q, k, v, pre, bias, fcol, frow, logits, gain, kept, delta):
    n, width = q.shape
    head, slots = width // heads, pre.shape[1] // heads
    pairs, per = heads * 2, n // BLOCK // 2
    return pl.pallas_call(
        functools.partial(return_kernel, size, heads),
        name="go_back",
        out_shape=[
            jax.ShapeDtypeStruct((n, width), bf16),
            jax.ShapeDtypeStruct((n, width), bf16),
            jax.ShapeDtypeStruct((n, width), bf16),
            jax.ShapeDtypeStruct(pre.shape, bf16),
            jax.ShapeDtypeStruct((n, width), bf16),
            jax.ShapeDtypeStruct((1, pre.shape[1]), f32),
            jax.ShapeDtypeStruct((1, head), f32),
        ],
        in_specs=[in_vmem()] * 17,
        out_specs=[in_vmem()] * 7,
        scratch_shapes=[
            VMEM((pairs * per, slots, 2 * head), f32),
            VMEM((pairs, slots, 2 * head), bf16),
            VMEM((pairs, slots, 2 * head), bf16),
            VMEM((n, width), f32),
            VMEM((n, width), f32),
            VMEM((8, 128), f32),
            VMEM(pre.shape, f32),
            VMEM(pre.shape, f32),
            pltpu.SemaphoreType.DMA((pairs,)),
            pltpu.SemaphoreType.DMA((pairs,)),
        ],
        compiler_params=pltpu.CompilerParams(
            collective_id=3, has_side_effects=True, vmem_limit_bytes=LIMIT
        ),
    )(q, k, v, pre, bias, fcol, frow, logits, gain, *kept, delta)


def cut(columns, flip):
    tiles = columns // TILE
    if tiles <= 1:
        half = columns // 2
        return [(0, half, flip), (half, half, 1 - flip)]
    pieces = 4 if tiles <= 4 else 6
    out, start = [], 0
    for i in range(pieces):
        count = tiles // pieces + (1 if i < tiles % pieces else 0)
        out.append((start, count * TILE, (i + flip) % 2))
        start += count * TILE
    return out


def sum_kernel(plan, n_left, n_right, *refs):
    lefts, refs = refs[:n_left], refs[n_left:]
    rights, refs = refs[:n_right], refs[n_right:]
    vec_in, refs = refs[0], refs[1:]
    outs, refs = refs[: len(plan)], refs[len(plan) :]
    vec_out, refs = refs[0], refs[1:]
    left_all, refs = refs[:n_left], refs[n_left:]
    right_all, refs = refs[:n_right], refs[n_right:]
    chunks = [(g,) + c for g, p in enumerate(plan) for c in p[5]]
    nc = len(chunks)
    sums, refs = refs[:nc], refs[nc:]
    landed = []
    for _ in range(4):
        landed.append(refs[:nc])
        refs = refs[nc:]
    vec_acc, vec_got, local, in_send, in_recv, st_send, st_recv, v_send, v_recv = refs
    s, f = lax.axis_index("seq"), lax.axis_index("fsdp")
    core, y = lax.rem(f, 2), f // 2
    x, z_low, z_high = lax.rem(s, 2), lax.rem(s // 2, 2), lax.rem(s // 4, 2)
    sib, far, nx, nz, nzz = (s, f ^ 1), (s, f ^ 2), (s ^ 1, f), (s ^ 2, f), (s ^ 4, f)
    greet([sib, far, nx, nz, nzz])
    started = []

    def go(copy):
        copy.start()
        started.append(copy)

    tokens = rights[0].shape[0]
    waiting = {}

    def exchange(kind, i):
        index = i if kind == 0 else n_left + i
        if (kind, i) in waiting:
            return
        if kind == 0:
            src_own, src_far = lefts[i].at[core], lefts[i].at[1 - core]
            dst_own, dst_far = left_all[i].at[:, pl.ds(0, tokens)], left_all[i].at[:, pl.ds(tokens, tokens)]
        else:
            src_own = src_far = rights[i]
            dst_own, dst_far = right_all[i].at[pl.ds(0, tokens)], right_all[i].at[pl.ds(tokens, tokens)]
        keep = pltpu.make_async_copy(src_own, dst_own, local.at[index])
        keep.start()
        copy = remote(src_far, dst_far, (in_send, in_recv), index, sib)
        go(copy)
        waiting[kind, i] = [keep, copy]

    def have(kind, i):
        pair = waiting[kind, i]
        if pair:
            pair[0].wait()
            pair[1].wait_recv()
            waiting[kind, i] = None

    for left, right, *_ in plan[:2]:
        exchange(0, left)
        exchange(1, right)

    def route(c):
        if chunks[c][3]:
            return (x, z_low, y, z_high), (nx, nz, far, nzz)
        return (y, z_low, x, z_high), (far, nz, nx, nzz)

    def stage_copy(c, stage):
        bits, partners = route(c)
        at = bits[:stage] + (1 - bits[stage],)
        return remote(sums[c].at[at], landed[stage][c], (st_send, st_recv), (stage, c), partners[stage])

    def produce(c):
        g, start, width, order = chunks[c]
        left, right, columns, rows, kept, _ = plan[g]
        have(0, left)
        have(1, right)
        for after in plan[g + 1 : g + 3]:
            exchange(0, after[0])
            exchange(1, after[1])
        tile = min(TILE, width)

        def body(i, carry):
            at = pl.multiple_of(start + i * tile, 128)
            to = pl.multiple_of(i * tile, 128)
            got = jnp.dot(
                left_all[left][...], right_all[right][:, pl.ds(at, tile)], preferred_element_type=f32
            ).astype(bf16)
            for group in range(16):
                zh, zl, xx, yy = (group >> 3) & 1, (group >> 2) & 1, (group >> 1) & 1, group & 1
                place = (xx, zl, yy, zh) if order else (yy, zl, xx, zh)
                sums[c][*place, :, pl.ds(to, tile)] = got[group * rows : (group + 1) * rows]
            return carry

        lax.fori_loop(0, width // tile, body, 0)
        go(stage_copy(c, 0))

    def advance(c, stage):
        stage_copy(c, stage).wait_recv()
        bits, _ = route(c)
        if stage == 3:
            g, start, width, _ = chunks[c]
            kept = plan[g][4]
            total = sums[c][bits].astype(f32) + landed[3][c][...].astype(f32)
            outs[g][:, start : start + width] = total[:kept]
            return
        for rest in range(1 << (3 - stage)):
            tail = tuple((rest >> k) & 1 for k in reversed(range(3 - stage)))
            at = bits[: stage + 1] + tail
            sums[c][at] = (sums[c][at].astype(f32) + landed[stage][c][tail].astype(f32)).astype(bf16)
        go(stage_copy(c, stage + 1))

    def v_copy(i):
        return remote(vec_acc.at[i], vec_got.at[i], (v_send, v_recv), i, (sib, far, nx, nz, nzz)[i])

    def vector(step):
        if step == 0:
            vec_acc[0] = vec_in[...]
        else:
            v_copy(step - 1).wait_recv()
            total = vec_acc[step - 1] + vec_got[step - 1]
            if step == 5:
                vec_out[...] = total
                return
            vec_acc[step] = total
        go(v_copy(step))

    lag = 3
    steps = nc + 4 * lag
    for t in range(steps):
        if t < nc:
            produce(t)
        for stage in range(4):
            c = t - (stage + 1) * lag
            if 0 <= c < nc:
                advance(c, stage)
        if steps - 7 <= t < steps - 1:
            vector(t - (steps - 7))
    for copy in started:
        copy.wait_send()


def sum_grads(plan, lefts, rights, vectors):
    tokens = rights[0].shape[0]
    chunks = [(p[3],) + c for p in plan for c in p[5]]
    nc = len(chunks)
    dma = pltpu.SemaphoreType.DMA
    n_in = len(lefts) + len(rights)
    scratch = [VMEM((a.shape[1], 2 * tokens), bf16) for a in lefts]
    scratch += [VMEM((2 * tokens, b.shape[1]), bf16) for b in rights]
    for lead in ((2, 2, 2, 2), (2, 2, 2), (2, 2), (2,), ()):
        scratch += [VMEM(lead + (r, w), bf16) for r, _, w, _ in chunks]
    scratch += [VMEM((5,) + vectors.shape, f32)] * 2
    scratch += [dma((n_in,))] * 3 + [dma((4, nc))] * 2 + [dma((5,))] * 2
    out = pl.pallas_call(
        functools.partial(sum_kernel, plan, len(lefts), len(rights)),
        name="sum_grads",
        out_shape=[jax.ShapeDtypeStruct((p[4], p[2]), f32) for p in plan]
        + [jax.ShapeDtypeStruct(vectors.shape, f32)],
        in_specs=[in_place()] * n_in + [in_vmem()],
        out_specs=[in_vmem()] * (len(plan) + 1),
        scratch_shapes=scratch,
        compiler_params=pltpu.CompilerParams(
            collective_id=4, has_side_effects=True, vmem_limit_bytes=LIMIT
        ),
    )(*lefts, *rights, vectors)
    return out[:-1], out[-1]


def rms_norm(values, gain):
    return values * lax.rsqrt(jnp.mean(values * values, axis=-1, keepdims=True) + norm_eps) * gain


def back_dot(left, right):
    return lax.dot_general(left, right, (((1,), (1,)), ((), ())), preferred_element_type=f32)


def by_owner(a, hi, lo):
    features, tokens = a.shape
    r = features // (hi * lo * 4)
    t = a.reshape(hi, lo, 2, 2, r, tokens).transpose(3, 1, 2, 0, 4, 5).reshape(2, lo * 2, hi * r, tokens)
    pad = -(hi * r) % 16
    if pad:
        t = jnp.pad(t, ((0, 0), (0, 0), (0, pad), (0, 0)))
    return t.reshape(2, -1, tokens)


def body(
    size, tokens, resets, pre_gain, query_weight, key_weight, value_weight, forget_weight, forget_bias,
    outgate_weight, output_weight, head_gain, post_gain, gate_weight, up_weight, down_weight, cotangent,
):
    lo = 8
    hi = size // lo
    streams, length, width = tokens.shape
    n = streams * length
    head = head_gain.shape[0]
    heads = width // head
    shards = {
        "query": query_weight, "key": key_weight, "value": value_weight, "forget": forget_weight,
        "outgate": outgate_weight, "output": output_weight, "gate": gate_weight, "up": up_weight, "down": down_weight,
    }
    cotan = cotangent.reshape(n, width)
    flags = resets.reshape(n).astype(f32)
    fcol = jnp.broadcast_to(flags[:, None], (n, 128))
    frow = jnp.broadcast_to(flags[None], (8, n))
    bias, gain = forget_bias[None], head_gain[None]
    (
        block_output, first_delta, attn_delta, merged_delta, postgain_grad,
        normed_t, merged_t, second_t, hidden_t, gate_delta, up_delta,
        q, k, v, pre, logits, *kept, wk, wv, wf, wq, wg,
    ) = front(
        size, heads, hi == 1, shards, tokens.reshape(n, width), cotan, pre_gain[None], post_gain[None],
        gain, bias, fcol, frow,
    )
    q_low, k_low, v_low, forget_low, logit_low, bias_grad, headgain_grad = go_back(
        size, heads, q, k, v, pre, bias, fcol, frow, logits, gain, kept, merged_delta
    )
    normed_delta = (
        back_dot(q_low, wq)
        + back_dot(k_low, wk)
        + back_dot(v_low, wv)
        + back_dot(forget_low, wf)
        + back_dot(logit_low, wg)
    )
    inputs = tokens.reshape(n, width).astype(f32)
    normed_full, norm_back = jax.vjp(rms_norm, inputs, pre_gain)
    input_delta, pregain_grad = norm_back(normed_delta)
    input_grad = (first_delta + input_delta).astype(bf16)

    lefts = [hidden_t, second_t, merged_t, normed_t]
    if hi > 1:
        lefts = [by_owner(a, hi, lo) for a in lefts]
    rights = [cotan, gate_delta, up_delta, attn_delta, logit_low, q_low, k_low, v_low, forget_low]
    which = (0, 1, 1, 2, 3, 3, 3, 3, 3)
    features = (gate_delta.shape[1],) + (width,) * 8
    plan = []
    for i, (left, right) in enumerate(zip(which, rights)):
        kept_rows = features[i] // (lo * 4)
        columns = right.shape[1]
        plan.append((left, i, columns, -(-kept_rows // 16) * 16, kept_rows, tuple(cut(columns, i % 2))))
    sizes = (width, bias.shape[1], head, width)
    vectors = jnp.concatenate([pregain_grad, bias_grad[0], headgain_grad[0], postgain_grad[0]])
    total = vectors.shape[0]
    vectors = jnp.pad(vectors, (0, -total % 1024)).reshape(8, -1)
    grads, vectors = sum_grads(tuple(plan), lefts, rights, vectors)
    if hi > 1:
        alike = [[a * lo + b for a in range(hi)] for b in range(lo)]
        grads = [
            lax.psum_scatter(g, "seq", scatter_dimension=0, axis_index_groups=alike, tiled=True)
            for g in grads
        ]
        vectors = lax.psum(vectors, "seq", axis_index_groups=alike)
    down_grad, gate_grad, up_grad, output_grad, outgate_grad, query_grad, key_grad, value_grad, forget_grad = grads
    vectors = vectors.reshape(-1)
    ends = [sum(sizes[: i + 1]) for i in range(4)]
    pregain, bias_total, headgain, postgain = [vectors[e - w : e] for e, w in zip(ends, sizes)]
    shape = tokens.shape
    return (
        block_output.reshape(shape), input_grad.reshape(shape), pregain, query_grad, key_grad, value_grad,
        forget_grad, bias_total, outgate_grad, output_grad, headgain, postgain, gate_grad, up_grad, down_grad,
    )


def solution(mesh):
    rows, whole, both = P("fsdp", None), P(), P(("seq", "fsdp"), None)
    return jax.shard_map(
        functools.partial(body, mesh.shape["seq"]),
        mesh=mesh,
        in_specs=(
            P("fsdp", "seq", None), P("fsdp", "seq"), whole, rows, rows, rows, rows, whole, rows, rows,
            whole, whole, rows, rows, rows, P("fsdp", "seq", None),
        ),
        out_specs=(
            P("fsdp", "seq", None), P("fsdp", "seq", None), whole, both, both, both, both, whole, both,
            both, whole, whole, both, both, both,
        ),
        check_vma=False,
    )
```

```python
import functools

import jax
import jax.numpy as jnp
from jax import lax
from jax.experimental import pallas as pl
from jax.experimental.pallas import tpu as pltpu
from jax.sharding import PartitionSpec as P

BLOCK = 64
TILE = 256
norm_eps = 1e-06
f32, bf16 = jnp.float32, jnp.bfloat16
MESH = pl.DeviceIdType.MESH
VMEM = pltpu.VMEM
ANY = pl.ANY
LIMIT = 60 * 2**20


def in_vmem():
    return pl.BlockSpec(memory_space=VMEM)


def in_place():
    return pl.BlockSpec(memory_space=ANY)


def greet(partners):
    barrier = pltpu.get_barrier_semaphore()
    for partner in partners:
        pl.semaphore_signal(barrier, inc=1, device_id=partner, device_id_type=MESH)
    pl.semaphore_wait(barrier, len(partners))


def remote(src, dst, sems, index, partner):
    return pltpu.make_async_remote_copy(
        src_ref=src,
        dst_ref=dst,
        send_sem=sems[0].at[index],
        recv_sem=sems[1].at[index],
        device_id=partner,
        device_id_type=MESH,
    )


def parts_of(a, count):
    if a.dtype == bf16:
        return [a]
    out = []
    for i in range(count):
        part = a.astype(bf16)
        out.append(part)
        if i + 1 < count:
            a = a - part.astype(f32)
    return out


def dot(a, b, ca=1, cb=0, count=1):
    total = None
    for right in reversed(parts_of(b, count)):
        term = lax.dot_general(
            a.astype(bf16), right, (((ca,), (cb,)), ((), ())), preferred_element_type=f32
        )
        total = term if total is None else total + term
    return total


def to_col(row):
    n = row.shape[1]
    i = lax.broadcasted_iota(jnp.int32, (n, n), 0)
    j = lax.broadcasted_iota(jnp.int32, (n, n), 1)
    return jnp.sum(jnp.where(i == j, jnp.broadcast_to(row, (n, n)), 0.0), axis=1, keepdims=True)


def mask_set(flags_col, flags_row):
    n = flags_col.shape[0]
    i = lax.broadcasted_iota(jnp.int32, (n, n), 0)
    j = lax.broadcasted_iota(jnp.int32, (n, n), 1)
    same = (i // BLOCK) == (j // BLOCK)
    lower = jnp.where(same & (i >= j), 1.0, 0.0)
    block = jnp.where(same, 1.0, 0.0)
    seen_col = dot(lower, flags_col)[:, :1]
    all_col = dot(block, flags_col)[:, :1]
    seen_row = dot(flags_row, lower, 1, 1)[:1, :]
    linked = jnp.where(seen_col == seen_row, lower, 0.0)
    fresh = jnp.where(seen_col == 0.0, 1.0, 0.0)
    ending = jnp.where(seen_col == all_col, 1.0, 0.0)
    unbroken = jnp.where(all_col == 0.0, 1.0, 0.0)
    return lower, linked, fresh, ending, unbroken


def gate_set(pre, bias, lower, ending):
    z = pre + bias
    u = jnp.exp(-jnp.abs(z))
    lp = jnp.where(
        u < 0.02, u * (1.0 - u * (0.5 - u * (1.0 / 3.0 - 0.25 * u))), jnp.log(1.0 + u)
    )
    g = (jnp.minimum(z, 0.0) - lp) * 0.125
    series = 1.0 + g * (1.0 / 7.0)
    for order in (6, 5, 4, 3, 2):
        series = 1.0 + g * (1.0 / order) * series
    oma = jnp.where(g > -0.35, -g * series, 1.0 - jnp.exp(g))
    a = dot(lower, g, count=3)
    n, lanes = a.shape
    last = jnp.concatenate(
        [
            jnp.broadcast_to(a[b * BLOCK + BLOCK - 1 : b * BLOCK + BLOCK], (BLOCK, lanes))
            for b in range(n // BLOCK)
        ],
        axis=0,
    )
    tail = jnp.exp(last - a) * ending
    return z, u, oma, jnp.exp(a), jnp.exp(-a), tail


def rows_of(b):
    return slice(b * BLOCK, (b + 1) * BLOCK)


def passing(growth, unbroken, b, hs):
    last = b * BLOCK + BLOCK - 1
    return to_col(growth[last : last + 1, hs] * unbroken[last : last + 1])


def sigmoid(v):
    return 1.0 / (1.0 + jnp.exp(-v))


WEIGHTS = ("key", "value", "forget", "query", "outgate", "output", "gate", "up", "down")
TWICE = ("gate", "up")


def front_kernel(size, heads, grouped, *refs):
    count = len(WEIGHTS)
    shards, refs = dict(zip(WEIGHTS, refs[:count])), refs[count:]
    (tok_ref, cot_ref, pre_gain, post_gain, head_gain, bias_ref, fcol_ref, frow_ref), refs = refs[:8], refs[8:]
    (
        out_ref, first_ref, attn_ref, mdelta_ref, postgain_grad,
        normed_t, merged_t, second_t, hidden_t, gate_delta, up_delta,
        q_ref, k_ref, v_ref, pre_ref, logit_ref,
        mixed_ref, aff_ref, mixing_ref, weight_ref, inner_ref, state_ref, pass_ref, pass_all,
    ), refs = refs[:24], refs[24:]
    passed, refs = dict(zip(WEIGHTS[:5], refs[:5])), refs[5:]
    whole, refs = dict(zip(WEIGHTS, refs[:count])), refs[count:]
    (
        normed, merged, one_ref, second, block_acc, delta_acc, flat_t,
        ends, going, gathered, prefix, came,
        local, send_sem, recv_sem, away, st_send, st_recv,
    ) = refs
    sems = (send_sem, recv_sem)
    s, f = lax.axis_index("seq"), lax.axis_index("fsdp")
    q = lax.rem(s, 4)
    kind_bit = lax.rem(q + q // 2, 2)
    sib, far, nx, nz = (s, f ^ 1), (s, f ^ 2), (s ^ 1, f), (s ^ 2, f)
    fy, fs = f ^ 2, f ^ 3
    others = [(lax.rem(s + d, size), f) for d in range(1, size)]
    greet([sib, far] + others)
    started = []

    def go(copy):
        copy.start()
        started.append(copy)

    def piece(m, owner, start, length):
        rows = shards[m].shape[0]
        return whole[m].at[pl.ds(pl.multiple_of(owner * rows + start, 16), length)]

    def quarter(m, owner, which, half=None):
        rows = shards[m].shape[0] // 4
        first = (rows // 2 + 15) // 16 * 16
        start, length = (0, rows) if half is None else ((0, first), (first, rows - first))[half]
        return piece(m, owner, which * rows + start, length)

    def eighth(m, owner, bit, half):
        rows = shards[m].shape[0] // 2
        return piece(m, owner, bit * rows + half * (rows // 2), rows // 2)

    def mine(m, owner):
        if m in TWICE:
            rows = shards[m].shape[0] // 2
            return piece(m, owner, kind_bit * rows, rows)
        return quarter(m, owner, q)

    def from_x(m, owner):
        return eighth(m, owner, 1 - kind_bit, 0) if m in TWICE else quarter(m, owner, q ^ 1)

    def from_z(m, owner):
        return eighth(m, owner, 1 - kind_bit, 1) if m in TWICE else quarter(m, owner, q ^ 2)

    def send(kind, m, part, partner):
        go(remote(part, part, sems, (kind, WEIGHTS.index(m)), partner))

    def arrived(kind, m, part):
        remote(part, part, sems, (kind, WEIGHTS.index(m)), sib).wait_recv()

    own = {}
    for i, m in enumerate(WEIGHTS):
        rows = shards[m].shape[0]
        if m in TWICE:
            src = shards[m].at[pl.ds(pl.multiple_of(kind_bit * (rows // 2), 16), rows // 2)]
        else:
            src = shards[m].at[pl.ds(pl.multiple_of(q * (rows // 4), 16), rows // 4)]
        go(remote(src, mine(m, f), sems, (1, i), far))
    for i, m in enumerate(WEIGHTS):
        rows = shards[m].shape[0]
        go(remote(shards[m], piece(m, f, 0, rows), sems, (0, i), sib))
        own[m] = pltpu.make_async_copy(shards[m], piece(m, f, 0, rows), local.at[i])
        own[m].start()

    def pump(step):
        if step < count:
            m = WEIGHTS[step]
            part = mine(m, fy)
            arrived(1, m, part)
            if m in TWICE:
                send(2, m, eighth(m, fy, kind_bit, 0), nx)
                send(3, m, eighth(m, fy, kind_bit, 1), nz)
            else:
                send(2, m, part, nx)
                send(3, m, part, nz)
            send(6, m, part, sib)
        if 0 <= step - 1 < count:
            m = WEIGHTS[step - 1]
            arrived(2, m, from_x(m, fy))
            if m not in TWICE:
                send(4, m, quarter(m, fy, q ^ 1, 0), nz)
            send(7, m, from_x(m, fy), sib)
            arrived(3, m, from_z(m, fy))
            if m not in TWICE:
                send(5, m, quarter(m, fy, q ^ 2, 1), nx)
            send(8, m, from_z(m, fy), sib)
        if 0 <= step - 2 < count:
            m = WEIGHTS[step - 2]
            if m not in TWICE:
                for kind in (4, 5):
                    part = quarter(m, fy, q ^ 3, kind - 4)
                    arrived(kind, m, part)
                    send(kind + 5, m, part, sib)

    def ready(m):
        own[m].wait()
        arrived(0, m, piece(m, f ^ 1, 0, shards[m].shape[0]))
        arrived(6, m, mine(m, fs))
        arrived(7, m, from_x(m, fs))
        arrived(8, m, from_z(m, fs))
        if m not in TWICE:
            arrived(9, m, quarter(m, fs, q ^ 3, 0))
            arrived(10, m, quarter(m, fs, q ^ 3, 1))

    n, width = tok_ref.shape
    head = width // heads
    slots = bias_ref.shape[1] // heads
    blocks = n // BLOCK
    streams = 2
    per = blocks // streams
    pairs = heads * streams
    scale = head ** (-0.5)

    def across(columns, step):
        def turn(i, carry):
            step(pl.ds(pl.multiple_of(i * TILE, TILE), TILE))
            return carry

        lax.fori_loop(0, columns // TILE, turn, 0)

    def project(m, to_ref):
        def step(at):
            to_ref[:, at] = dot(normed[...], whole[m][:, at]).astype(to_ref.dtype)

        across(whole[m].shape[1], step)

    def turn_over(source, to_ref, rows, padded):
        if not grouped:
            to_ref[...] = source[...].astype(bf16)
            return
        for group in range(16):
            for core in range(2):
                at = (group * 2 + core) * rows
                to_ref[core, group * padded : group * padded + rows] = source[at : at + rows].astype(bf16)

    inputs = tok_ref[...].astype(f32)
    unit = inputs * lax.rsqrt(jnp.mean(inputs * inputs, axis=1, keepdims=True) + norm_eps)
    scaled = unit * pre_gain[...]
    normed[...] = scaled.astype(bf16)
    turn_over(scaled.T, normed_t, width // 32, width // 32)
    for step in range(5):
        pump(step)
    for m, to_ref in (("key", k_ref), ("value", v_ref), ("forget", pre_ref)):
        ready(m)
        project(m, to_ref)
    lower, linked, fresh, ending, unbroken = mask_set(fcol_ref[...], frow_ref[...])
    z, u, oma, growth, inverse, tail = gate_set(pre_ref[...], bias_ref[...], lower, ending)
    shrink, kept = inverse * oma, tail * oma
    for h in range(heads):
        hs, hd = slice(h * slots, (h + 1) * slots), slice(h * head, (h + 1) * head)
        for stream in range(streams):
            pair = h * streams + stream
            total, through = None, None
            for b in range(stream * per, (stream + 1) * per):
                part = kept[rows_of(b), hs].astype(bf16)
                at = pair * per + b % per
                end_k = dot(part, k_ref[rows_of(b), hd], 0, 0)
                end_v = dot(part, v_ref[rows_of(b), hd], 0, 0)
                ends[at, :, :head] = end_k
                ends[at, :, head:] = end_v
                factor = passing(growth, unbroken, b, hs)
                pass_ref[at] = jnp.broadcast_to(factor, pass_ref.shape[1:])
                if total is None:
                    total, through = (end_k, end_v), factor
                else:
                    total = (factor * total[0] + end_k, factor * total[1] + end_v)
                    through = through * factor
            at = slice(pair * slots, (pair + 1) * slots)
            going[at, :head] = total[0].astype(bf16)
            going[at, head : 2 * head] = total[1].astype(bf16)
            going[at, 2 * head :] = jnp.broadcast_to(through, (slots, going.shape[1] - 2 * head)).astype(bf16)

    share = pairs * slots // size

    def rows_for(place):
        return pl.ds(pl.multiple_of(place * share, 16), share)

    first_hop, second_hop = [], []
    for d in range(1, size):
        to = others[d - 1]
        copy = remote(going.at[rows_for(to[0])], gathered.at[s], (st_send, st_recv), (0, d - 1), to)
        go(copy)
        first_hop.append(lax.rem(s + size - d, size))
    gathered[s] = going[rows_for(s)]
    pump(5)
    pump(6)
    for m, to_ref in (("query", q_ref), ("outgate", logit_ref)):
        ready(m)
        project(m, to_ref)
    for i, m in enumerate(WEIGHTS[:5]):
        copy = pltpu.make_async_copy(whole[m], passed[m], away.at[i])
        copy.start()
        own[m] = copy
    for d in range(1, size):
        source = first_hop[d - 1]
        remote(gathered.at[source], gathered.at[source], (st_send, st_recv), (0, d - 1), sib).wait_recv()
    state = jnp.zeros((share, 2 * head), f32)
    for place in range(size):
        prefix[place] = state.astype(bf16)
        entry = gathered[place].astype(f32)
        pass_all[place] = gathered[place][:, 2 * head :]
        state = entry[:, 2 * head : 2 * head + 1] * state + entry[:, : 2 * head]
    for d in range(1, size):
        to = others[d - 1]
        go(remote(prefix.at[to[0]], came.at[rows_for(s)], (st_send, st_recv), (1, d - 1), to))
    came[rows_for(s)] = prefix[s]
    pump(7)
    for h in range(heads):
        hd = slice(h * head, (h + 1) * head)
        aff_ref[h] = (dot(q_ref[:, hd], k_ref[:, hd], 1, 1) * (linked * scale)).astype(bf16)
    for d in range(1, size):
        part = came.at[rows_for(first_hop[d - 1])]
        remote(part, part, (st_send, st_recv), (1, d - 1), sib).wait_recv()
    pump(8)
    for h in range(heads):
        hs, hd = slice(h * slots, (h + 1) * slots), slice(h * head, (h + 1) * head)
        for stream in range(streams):
            pair = h * streams + stream
            state = came[pair * slots : (pair + 1) * slots].astype(f32)
            for b in range(per):
                at = pair * per + b
                state_ref[pair, b] = state.astype(bf16)
                state = pass_ref[at][:, :1] * state + ends[at]
            state_ref[pair, per] = state.astype(bf16)
        gr, sh = growth[:, hs], shrink[:, hs]
        qh, vh = q_ref[:, hd], v_ref[:, hd]
        carried = jnp.concatenate(
            [
                dot(qh[rows_of(b)], state_ref[h * streams + b // per, b % per, :, :head], 1, 1)
                for b in range(blocks)
            ],
            axis=0,
        )
        inner = dot(aff_ref[h], sh) + carried * (scale * fresh)
        scores = gr * inner
        e = jnp.exp(scores - jnp.max(scores, axis=1, keepdims=True))
        weights = e / jnp.sum(e, axis=1, keepdims=True)
        weight_ref[:, hs] = weights
        inner_ref[:, hs] = inner
        lifted = weights * gr
        mixing = (dot(lifted, sh.astype(bf16), 1, 1) * linked).astype(bf16)
        mixing_ref[h] = mixing
        brought = jnp.concatenate(
            [
                dot(lifted[rows_of(b)], state_ref[h * streams + b // per, b % per, :, head:])
                for b in range(blocks)
            ],
            axis=0,
        )
        mixed = dot(mixing, vh) + brought * fresh
        mixed_ref[:, hd] = mixed
        r = lax.rsqrt(jnp.mean(mixed * mixed, axis=1, keepdims=True) + norm_eps)
        logits = logit_ref[:, hd]
        delta_acc[:, hd] = mixed * r * head_gain[...] * (logits * sigmoid(logits))
        merged[:, hd] = delta_acc[:, hd].astype(bf16)
    ready("output")

    def join(at):
        one_ref[:, at] = tok_ref[:, at].astype(f32) + dot(merged[...], whole["output"][:, at])

    across(width, join)
    turn_over(delta_acc[...].T, merged_t, width // 32, width // 32)
    one = one_ref[...]
    scaled = one * lax.rsqrt(jnp.mean(one * one, axis=1, keepdims=True) + norm_eps) * post_gain[...]
    second[...] = scaled.astype(bf16)
    turn_over(scaled.T, second_t, width // 32, width // 32)
    pump(9)
    pump(10)
    ready("gate")
    ready("up")
    ready("down")
    block_acc[...] = one
    delta_acc[...] = jnp.zeros_like(delta_acc)

    def unit_tile(i, carry):
        at = pl.ds(pl.multiple_of(i * TILE, TILE), TILE)
        w_gate, w_up, w_down = whole["gate"][:, at], whole["up"][:, at], whole["down"][at]
        gate_vals, up_vals = dot(second[...], w_gate), dot(second[...], w_up)
        sig = sigmoid(gate_vals)
        silu = gate_vals * sig
        full = silu * up_vals
        flat_t[at] = full.T
        hidden_delta = dot(cot_ref[...], w_down, 1, 1)
        d_up = (hidden_delta * silu).astype(bf16)
        d_gate = (hidden_delta * up_vals * (sig + silu * (1.0 - sig))).astype(bf16)
        gate_delta[:, at] = d_gate
        up_delta[:, at] = d_up
        block_acc[...] += dot(full, w_down)
        delta_acc[...] += dot(d_gate, w_gate, 1, 1) + dot(d_up, w_up, 1, 1)
        return carry

    ff = whole["down"].shape[0]
    lax.fori_loop(0, ff // TILE, unit_tile, 0)
    out_ref[...] = block_acc[...].astype(bf16)
    turn_over(flat_t, hidden_t, ff // 32, -(-(ff // 32) // 16) * 16)
    one = one_ref[...]
    r = lax.rsqrt(jnp.mean(one * one, axis=1, keepdims=True) + norm_eps)
    unit = one * r
    delta = delta_acc[...]
    postgain_grad[...] = jnp.sum(delta * unit, axis=0, keepdims=True)
    delta = delta * post_gain[...]
    first = cot_ref[...].astype(f32) + r * (delta - unit * jnp.mean(unit * delta, axis=1, keepdims=True))
    first_ref[...] = first
    attn_ref[...] = first.astype(bf16)

    def split(at):
        mdelta_ref[:, at] = dot(attn_ref[...], whole["output"][at], 1, 1)

    across(width, split)
    for m in WEIGHTS[:5]:
        own[m].wait()
    for copy in started:
        copy.wait_send()


def front(size, heads, grouped, shards, tokens, cotan, pre_gain, post_gain, head_gain, bias, fcol, frow):
    n, width = tokens.shape
    head, slots = width // heads, bias.shape[1] // heads
    pairs, per = heads * 2, n // BLOCK // 2
    ff = shards["gate"].shape[1]
    shards = [shards[m] for m in WEIGHTS]
    count = len(shards)
    padded = -(-(ff // 32) // 16) * 512

    def turned(rows, grouped_rows):
        shape = (2, grouped_rows // 2, n) if grouped else (rows, n)
        return jax.ShapeDtypeStruct(shape, bf16)

    def low(*shape):
        return jax.ShapeDtypeStruct(shape, bf16)

    def full(*shape):
        return jax.ShapeDtypeStruct(shape, f32)

    outs = [
        low(n, width), full(n, width), low(n, width), full(n, width), full(1, width),
        turned(width, width), turned(width, width), turned(width, width), turned(ff, padded),
        low(n, ff), low(n, ff),
        low(n, width), low(n, width), low(n, width), full(n, heads * slots), full(n, width),
        full(n, width), low(heads, n, n), low(heads, n, n), full(n, heads * slots), full(n, heads * slots),
        low(pairs, per + 1, slots, 2 * head), full(pairs * per, slots, 128),
        low(size, pairs * slots // size, 128),
    ]
    wholes = [low(4 * w.shape[0], w.shape[1]) for w in shards]
    share = pairs * slots // size
    dma = pltpu.SemaphoreType.DMA
    got = pl.pallas_call(
        functools.partial(front_kernel, size, heads, grouped),
        name="front",
        out_shape=outs + wholes[:5],
        in_specs=[in_place()] * count + [in_vmem()] * 8,
        out_specs=[in_vmem()] * len(outs) + [in_place()] * 5,
        scratch_shapes=[VMEM(w.shape, bf16) for w in wholes]
        + [
            VMEM((n, width), bf16),
            VMEM((n, width), bf16),
            VMEM((n, width), f32),
            VMEM((n, width), bf16),
            VMEM((n, width), f32),
            VMEM((n, width), f32),
            VMEM((ff, n), f32),
            VMEM((pairs * per, slots, 2 * head), f32),
            VMEM((pairs * slots, 2 * head + 128), bf16),
            VMEM((size, share, 2 * head + 128), bf16),
            VMEM((size, share, 2 * head), bf16),
            VMEM((pairs * slots, 2 * head), bf16),
            dma((count,)),
            dma((11, count)),
            dma((11, count)),
            dma((5,)),
            dma((2, size - 1)),
            dma((2, size - 1)),
        ],
        compiler_params=pltpu.CompilerParams(
            collective_id=1, has_side_effects=True, vmem_limit_bytes=LIMIT
        ),
    )(*shards, tokens, cotan, pre_gain, post_gain, head_gain, bias, fcol, frow)
    return got


def to_row(col):
    n = col.shape[0]
    i = lax.broadcasted_iota(jnp.int32, (n, n), 0)
    j = lax.broadcasted_iota(jnp.int32, (n, n), 1)
    return jnp.sum(jnp.where(i == j, jnp.broadcast_to(col, (n, n)), 0.0), axis=0, keepdims=True)


LEAST, SHALLOW, DEEP = 4.0, 8.0, 10.0
STRIPS = 3
BACK_LIMIT = 63 * 2**20


def cut(columns, flip):
    tiles = columns // TILE
    if tiles <= 1:
        half = columns // 2
        return [(0, half, flip), (half, half, 1 - flip)]
    pieces = 4 if tiles <= 4 else 6
    out, start = [], 0
    for i in range(pieces):
        count = tiles // pieces + (1 if i < tiles % pieces else 0)
        out.append((start, count * TILE, (i + flip) % 2))
        start += count * TILE
    return out


def in_order(chunks, path, held_back, least, shallow, deep):
    now, free = 0.0, dict.fromkeys(("x", "y", "z", "zz"), 0.0)
    came, done, coming, out = {}, set(), [], []
    path, left = list(path), list(range(len(chunks)))
    rate, delay = 0.045, 2.0

    def leave(c, stage):
        rows, width, order = chunks[c][1], chunks[c][3], chunks[c][4]
        link = (("y", "z", "x", "zz"), ("x", "z", "y", "zz"))[order][stage]
        size = 16 * rows * width * 2 / 1e6 / 2 ** (stage + 1)
        free[link] = max(now, free[link]) + size / rate * (2 if stage == 3 else 1)
        coming.append((free[link] + delay, c, stage))

    while left or path or coming:
        here = sorted(a for a in coming if a[0] <= now)
        open_ = [c for c in left if held_back.get(chunks[c][0], None) in done or chunks[c][0] not in held_back]
        depth = deep if "second hop" in done else shallow
        queue = free[("y", "x")[chunks[open_[0]][4]]] - now if open_ else 0.0
        ready = path and came.get(path[0][2], 0.0 if path[0][2] is None else 1e9) <= now
        if here:
            _, c, stage = here[0]
            coming.remove(here[0])
            now += 0.1 + 0.1 * chunks[c][1] / 32 * chunks[c][3] / TILE / 2**stage
            out.append(("advance", c, stage))
            if stage < 3:
                leave(c, stage + 1)
        elif ready and not (open_ and queue < least):
            name, time, _, starts, takes = path.pop(0)
            now += time
            done.add(name)
            out.append(("path", name, None))
            if starts:
                came[starts] = now + takes
        elif open_ and queue < depth:
            c = open_[0]
            left.remove(c)
            now += 0.1 + 0.3 * chunks[c][1] / 32 * chunks[c][3] / TILE
            out.append(("produce", c, None))
            leave(c, 0)
        else:
            later = [a[0] for a in coming]
            if path and path[0][2] in came:
                later.append(came[path[0][2]])
            if open_:
                later.append(now + queue - depth)
            now = max(now + 0.05, min(later))
    return out


FORM = (("cotan", 0), ("gate", 1), ("up", 1), ("attn", 2), ("outgate", 3), ("query", 3), ("key", 3), ("value", 3), ("forget", 3))
SAVED = ("q", "k", "v", "pre", "logits", "mixed", "aff", "mixing", "weights", "inner", "state", "pass", "mdelta", "pass_all")


def back_kernel(size, heads, plan, *refs):
    def take(count):
        nonlocal refs
        got, refs = refs[:count], refs[count:]
        return got

    lefts, rights, saved = take(4), take(4), dict(zip(SAVED, take(len(SAVED))))
    weights, (first_in, tokens_in) = take(5), take(2)
    bias_ref, fcol_ref, frow_ref, head_gain, pre_gain, postgain_ref = take(6)
    outs, (vec_out, input_grad) = take(9), take(2)
    left_all, right_all = take(4), take(9)
    have_ref = dict(zip(SAVED, take(len(SAVED))))
    chunks = [(g, p[2]) + c for g, p in enumerate(plan) for c in p[4]]
    nc = len(chunks)
    sums = take(nc)
    landed = [take(nc) for _ in range(4)]
    owed, da_acc, doma_acc, strip, going, gathered, prefix, came, vec_acc, vec_got = take(10)
    loads, in_local, in_send, in_recv, strip_sem, first_sem = take(6)
    hop_send, hop_recv, st_send, st_recv, v_send, v_recv = take(6)
    q_ref, k_ref, v_ref = have_ref["q"], have_ref["k"], have_ref["v"]
    logit_ref, mixed_ref, mdelta_ref = have_ref["logits"], have_ref["mixed"], have_ref["mdelta"]
    state_ref, pass_ref = have_ref["state"], have_ref["pass"]

    s, f = lax.axis_index("seq"), lax.axis_index("fsdp")
    core, y = lax.rem(f, 2), f // 2
    x, z_low, z_high = lax.rem(s, 2), lax.rem(s // 2, 2), lax.rem(s // 4, 2)
    sib, far, nx, nz, nzz = (s, f ^ 1), (s, f ^ 2), (s ^ 1, f), (s ^ 2, f), (s ^ 4, f)
    others = [(lax.rem(s + d, size), f) for d in range(1, size)]
    greet([sib, far] + others)
    started = []

    def go(copy):
        copy.start()
        started.append(copy)

    n, width = q_ref.shape
    head = width // heads
    slots = bias_ref.shape[1] // heads
    blocks = n // BLOCK
    streams = 2
    per = blocks // streams
    pairs = heads * streams
    scale = head ** (-0.5)
    share = pairs * slots // size

    waiting = {}

    def fetch_left(i):
        keep = pltpu.make_async_copy(lefts[i].at[core], left_all[i].at[:, pl.ds(0, n)], in_local.at[i])
        keep.start()
        copy = remote(lefts[i].at[1 - core], left_all[i].at[:, pl.ds(n, n)], (in_send, in_recv), i, sib)
        go(copy)
        waiting["left", i] = [keep, copy]

    def fetch_right(i):
        own, other = right_all[i].at[pl.ds(0, n)], right_all[i].at[pl.ds(n, n)]
        keep = None
        src = own
        if i < 4:
            src = rights[i]
            keep = pltpu.make_async_copy(src, own, in_local.at[4 + i])
            keep.start()
        copy = remote(src, other, (in_send, in_recv), 4 + i, sib)
        go(copy)
        waiting["right", i] = [keep, copy]

    def have(kind, i):
        pair = waiting[kind, i]
        if pair:
            if pair[0] is not None:
                pair[0].wait()
            pair[1].wait_recv()
            waiting[kind, i] = None

    fetch_left(0)
    fetch_right(0)
    loading = []
    for i, name in enumerate(SAVED):
        copy = pltpu.make_async_copy(saved[name], have_ref[name], loads.at[i])
        copy.start()
        loading.append(copy)
    for i in (1, 2, 3):
        fetch_right(i)
    for i in (1, 2, 3):
        fetch_left(i)

    strips = [(w, t * TILE) for w in range(5) for t in range(weights[w].shape[1] // TILE)]

    def strip_copy(i):
        w, at = strips[i]
        return pltpu.make_async_copy(weights[w].at[:, pl.ds(at, TILE)], strip.at[i % STRIPS], strip_sem.at[i % STRIPS])

    for i in range(STRIPS):
        strip_copy(i).start()

    def route(c):
        if chunks[c][4]:
            return (x, z_low, y, z_high), (nx, nz, far, nzz)
        return (y, z_low, x, z_high), (far, nz, nx, nzz)

    def stage_copy(c, stage):
        bits, partners = route(c)
        at = bits[:stage] + (1 - bits[stage],)
        return remote(sums[c].at[at], landed[stage][c], (st_send, st_recv), (stage, c), partners[stage])

    def produce(c):
        g, rows, start, wide, order = chunks[c]
        left = plan[g][0]
        have("left", left)
        have("right", g)
        tile = min(TILE, wide)

        def turn(i, carry):
            at = pl.multiple_of(start + i * tile, 128)
            to = pl.multiple_of(i * tile, 128)
            got = jnp.dot(
                left_all[left][...], right_all[g][:, pl.ds(at, tile)], preferred_element_type=f32
            ).astype(bf16)
            for group in range(16):
                zh, zl, xx, yy = (group >> 3) & 1, (group >> 2) & 1, (group >> 1) & 1, group & 1
                place = (xx, zl, yy, zh) if order else (yy, zl, xx, zh)
                sums[c][*place, :, pl.ds(to, tile)] = got[group * rows : (group + 1) * rows]
            return carry

        lax.fori_loop(0, wide // tile, turn, 0)
        go(stage_copy(c, 0))

    def advance(c, stage):
        stage_copy(c, stage).wait_recv()
        bits, _ = route(c)
        if stage == 3:
            g, rows, start, wide, _ = chunks[c]
            total = sums[c][bits].astype(f32) + landed[3][c][...].astype(f32)
            outs[g][:, start : start + wide] = total[: plan[g][3]]
            return
        for rest in range(1 << (3 - stage)):
            tail = tuple((rest >> k) & 1 for k in reversed(range(3 - stage)))
            at = bits[: stage + 1] + tail
            sums[c][at] = (sums[c][at].astype(f32) + landed[stage][c][tail].astype(f32)).astype(bf16)
        go(stage_copy(c, stage + 1))

    keep = {}

    def begin():
        for copy in loading:
            copy.wait()
        lower, linked, fresh, ending, unbroken = mask_set(fcol_ref[...], frow_ref[...])
        z, u, oma, growth, inverse, tail = gate_set(have_ref["pre"][...], bias_ref[...], lower, ending)
        keep.update(lower=lower, linked=linked, fresh=fresh, z=z, u=u, oma=oma, growth=growth)
        keep.update(inverse=inverse, tail=tail, shrink=inverse * oma, kept=tail * oma)
        keep["gain"] = jnp.zeros((1, head), f32)

    def states(h, b):
        return state_ref.at[h * streams + b // per, b % per]

    def one_head(h):
        linked, fresh, growth, shrink = keep["linked"], keep["fresh"], keep["growth"], keep["shrink"]
        hs, hd = slice(h * slots, (h + 1) * slots), slice(h * head, (h + 1) * head)
        mixed, logits, delta = mixed_ref[:, hd], logit_ref[:, hd], mdelta_ref[:, hd]
        r = lax.rsqrt(jnp.mean(mixed * mixed, axis=1, keepdims=True) + norm_eps)
        sig = sigmoid(logits)
        silu = logits * sig
        unit = mixed * r
        dy = delta * silu
        right_all[4][0:n, hd] = (delta * unit * head_gain[...] * (sig + silu * (1.0 - sig))).astype(bf16)
        keep["gain"] = keep["gain"] + jnp.sum(dy * unit, axis=0, keepdims=True)
        dy = dy * head_gain[...]
        dmixed = r * (dy - unit * jnp.mean(unit * dy, axis=1, keepdims=True))
        gr, sh = growth[:, hs], shrink[:, hs].astype(bf16)
        weigh, inner = have_ref["weights"][:, hs], have_ref["inner"][:, hs]
        aff, mixing = have_ref["aff"][h], have_ref["mixing"][h]
        qh, kh, vh = q_ref[:, hd], k_ref[:, hd], v_ref[:, hd]
        do = dmixed.astype(bf16)
        lifted = (weigh * gr).astype(bf16)
        dm = (dot(do, vh, 1, 1) * linked).astype(bf16)
        mixed_ref[:, hd] = dot(mixing, do, 0, 0)
        fdo = (dmixed * fresh).astype(bf16)
        dlift = dot(dm, sh) + jnp.concatenate(
            [dot(fdo[rows_of(b)], states(h, b)[:, head:], 1, 1) for b in range(blocks)], axis=0
        )
        dsh = dot(dm, lifted, 0, 0)
        dw = dlift * gr
        dsc = weigh * (dw - jnp.sum(weigh * dw, axis=1, keepdims=True))
        du = dsc * gr
        du_low = du.astype(bf16)
        da = (dot(du_low, sh, 1, 1) * (linked * scale)).astype(bf16)
        dsh = dsh + dot(aff, du_low, 0, 0)
        fdu = (du * (fresh * scale)).astype(bf16)
        right_all[5][0:n, hd] = (
            dot(da, kh)
            + jnp.concatenate([dot(fdu[rows_of(b)], states(h, b)[:, :head]) for b in range(blocks)], axis=0)
        ).astype(bf16)
        mdelta_ref[:, hd] = dot(da, qh, 0, 0)
        for stream in range(streams):
            pair = h * streams + stream
            total = None
            for b in reversed(range(stream * per, (stream + 1) * per)):
                at = pair * per + b % per
                own_k = dot(fdu[rows_of(b)], qh[rows_of(b)], 0, 0)
                own_v = dot(lifted[rows_of(b)], fdo[rows_of(b)], 0, 0)
                owed[at, :, :head] = own_k.astype(bf16)
                owed[at, :, head:] = own_v.astype(bf16)
                if total is not None:
                    factor = pass_ref[at][:, :1]
                    own_k, own_v = own_k + factor * total[0], own_v + factor * total[1]
                total = (own_k, own_v)
            at = slice(pair * slots, (pair + 1) * slots)
            going[at, :head] = total[0].astype(bf16)
            going[at, head:] = total[1].astype(bf16)
        da_acc[:, hs] = lifted.astype(f32) * dlift + du_low.astype(f32) * inner - dsh * sh.astype(f32)
        doma_acc[:, hs] = dsh * keep["inverse"][:, hs]

    def rows_for(place):
        return pl.ds(pl.multiple_of(place * share, 16), share)

    sources = [lax.rem(s + size - d, size) for d in range(1, size)]

    def first_hop():
        for d in range(1, size):
            to = others[d - 1]
            go(remote(going.at[rows_for(to[0])], gathered.at[s], (hop_send, hop_recv), (0, d - 1), to))
        gathered[s] = going[rows_for(s)]
        fetch_right(4)
        fetch_right(5)

    def second_hop():
        for d in range(1, size):
            part = gathered.at[sources[d - 1]]
            remote(part, part, (hop_send, hop_recv), (0, d - 1), sib).wait_recv()
        state = jnp.zeros((share, 2 * head), f32)
        for place in reversed(range(size)):
            prefix[place] = state.astype(bf16)
            state = have_ref["pass_all"][place][:, :1].astype(f32) * state + gathered[place].astype(f32)
        for d in range(1, size):
            to = others[d - 1]
            go(remote(prefix.at[to[0]], came.at[rows_for(s)], (hop_send, hop_recv), (1, d - 1), to))
        came[rows_for(s)] = prefix[s]

    def last_hop():
        for d in range(1, size):
            part = came.at[rows_for(sources[d - 1])]
            remote(part, part, (hop_send, hop_recv), (1, d - 1), sib).wait_recv()

    def end_head(h):
        kept, tail = keep["kept"], keep["tail"]
        row = lax.broadcasted_iota(jnp.int32, (BLOCK, 1), 0)
        hs, hd = slice(h * slots, (h + 1) * slots), slice(h * head, (h + 1) * head)
        for stream in range(streams):
            pair = h * streams + stream
            leaving = came[pair * slots : (pair + 1) * slots].astype(f32)
            for i in reversed(range(per)):
                at, rb = pair * per + i, rows_of(stream * per + i)
                low = leaving.astype(bf16)
                part = kept[rb, hs].astype(bf16)
                dkept = dot(k_ref[rb, hd], low[:, :head], 1, 1) + dot(v_ref[rb, hd], low[:, head:], 1, 1)
                right_all[6][rb, hd] = (mdelta_ref[rb, hd] + dot(part, low[:, :head])).astype(bf16)
                right_all[7][rb, hd] = (mixed_ref[rb, hd] + dot(part, low[:, head:])).astype(bf16)
                held = jnp.sum(low.astype(f32) * state_ref[pair, i + 1].astype(f32), axis=1, keepdims=True)
                da_acc[rb, hs] = (
                    da_acc[rb, hs] - dkept * part.astype(f32) + jnp.where(row == BLOCK - 1, to_row(held), 0.0)
                )
                doma_acc[rb, hs] = doma_acc[rb, hs] + dkept * tail[rb, hs]
                if i > 0:
                    leaving = owed[at].astype(f32) + pass_ref[at][:, :1] * leaving

    def end_gates():
        fetch_right(6)
        fetch_right(7)
        z, u = keep["z"], keep["u"]
        dg = dot(keep["lower"], da_acc[...], 0, 0, count=3) - doma_acc[...] * (1.0 - keep["oma"])
        sig = jnp.where(z >= 0.0, u / (1.0 + u), 1.0 / (1.0 + u))
        dpre = dg * sig * 0.125
        right_all[8][0:n] = dpre.astype(bf16)
        fetch_right(8)
        pltpu.make_async_copy(first_in, mdelta_ref, first_sem.at[0]).start()
        pltpu.make_async_copy(tokens_in, q_ref, first_sem.at[1]).start()
        vec_acc[0] = jnp.zeros(vec_acc.shape[1:], f32)
        vec_acc[0, 1:2, : dpre.shape[1]] = jnp.sum(dpre, axis=0, keepdims=True)
        vec_acc[0, 2:3, :head] = keep["gain"]
        vec_acc[0, 3:4, :] = postgain_ref[...]

    def strip_step(i):
        strip_copy(i).wait()
        w, at = strips[i]
        term = dot(right_all[(6, 7, 8, 5, 4)[w]][0:n, at : at + TILE], strip[i % STRIPS], 1, 1)
        logit_ref[...] = term if i == 0 else logit_ref[...] + term
        if i + STRIPS < len(strips):
            strip_copy(i + STRIPS).start()

    def end_norm():
        pltpu.make_async_copy(first_in, mdelta_ref, first_sem.at[0]).wait()
        pltpu.make_async_copy(tokens_in, q_ref, first_sem.at[1]).wait()
        inputs = q_ref[...].astype(f32)
        r = lax.rsqrt(jnp.mean(inputs * inputs, axis=1, keepdims=True) + norm_eps)
        unit = inputs * r
        delta = logit_ref[...]
        vec_acc[0, 0:1, :] = jnp.sum(delta * unit, axis=0, keepdims=True)
        delta = delta * pre_gain[...]
        input_grad[...] = (
            mdelta_ref[...] + r * (delta - unit * jnp.mean(unit * delta, axis=1, keepdims=True))
        ).astype(bf16)
        go(v_copy(0))

    def v_copy(i):
        return remote(vec_acc.at[i], vec_got.at[i], (v_send, v_recv), i, (sib, far, nx, nz, nzz)[i])

    def vector(i):
        v_copy(i).wait_recv()
        total = vec_acc[i] + vec_got[i]
        if i == 4:
            vec_out[...] = total
            return
        vec_acc[i + 1] = total
        go(v_copy(i + 1))

    steps = {"begin": begin}
    path = [("begin", 2.0, None, None, 0)]
    for h in range(heads):
        steps["head", h] = functools.partial(one_head, h)
        path.append((("head", h), 3.0, None, None, 0))
    steps.update({"first hop": first_hop, "second hop": second_hop, "last hop": last_hop})
    path.append(("first hop", 0.5, None, "first", 12.0))
    path.append(("second hop", 1.0, "first", "second", 12.0))
    path.append(("last hop", 0.1, "second", None, 0))
    for h in range(heads):
        steps["end", h] = functools.partial(end_head, h)
        path.append((("end", h), 1.2, None, None, 0))
    steps["gates"] = end_gates
    path.append(("gates", 1.0, None, None, 0))
    for i in range(len(strips)):
        steps["strip", i] = functools.partial(strip_step, i)
        path.append((("strip", i), 0.4, None, None, 0))
    steps["norm"] = end_norm
    path.append(("norm", 1.5, None, ("vector", 0), 3.0))
    for i in range(5):
        steps["vector", i] = functools.partial(vector, i)
        path.append((("vector", i), 0.1, ("vector", i), ("vector", i + 1), 4.0))
    held_back = {4: "first hop", 5: "first hop", 6: "gates", 7: "gates", 8: "gates"}
    for what, which, stage in in_order(chunks, path, held_back, LEAST, SHALLOW, DEEP):
        if what == "path":
            steps[which]()
        elif what == "produce":
            produce(which)
        else:
            advance(which, stage)
    for copy in started:
        copy.wait_send()


def back(size, heads, plan, lefts, rights, saved, weights, first, tokens, bias, fcol, frow, head_gain, pre_gain, postgain):
    n, width = saved["q"].shape
    head, slots = width // heads, bias.shape[1] // heads
    pairs, per = heads * 2, n // BLOCK // 2
    share = pairs * slots // size
    chunks = [(p[2],) + c for p in plan for c in p[4]]
    nc = len(chunks)
    dma = pltpu.SemaphoreType.DMA
    saved = [saved[name] for name in SAVED]
    scratch = [VMEM((a.shape[1], 2 * n), bf16) for a in lefts]
    scratch += [VMEM((2 * n, p[1]), bf16) for p in plan]
    scratch += [VMEM(a.shape, a.dtype) for a in saved]
    for lead in ((2, 2, 2, 2), (2, 2, 2), (2, 2), (2,), ()):
        scratch += [VMEM(lead + (r, w), bf16) for r, _, w, _ in chunks]
    scratch += [
        VMEM((pairs * per, slots, 2 * head), bf16),
        VMEM((n, heads * slots), f32),
        VMEM((n, heads * slots), f32),
        VMEM((STRIPS, width, TILE), bf16),
        VMEM((pairs * slots, 2 * head), bf16),
        VMEM((size, share, 2 * head), bf16),
        VMEM((size, share, 2 * head), bf16),
        VMEM((pairs * slots, 2 * head), bf16),
        VMEM((5, 8, width), f32),
        VMEM((5, 8, width), f32),
        dma((len(SAVED),)),
        dma((8,)),
        dma((13,)),
        dma((13,)),
        dma((STRIPS,)),
        dma((2,)),
        dma((2, size - 1)),
        dma((2, size - 1)),
        dma((4, nc)),
        dma((4, nc)),
        dma((5,)),
        dma((5,)),
    ]
    out = pl.pallas_call(
        functools.partial(back_kernel, size, heads, plan),
        name="back",
        out_shape=[jax.ShapeDtypeStruct((p[3], p[1]), f32) for p in plan]
        + [jax.ShapeDtypeStruct((8, width), f32), jax.ShapeDtypeStruct((n, width), bf16)],
        in_specs=[in_place()] * (8 + len(saved) + 7) + [in_vmem()] * 6,
        out_specs=[in_vmem()] * (len(plan) + 2),
        scratch_shapes=scratch,
        compiler_params=pltpu.CompilerParams(
            collective_id=2, has_side_effects=True, vmem_limit_bytes=BACK_LIMIT
        ),
    )(*lefts, *rights, *saved, *weights, first, tokens, bias, fcol, frow, head_gain, pre_gain, postgain)
    return out[: len(plan)], out[-2], out[-1]


def by_owner(a, hi, lo):
    features, tokens = a.shape
    r = features // (hi * lo * 4)
    t = a.reshape(hi, lo, 2, 2, r, tokens).transpose(3, 1, 2, 0, 4, 5).reshape(2, lo * 2, hi * r, tokens)
    pad = -(hi * r) % 16
    if pad:
        t = jnp.pad(t, ((0, 0), (0, 0), (0, pad), (0, 0)))
    return t.reshape(2, -1, tokens)


def body(
    size, tokens, resets, pre_gain, query_weight, key_weight, value_weight, forget_weight, forget_bias,
    outgate_weight, output_weight, head_gain, post_gain, gate_weight, up_weight, down_weight, cotangent,
):
    lo = 8
    hi = size // lo
    streams, length, width = tokens.shape
    n = streams * length
    head = head_gain.shape[0]
    heads = width // head
    shards = {
        "query": query_weight, "key": key_weight, "value": value_weight, "forget": forget_weight,
        "outgate": outgate_weight, "output": output_weight, "gate": gate_weight, "up": up_weight, "down": down_weight,
    }
    ff = gate_weight.shape[1]
    flat, cotan = tokens.reshape(n, width), cotangent.reshape(n, width)
    flags = resets.reshape(n).astype(f32)
    fcol = jnp.broadcast_to(flags[:, None], (n, 128))
    frow = jnp.broadcast_to(flags[None], (8, n))
    bias, gain = forget_bias[None], head_gain[None]
    (
        block_output, first_delta, attn_delta, merged_delta, postgain_grad,
        normed_t, merged_t, second_t, hidden_t, gate_delta, up_delta,
        q, k, v, pre, logits, mixed, aff, mixing, weights, inner, state, passed, pass_all, *wholes,
    ) = front(
        size, heads, hi == 1, shards, flat, cotan, pre_gain[None], post_gain[None],
        gain, bias, fcol, frow,
    )
    lefts = [hidden_t, second_t, merged_t, normed_t]
    if hi > 1:
        lefts = [by_owner(a, hi, lo) for a in lefts]
    rights = [cotan, gate_delta, up_delta, attn_delta]
    columns = (width, ff, ff, width, width, width, width, width, bias.shape[1])
    plan = []
    for i, (name, left) in enumerate(FORM):
        kept_rows = (ff if i == 0 else width) // (lo * 4)
        plan.append((left, columns[i], -(-kept_rows // 16) * 16, kept_rows, tuple(cut(columns[i], i % 2))))
    saved = dict(
        q=q, k=k, v=v, pre=pre, logits=logits, mixed=mixed, aff=aff, mixing=mixing, weights=weights, inner=inner,
        state=state, mdelta=merged_delta, pass_all=pass_all,
    )
    saved["pass"] = passed
    grads, vectors, input_grad = back(
        size, heads, tuple(plan), lefts, rights, saved, wholes, first_delta, flat, bias, fcol, frow, gain,
        pre_gain[None], postgain_grad,
    )
    if hi > 1:
        alike = [[a * lo + b for a in range(hi)] for b in range(lo)]
        grads = [
            lax.psum_scatter(g, "seq", scatter_dimension=0, axis_index_groups=alike, tiled=True)
            for g in grads
        ]
        vectors = lax.psum(vectors, "seq", axis_index_groups=alike)
    down_grad, gate_grad, up_grad, output_grad, outgate_grad, query_grad, key_grad, value_grad, forget_grad = grads
    pregain, bias_total, headgain, postgain = vectors[0], vectors[1, : bias.shape[1]], vectors[2, :head], vectors[3]
    shape = tokens.shape
    return (
        block_output.reshape(shape), input_grad.reshape(shape), pregain, query_grad, key_grad, value_grad,
        forget_grad, bias_total, outgate_grad, output_grad, headgain, postgain, gate_grad, up_grad, down_grad,
    )


def solution(mesh):
    rows, whole, both = P("fsdp", None), P(), P(("seq", "fsdp"), None)
    return jax.shard_map(
        functools.partial(body, mesh.shape["seq"]),
        mesh=mesh,
        in_specs=(
            P("fsdp", "seq", None), P("fsdp", "seq"), whole, rows, rows, rows, rows, whole, rows, rows,
            whole, whole, rows, rows, rows, P("fsdp", "seq", None),
        ),
        out_specs=(
            P("fsdp", "seq", None), P("fsdp", "seq", None), whole, both, both, both, both, whole, both,
            both, whole, whole, both, both, both,
        ),
        check_vma=False,
    )
```

```python
import functools

import jax
import jax.numpy as jnp
from jax import lax
from jax.experimental import pallas as pl
from jax.experimental.pallas import tpu as pltpu
from jax.sharding import PartitionSpec as P

BLOCK = 64
TILE = 256
norm_eps = 1e-06
f32, bf16 = jnp.float32, jnp.bfloat16
MESH = pl.DeviceIdType.MESH
VMEM = pltpu.VMEM
ANY = pl.ANY
LIMIT = 60 * 2**20


def in_vmem():
    return pl.BlockSpec(memory_space=VMEM)


def in_place():
    return pl.BlockSpec(memory_space=ANY)


def greet(partners):
    barrier = pltpu.get_barrier_semaphore()
    for partner in partners:
        pl.semaphore_signal(barrier, inc=1, device_id=partner, device_id_type=MESH)
    pl.semaphore_wait(barrier, len(partners))


def remote(src, dst, sems, index, partner):
    return pltpu.make_async_remote_copy(
        src_ref=src,
        dst_ref=dst,
        send_sem=sems[0].at[index],
        recv_sem=sems[1].at[index],
        device_id=partner,
        device_id_type=MESH,
    )


def parts_of(a, count):
    if a.dtype == bf16:
        return [a]
    out = []
    for i in range(count):
        part = a.astype(bf16)
        out.append(part)
        if i + 1 < count:
            a = a - part.astype(f32)
    return out


def dot(a, b, ca=1, cb=0, count=1):
    total = None
    for right in reversed(parts_of(b, count)):
        term = lax.dot_general(
            a.astype(bf16), right, (((ca,), (cb,)), ((), ())), preferred_element_type=f32
        )
        total = term if total is None else total + term
    return total


def to_col(row):
    n = row.shape[1]
    i = lax.broadcasted_iota(jnp.int32, (n, n), 0)
    j = lax.broadcasted_iota(jnp.int32, (n, n), 1)
    return jnp.sum(jnp.where(i == j, jnp.broadcast_to(row, (n, n)), 0.0), axis=1, keepdims=True)


def mask_set(flags):
    row = jnp.concatenate([flags[i : i + 1].astype(f32) for i in range(flags.shape[0])], axis=1)
    n = row.shape[1]
    flags_row = jnp.broadcast_to(row, (8, n))
    i = lax.broadcasted_iota(jnp.int32, (n, n), 0)
    j = lax.broadcasted_iota(jnp.int32, (n, n), 1)
    same = (i // BLOCK) == (j // BLOCK)
    lower = jnp.where(same & (i >= j), 1.0, 0.0)
    block = jnp.where(same, 1.0, 0.0)
    seen_col = dot(lower, flags_row, 1, 1)[:, :1]
    all_col = dot(block, flags_row, 1, 1)[:, :1]
    seen_row = dot(flags_row, lower, 1, 1)[:1, :]
    linked = jnp.where(seen_col == seen_row, lower, 0.0)
    fresh = jnp.where(seen_col == 0.0, 1.0, 0.0)
    ending = jnp.where(seen_col == all_col, 1.0, 0.0)
    unbroken = jnp.where(all_col == 0.0, 1.0, 0.0)
    return lower, linked, fresh, ending, unbroken


def gate_set(pre, bias, lower, ending):
    z = pre + bias
    u = jnp.exp(-jnp.abs(z))
    lp = jnp.where(
        u < 0.02, u * (1.0 - u * (0.5 - u * (1.0 / 3.0 - 0.25 * u))), jnp.log(1.0 + u)
    )
    g = (jnp.minimum(z, 0.0) - lp) * 0.125
    series = 1.0 + g * (1.0 / 7.0)
    for order in (6, 5, 4, 3, 2):
        series = 1.0 + g * (1.0 / order) * series
    oma = jnp.where(g > -0.35, -g * series, 1.0 - jnp.exp(g))
    a = dot(lower, g, count=3)
    n, lanes = a.shape
    last = jnp.concatenate(
        [
            jnp.broadcast_to(a[b * BLOCK + BLOCK - 1 : b * BLOCK + BLOCK], (BLOCK, lanes))
            for b in range(n // BLOCK)
        ],
        axis=0,
    )
    tail = jnp.exp(last - a) * ending
    return z, u, oma, jnp.exp(a), jnp.exp(-a), tail


def rows_of(b):
    return slice(b * BLOCK, (b + 1) * BLOCK)


def passing(growth, unbroken, b, hs):
    last = b * BLOCK + BLOCK - 1
    return to_col(growth[last : last + 1, hs] * unbroken[last : last + 1])


def sigmoid(v):
    return 1.0 / (1.0 + jnp.exp(-v))


WEIGHTS = ("key", "value", "forget", "query", "outgate", "output", "gate", "up", "down")
TWICE = ("gate", "up", "down")


def front_kernel(size, heads, grouped, *refs):
    count = len(WEIGHTS)
    shards, refs = dict(zip(WEIGHTS, refs[:count])), refs[count:]
    (tok_ref, cot_ref, pre_gain, post_gain, head_gain, bias_ref, flag_ref), refs = refs[:7], refs[7:]
    (
        out_ref, first_ref, attn_ref, mdelta_ref, postgain_grad,
        normed_t, merged_t, second_t, hidden_t, gate_delta, up_delta,
        q_ref, k_ref, v_ref, pre_ref, logit_ref,
        mixed_ref, aff_ref, mixing_ref, weight_ref, inner_ref, state_ref, pass_ref, pass_all,
    ), refs = refs[:24], refs[24:]
    passed, refs = dict(zip(WEIGHTS[:5], refs[:5])), refs[5:]
    whole, refs = dict(zip(WEIGHTS, refs[:count])), refs[count:]
    (
        normed, merged, one_ref, second, block_acc, delta_acc, flat_t,
        ends, going, gathered, prefix, came,
        local, send_sem, recv_sem, away, st_send, st_recv,
    ) = refs
    sems = (send_sem, recv_sem)
    s, f = lax.axis_index("seq"), lax.axis_index("fsdp")
    q = lax.rem(s, 4)
    kind_bit = lax.rem(q + q // 2, 2)
    sib, far, nx, nz = (s, f ^ 1), (s, f ^ 2), (s ^ 1, f), (s ^ 2, f)
    fy, fs = f ^ 2, f ^ 3
    others = [(lax.rem(s + d, size), f) for d in range(1, size)]
    greet([sib, far] + others)
    started = []

    def go(copy):
        copy.start()
        started.append(copy)

    def piece(m, owner, start, length):
        rows = shards[m].shape[0]
        return whole[m].at[pl.ds(pl.multiple_of(owner * rows + start, 16), length)]

    def quarter(m, owner, which, half=None):
        rows = shards[m].shape[0] // 4
        first = (rows // 2 + 15) // 16 * 16
        start, length = (0, rows) if half is None else ((0, first), (first, rows - first))[half]
        return piece(m, owner, which * rows + start, length)

    def eighth(m, owner, bit, half):
        rows = shards[m].shape[0] // 2
        return piece(m, owner, bit * rows + half * (rows // 2), rows // 2)

    def mine(m, owner):
        if m in TWICE:
            rows = shards[m].shape[0] // 2
            return piece(m, owner, kind_bit * rows, rows)
        return quarter(m, owner, q)

    def from_x(m, owner):
        return eighth(m, owner, 1 - kind_bit, 0) if m in TWICE else quarter(m, owner, q ^ 1)

    def from_z(m, owner):
        return eighth(m, owner, 1 - kind_bit, 1) if m in TWICE else quarter(m, owner, q ^ 2)

    def send(kind, m, part, partner):
        go(remote(part, part, sems, (kind, WEIGHTS.index(m)), partner))

    def arrived(kind, m, part):
        remote(part, part, sems, (kind, WEIGHTS.index(m)), sib).wait_recv()

    own = {}
    for i, m in enumerate(WEIGHTS):
        rows = shards[m].shape[0]
        if m in TWICE:
            src = shards[m].at[pl.ds(pl.multiple_of(kind_bit * (rows // 2), 16), rows // 2)]
        else:
            src = shards[m].at[pl.ds(pl.multiple_of(q * (rows // 4), 16), rows // 4)]
        go(remote(src, mine(m, f), sems, (1, i), far))
    for i, m in enumerate(WEIGHTS):
        rows = shards[m].shape[0]
        go(remote(shards[m], piece(m, f, 0, rows), sems, (0, i), sib))
        own[m] = pltpu.make_async_copy(shards[m], piece(m, f, 0, rows), local.at[i])
        own[m].start()

    def pump(step):
        if step < count:
            m = WEIGHTS[step]
            part = mine(m, fy)
            arrived(1, m, part)
            if m in TWICE:
                send(2, m, eighth(m, fy, kind_bit, 0), nx)
                send(3, m, eighth(m, fy, kind_bit, 1), nz)
            else:
                send(2, m, part, nx)
                send(3, m, part, nz)
            send(6, m, part, sib)
        if 0 <= step - 1 < count:
            m = WEIGHTS[step - 1]
            arrived(2, m, from_x(m, fy))
            if m not in TWICE:
                send(4, m, quarter(m, fy, q ^ 1, 0), nz)
            send(7, m, from_x(m, fy), sib)
            arrived(3, m, from_z(m, fy))
            if m not in TWICE:
                send(5, m, quarter(m, fy, q ^ 2, 1), nx)
            send(8, m, from_z(m, fy), sib)
        if 0 <= step - 2 < count:
            m = WEIGHTS[step - 2]
            if m not in TWICE:
                for kind in (4, 5):
                    part = quarter(m, fy, q ^ 3, kind - 4)
                    arrived(kind, m, part)
                    send(kind + 5, m, part, sib)

    def ready(m):
        own[m].wait()
        arrived(0, m, piece(m, f ^ 1, 0, shards[m].shape[0]))
        arrived(6, m, mine(m, fs))
        arrived(7, m, from_x(m, fs))
        arrived(8, m, from_z(m, fs))
        if m not in TWICE:
            arrived(9, m, quarter(m, fs, q ^ 3, 0))
            arrived(10, m, quarter(m, fs, q ^ 3, 1))

    n, width = tok_ref.shape
    head = width // heads
    slots = bias_ref.shape[1] // heads
    blocks = n // BLOCK
    streams = 2
    per = blocks // streams
    pairs = heads * streams
    scale = head ** (-0.5)

    def across(columns, step):
        def turn(i, carry):
            step(pl.ds(pl.multiple_of(i * TILE, TILE), TILE))
            return carry

        lax.fori_loop(0, columns // TILE, turn, 0)

    def project(m, to_ref):
        def step(at):
            to_ref[:, at] = dot(normed[...], whole[m][:, at]).astype(to_ref.dtype)

        across(whole[m].shape[1], step)

    def turn_over(source, to_ref, rows, padded):
        if not grouped:
            to_ref[...] = source[...].astype(bf16)
            return
        for group in range(16):
            for core in range(2):
                at = (group * 2 + core) * rows
                to_ref[core, group * padded : group * padded + rows] = source[at : at + rows].astype(bf16)

    inputs = tok_ref[...].astype(f32)
    unit = inputs * lax.rsqrt(jnp.mean(inputs * inputs, axis=1, keepdims=True) + norm_eps)
    scaled = unit * pre_gain[...]
    normed[...] = scaled.astype(bf16)
    turn_over(scaled.T, normed_t, width // 32, width // 32)
    for step in range(5):
        pump(step)
    for m, to_ref in (("key", k_ref), ("value", v_ref), ("forget", pre_ref)):
        ready(m)
        project(m, to_ref)
    lower, linked, fresh, ending, unbroken = mask_set(flag_ref[...])
    z, u, oma, growth, inverse, tail = gate_set(pre_ref[...], bias_ref[...], lower, ending)
    shrink, kept = inverse * oma, tail * oma
    for h in range(heads):
        hs, hd = slice(h * slots, (h + 1) * slots), slice(h * head, (h + 1) * head)
        for stream in range(streams):
            pair = h * streams + stream
            total, through = None, None
            for b in range(stream * per, (stream + 1) * per):
                part = kept[rows_of(b), hs].astype(bf16)
                at = pair * per + b % per
                end_k = dot(part, k_ref[rows_of(b), hd], 0, 0)
                end_v = dot(part, v_ref[rows_of(b), hd], 0, 0)
                ends[at, :, :head] = end_k
                ends[at, :, head:] = end_v
                factor = passing(growth, unbroken, b, hs)
                pass_ref[at] = jnp.broadcast_to(factor, pass_ref.shape[1:])
                if total is None:
                    total, through = (end_k, end_v), factor
                else:
                    total = (factor * total[0] + end_k, factor * total[1] + end_v)
                    through = through * factor
            at = slice(pair * slots, (pair + 1) * slots)
            going[at, :head] = total[0].astype(bf16)
            going[at, head : 2 * head] = total[1].astype(bf16)
            going[at, 2 * head :] = jnp.broadcast_to(through, (slots, going.shape[1] - 2 * head)).astype(bf16)

    share = pairs * slots // size

    def rows_for(place):
        return pl.ds(pl.multiple_of(place * share, 16), share)

    first_hop, second_hop = [], []
    for d in range(1, size):
        to = others[d - 1]
        copy = remote(going.at[rows_for(to[0])], gathered.at[s], (st_send, st_recv), (0, d - 1), to)
        go(copy)
        first_hop.append(lax.rem(s + size - d, size))
    gathered[s] = going[rows_for(s)]
    pump(5)
    pump(6)
    for m, to_ref in (("query", q_ref), ("outgate", logit_ref)):
        ready(m)
        project(m, to_ref)
    for i, m in enumerate(WEIGHTS[:5]):
        copy = pltpu.make_async_copy(whole[m], passed[m], away.at[i])
        copy.start()
        own[m] = copy
    for d in range(1, size):
        source = first_hop[d - 1]
        remote(gathered.at[source], gathered.at[source], (st_send, st_recv), (0, d - 1), sib).wait_recv()
    state = jnp.zeros((share, 2 * head), f32)
    for place in range(size):
        prefix[place] = state.astype(bf16)
        entry = gathered[place].astype(f32)
        pass_all[place] = gathered[place][:, 2 * head :]
        state = entry[:, 2 * head : 2 * head + 1] * state + entry[:, : 2 * head]
    for d in range(1, size):
        to = others[d - 1]
        go(remote(prefix.at[to[0]], came.at[rows_for(s)], (st_send, st_recv), (1, d - 1), to))
    came[rows_for(s)] = prefix[s]
    pump(7)
    for h in range(heads):
        hd = slice(h * head, (h + 1) * head)
        aff_ref[h] = (dot(q_ref[:, hd], k_ref[:, hd], 1, 1) * (linked * scale)).astype(bf16)
    for d in range(1, size):
        part = came.at[rows_for(first_hop[d - 1])]
        remote(part, part, (st_send, st_recv), (1, d - 1), sib).wait_recv()
    pump(8)
    for h in range(heads):
        hs, hd = slice(h * slots, (h + 1) * slots), slice(h * head, (h + 1) * head)
        for stream in range(streams):
            pair = h * streams + stream
            state = came[pair * slots : (pair + 1) * slots].astype(f32)
            for b in range(per):
                at = pair * per + b
                state_ref[pair, b] = state.astype(bf16)
                state = pass_ref[at][:, :1] * state + ends[at]
            state_ref[pair, per] = state.astype(bf16)
        gr, sh = growth[:, hs], shrink[:, hs]
        qh, vh = q_ref[:, hd], v_ref[:, hd]
        carried = jnp.concatenate(
            [
                dot(qh[rows_of(b)], state_ref[h * streams + b // per, b % per, :, :head], 1, 1)
                for b in range(blocks)
            ],
            axis=0,
        )
        inner = dot(aff_ref[h], sh) + carried * (scale * fresh)
        scores = gr * inner
        e = jnp.exp(scores - jnp.max(scores, axis=1, keepdims=True))
        weights = e / jnp.sum(e, axis=1, keepdims=True)
        weight_ref[:, hs] = weights
        inner_ref[:, hs] = inner
        lifted = weights * gr
        mixing = (dot(lifted, sh.astype(bf16), 1, 1) * linked).astype(bf16)
        mixing_ref[h] = mixing
        brought = jnp.concatenate(
            [
                dot(lifted[rows_of(b)], state_ref[h * streams + b // per, b % per, :, head:])
                for b in range(blocks)
            ],
            axis=0,
        )
        mixed = dot(mixing, vh) + brought * fresh
        mixed_ref[:, hd] = mixed
        r = lax.rsqrt(jnp.mean(mixed * mixed, axis=1, keepdims=True) + norm_eps)
        logits = logit_ref[:, hd]
        delta_acc[:, hd] = mixed * r * head_gain[...] * (logits * sigmoid(logits))
        merged[:, hd] = delta_acc[:, hd].astype(bf16)
    ready("output")

    def join(at):
        one_ref[:, at] = tok_ref[:, at].astype(f32) + dot(merged[...], whole["output"][:, at])

    across(width, join)
    turn_over(delta_acc[...].T, merged_t, width // 32, width // 32)
    one = one_ref[...]
    scaled = one * lax.rsqrt(jnp.mean(one * one, axis=1, keepdims=True) + norm_eps) * post_gain[...]
    second[...] = scaled.astype(bf16)
    turn_over(scaled.T, second_t, width // 32, width // 32)
    pump(9)
    pump(10)
    ready("gate")
    ready("up")
    ready("down")
    block_acc[...] = one
    delta_acc[...] = jnp.zeros_like(delta_acc)

    def unit_tile(i, carry):
        at = pl.ds(pl.multiple_of(i * TILE, TILE), TILE)
        w_gate, w_up, w_down = whole["gate"][:, at], whole["up"][:, at], whole["down"][at]
        gate_vals, up_vals = dot(second[...], w_gate), dot(second[...], w_up)
        sig = sigmoid(gate_vals)
        silu = gate_vals * sig
        full = silu * up_vals
        flat_t[at] = full.T
        hidden_delta = dot(cot_ref[...], w_down, 1, 1)
        d_up = (hidden_delta * silu).astype(bf16)
        d_gate = (hidden_delta * up_vals * (sig + silu * (1.0 - sig))).astype(bf16)
        gate_delta[:, at] = d_gate
        up_delta[:, at] = d_up
        block_acc[...] += dot(full, w_down)
        delta_acc[...] += dot(d_gate, w_gate, 1, 1) + dot(d_up, w_up, 1, 1)
        return carry

    ff = whole["down"].shape[0]
    lax.fori_loop(0, ff // TILE, unit_tile, 0)
    out_ref[...] = block_acc[...].astype(bf16)
    turn_over(flat_t, hidden_t, ff // 32, -(-(ff // 32) // 16) * 16)
    one = one_ref[...]
    r = lax.rsqrt(jnp.mean(one * one, axis=1, keepdims=True) + norm_eps)
    unit = one * r
    delta = delta_acc[...]
    postgain_grad[...] = jnp.sum(delta * unit, axis=0, keepdims=True)
    delta = delta * post_gain[...]
    first = cot_ref[...].astype(f32) + r * (delta - unit * jnp.mean(unit * delta, axis=1, keepdims=True))
    first_ref[...] = first
    attn_ref[...] = first.astype(bf16)

    def split(at):
        mdelta_ref[:, at] = dot(attn_ref[...], whole["output"][at], 1, 1)

    across(width, split)
    for m in WEIGHTS[:5]:
        own[m].wait()
    for copy in started:
        copy.wait_send()


def front(size, heads, grouped, shards, tokens, cotan, pre_gain, post_gain, head_gain, bias, flags):
    n, width = tokens.shape
    head, slots = width // heads, bias.shape[1] // heads
    pairs, per = heads * 2, n // BLOCK // 2
    ff = shards["gate"].shape[1]
    shards = [shards[m] for m in WEIGHTS]
    count = len(shards)
    padded = -(-(ff // 32) // 16) * 512

    def turned(rows, grouped_rows):
        shape = (2, grouped_rows // 2, n) if grouped else (rows, n)
        return jax.ShapeDtypeStruct(shape, bf16)

    def low(*shape):
        return jax.ShapeDtypeStruct(shape, bf16)

    def full(*shape):
        return jax.ShapeDtypeStruct(shape, f32)

    outs = [
        low(n, width), full(n, width), low(n, width), full(n, width), full(1, width),
        turned(width, width), turned(width, width), turned(width, width), turned(ff, padded),
        low(n, ff), low(n, ff),
        low(n, width), low(n, width), low(n, width), full(n, heads * slots), full(n, width),
        full(n, width), low(heads, n, n), low(heads, n, n), full(n, heads * slots), full(n, heads * slots),
        low(pairs, per + 1, slots, 2 * head), full(pairs * per, slots, 128),
        low(size, pairs * slots // size, 128),
    ]
    wholes = [low(4 * w.shape[0], w.shape[1]) for w in shards]
    share = pairs * slots // size
    dma = pltpu.SemaphoreType.DMA
    got = pl.pallas_call(
        functools.partial(front_kernel, size, heads, grouped),
        name="front",
        out_shape=outs + wholes[:5],
        in_specs=[in_place()] * count + [in_vmem()] * 7,
        out_specs=[in_vmem()] * len(outs) + [in_place()] * 5,
        scratch_shapes=[VMEM(w.shape, bf16) for w in wholes]
        + [
            VMEM((n, width), bf16),
            VMEM((n, width), bf16),
            VMEM((n, width), f32),
            VMEM((n, width), bf16),
            VMEM((n, width), f32),
            VMEM((n, width), f32),
            VMEM((ff, n), f32),
            VMEM((pairs * per, slots, 2 * head), f32),
            VMEM((pairs * slots, 2 * head + 128), bf16),
            VMEM((size, share, 2 * head + 128), bf16),
            VMEM((size, share, 2 * head), bf16),
            VMEM((pairs * slots, 2 * head), bf16),
            dma((count,)),
            dma((11, count)),
            dma((11, count)),
            dma((5,)),
            dma((2, size - 1)),
            dma((2, size - 1)),
        ],
        compiler_params=pltpu.CompilerParams(
            collective_id=1, has_side_effects=True, vmem_limit_bytes=LIMIT
        ),
    )(*shards, tokens, cotan, pre_gain, post_gain, head_gain, bias, flags)
    return got


def to_row(col):
    n = col.shape[0]
    i = lax.broadcasted_iota(jnp.int32, (n, n), 0)
    j = lax.broadcasted_iota(jnp.int32, (n, n), 1)
    return jnp.sum(jnp.where(i == j, jnp.broadcast_to(col, (n, n)), 0.0), axis=0, keepdims=True)


LEAST, SHALLOW, DEEP = 4.0, 8.0, 10.0
STRIPS = 3
BACK_LIMIT = 63 * 2**20


ROUTES = (("y", "z", "x", "zz"), ("x", "z", "y", "zz"), ("y", "x", "z", "zz"), ("x", "y", "z", "zz"))
STATES = {"x": 1.15, "y": 0.0, "z": 1.75}


def cut(sizes):
    load, plan, last = dict(STATES), [], 1
    for columns, rows in sizes:
        tiles = columns // TILE
        pieces = min(4, 2 * tiles) if tiles <= 4 else 6
        width = columns // pieces if tiles <= 1 else TILE
        out, start = [], 0
        for i in range(pieces):
            count = 1 if tiles <= 1 else tiles // pieces + (1 if i < tiles % pieces else 0)
            size = 2 * 16 * rows * width * count * 2 / 1e6

            def after(route):
                new = dict(load)
                for stage, link in enumerate(ROUTES[route]):
                    new["z" if link == "zz" else link] += size / 2 ** (stage + 1)
                return new

            route = min((1 - last, 3 - last), key=lambda r: sum(v**4 for v in after(r).values()))
            load, last = after(route), route % 2
            out.append((start, width * count, route))
            start += width * count
        plan.append(tuple(out))
    return plan


def in_order(chunks, path, held_back, least, shallow, deep):
    now, free = 0.0, dict.fromkeys(("x", "y", "z", "zz"), 0.0)
    came, done, coming, out = {}, set(), [], []
    path, left = list(path), list(range(len(chunks)))
    rate, delay = 0.045, 2.0

    def leave(c, stage):
        rows, width, order = chunks[c][1], chunks[c][3], chunks[c][4]
        link = ROUTES[order][stage]
        size = 16 * rows * width * 2 / 1e6 / 2 ** (stage + 1)
        free[link] = max(now, free[link]) + size / rate * (2 if stage == 3 else 1)
        coming.append((free[link] + delay, c, stage))

    while left or path or coming:
        here = sorted(a for a in coming if a[0] <= now)
        open_ = [c for c in left if held_back.get(chunks[c][0], None) in done or chunks[c][0] not in held_back]
        depth = deep if "second hop" in done else shallow
        queue = free[ROUTES[chunks[open_[0]][4]][0]] - now if open_ else 0.0
        ready = path and came.get(path[0][2], 0.0 if path[0][2] is None else 1e9) <= now
        if here:
            _, c, stage = here[0]
            coming.remove(here[0])
            now += 0.1 + 0.1 * chunks[c][1] / 32 * chunks[c][3] / TILE / 2**stage
            out.append(("advance", c, stage))
            if stage < 3:
                leave(c, stage + 1)
        elif ready and not (open_ and queue < least):
            name, time, _, starts, takes = path.pop(0)
            now += time
            done.add(name)
            out.append(("path", name, None))
            if starts:
                came[starts] = now + takes
        elif open_ and queue < depth:
            c = open_[0]
            left.remove(c)
            now += 0.1 + 0.3 * chunks[c][1] / 32 * chunks[c][3] / TILE
            out.append(("produce", c, None))
            leave(c, 0)
        else:
            later = [a[0] for a in coming]
            if path and path[0][2] in came:
                later.append(came[path[0][2]])
            if open_:
                later.append(now + queue - depth)
            now = max(now + 0.05, min(later))
    return out


FORM = (("cotan", 0), ("gate", 1), ("up", 1), ("attn", 2), ("outgate", 3), ("query", 3), ("key", 3), ("value", 3), ("forget", 3))
SAVED = ("q", "k", "v", "pre", "logits", "mixed", "aff", "mixing", "weights", "inner", "state", "pass", "mdelta", "pass_all")


def back_kernel(size, heads, plan, *refs):
    def take(count):
        nonlocal refs
        got, refs = refs[:count], refs[count:]
        return got

    lefts, rights, saved = take(4), take(4), dict(zip(SAVED, take(len(SAVED))))
    weights, (first_in, tokens_in) = take(5), take(2)
    bias_ref, flag_ref, head_gain, pre_gain, postgain_ref = take(5)
    outs, (vec_out, input_grad) = take(9), take(2)
    left_all, right_all = take(4), take(9)
    have_ref = dict(zip(SAVED, take(len(SAVED))))
    chunks = [(g, p[2]) + c for g, p in enumerate(plan) for c in p[4]]
    nc = len(chunks)
    sums = take(nc)
    landed = [take(nc) for _ in range(4)]
    owed, da_acc, doma_acc, strip, going, gathered, prefix, came, vec_acc, vec_got = take(10)
    loads, in_local, in_send, in_recv, strip_sem, first_sem = take(6)
    hop_send, hop_recv, st_send, st_recv, v_send, v_recv = take(6)
    q_ref, k_ref, v_ref = have_ref["q"], have_ref["k"], have_ref["v"]
    logit_ref, mixed_ref, mdelta_ref = have_ref["logits"], have_ref["mixed"], have_ref["mdelta"]
    state_ref, pass_ref = have_ref["state"], have_ref["pass"]

    s, f = lax.axis_index("seq"), lax.axis_index("fsdp")
    core, y = lax.rem(f, 2), f // 2
    x, z_low, z_high = lax.rem(s, 2), lax.rem(s // 2, 2), lax.rem(s // 4, 2)
    sib, far, nx, nz, nzz = (s, f ^ 1), (s, f ^ 2), (s ^ 1, f), (s ^ 2, f), (s ^ 4, f)
    others = [(lax.rem(s + d, size), f) for d in range(1, size)]
    greet([sib, far] + others)
    started = []

    def go(copy):
        copy.start()
        started.append(copy)

    n, width = q_ref.shape
    head = width // heads
    slots = bias_ref.shape[1] // heads
    blocks = n // BLOCK
    streams = 2
    per = blocks // streams
    pairs = heads * streams
    scale = head ** (-0.5)
    share = pairs * slots // size

    waiting = {}

    def fetch_left(i):
        keep = pltpu.make_async_copy(lefts[i].at[core], left_all[i].at[:, pl.ds(0, n)], in_local.at[i])
        keep.start()
        copy = remote(lefts[i].at[1 - core], left_all[i].at[:, pl.ds(n, n)], (in_send, in_recv), i, sib)
        go(copy)
        waiting["left", i] = [keep, copy]

    def fetch_right(i):
        own, other = right_all[i].at[pl.ds(0, n)], right_all[i].at[pl.ds(n, n)]
        keep = None
        src = own
        if i < 4:
            src = rights[i]
            keep = pltpu.make_async_copy(src, own, in_local.at[4 + i])
            keep.start()
        copy = remote(src, other, (in_send, in_recv), 4 + i, sib)
        go(copy)
        waiting["right", i] = [keep, copy]

    def have(kind, i):
        pair = waiting[kind, i]
        if pair:
            if pair[0] is not None:
                pair[0].wait()
            pair[1].wait_recv()
            waiting[kind, i] = None

    fetch_left(0)
    fetch_right(0)
    loading = []
    for i, name in enumerate(SAVED):
        copy = pltpu.make_async_copy(saved[name], have_ref[name], loads.at[i])
        copy.start()
        loading.append(copy)
    for i in (1, 2, 3):
        fetch_right(i)
    for i in (1, 2, 3):
        fetch_left(i)

    strips = [(w, t * TILE) for w in range(5) for t in range(weights[w].shape[1] // TILE)]

    def strip_copy(i):
        w, at = strips[i]
        return pltpu.make_async_copy(weights[w].at[:, pl.ds(at, TILE)], strip.at[i % STRIPS], strip_sem.at[i % STRIPS])

    for i in range(STRIPS):
        strip_copy(i).start()

    def route(c):
        names = ROUTES[chunks[c][4]]
        places, partners = dict(x=x, y=y, z=z_low, zz=z_high), dict(x=nx, y=far, z=nz, zz=nzz)
        return tuple(places[i] for i in names), tuple(partners[i] for i in names)

    def stage_copy(c, stage):
        bits, partners = route(c)
        at = bits[:stage] + (1 - bits[stage],)
        return remote(sums[c].at[at], landed[stage][c], (st_send, st_recv), (stage, c), partners[stage])

    def produce(c):
        g, rows, start, wide, order = chunks[c]
        left = plan[g][0]
        have("left", left)
        have("right", g)
        tile = min(TILE, wide)

        def turn(i, carry):
            at = pl.multiple_of(start + i * tile, 128)
            to = pl.multiple_of(i * tile, 128)
            got = jnp.dot(
                left_all[left][...], right_all[g][:, pl.ds(at, tile)], preferred_element_type=f32
            ).astype(bf16)
            for group in range(16):
                bits = dict(zz=group >> 3 & 1, z=group >> 2 & 1, x=group >> 1 & 1, y=group & 1)
                place = tuple(bits[i] for i in ROUTES[order])
                sums[c][*place, :, pl.ds(to, tile)] = got[group * rows : (group + 1) * rows]
            return carry

        lax.fori_loop(0, wide // tile, turn, 0)
        go(stage_copy(c, 0))

    def advance(c, stage):
        stage_copy(c, stage).wait_recv()
        bits, _ = route(c)
        if stage == 3:
            g, rows, start, wide, _ = chunks[c]
            total = sums[c][bits].astype(f32) + landed[3][c][...].astype(f32)
            outs[g][:, start : start + wide] = total[: plan[g][3]]
            return
        for rest in range(1 << (3 - stage)):
            tail = tuple((rest >> k) & 1 for k in reversed(range(3 - stage)))
            at = bits[: stage + 1] + tail
            sums[c][at] = (sums[c][at].astype(f32) + landed[stage][c][tail].astype(f32)).astype(bf16)
        go(stage_copy(c, stage + 1))

    keep = {}

    def begin():
        for copy in loading:
            copy.wait()
        lower, linked, fresh, ending, unbroken = mask_set(flag_ref[...])
        z, u, oma, growth, inverse, tail = gate_set(have_ref["pre"][...], bias_ref[...], lower, ending)
        keep.update(lower=lower, linked=linked, fresh=fresh, z=z, u=u, oma=oma, growth=growth)
        keep.update(inverse=inverse, tail=tail, shrink=inverse * oma, kept=tail * oma)
        keep["gain"] = jnp.zeros((1, head), f32)

    def states(h, b):
        return state_ref.at[h * streams + b // per, b % per]

    def one_head(h):
        linked, fresh, growth, shrink = keep["linked"], keep["fresh"], keep["growth"], keep["shrink"]
        hs, hd = slice(h * slots, (h + 1) * slots), slice(h * head, (h + 1) * head)
        mixed, logits, delta = mixed_ref[:, hd], logit_ref[:, hd], mdelta_ref[:, hd]
        r = lax.rsqrt(jnp.mean(mixed * mixed, axis=1, keepdims=True) + norm_eps)
        sig = sigmoid(logits)
        silu = logits * sig
        unit = mixed * r
        dy = delta * silu
        right_all[4][0:n, hd] = (delta * unit * head_gain[...] * (sig + silu * (1.0 - sig))).astype(bf16)
        keep["gain"] = keep["gain"] + jnp.sum(dy * unit, axis=0, keepdims=True)
        dy = dy * head_gain[...]
        dmixed = r * (dy - unit * jnp.mean(unit * dy, axis=1, keepdims=True))
        gr, sh = growth[:, hs], shrink[:, hs].astype(bf16)
        weigh, inner = have_ref["weights"][:, hs], have_ref["inner"][:, hs]
        aff, mixing = have_ref["aff"][h], have_ref["mixing"][h]
        qh, kh, vh = q_ref[:, hd], k_ref[:, hd], v_ref[:, hd]
        do = dmixed.astype(bf16)
        lifted = (weigh * gr).astype(bf16)
        dm = (dot(do, vh, 1, 1) * linked).astype(bf16)
        mixed_ref[:, hd] = dot(mixing, do, 0, 0)
        fdo = (dmixed * fresh).astype(bf16)
        dlift = dot(dm, sh) + jnp.concatenate(
            [dot(fdo[rows_of(b)], states(h, b)[:, head:], 1, 1) for b in range(blocks)], axis=0
        )
        dsh = dot(dm, lifted, 0, 0)
        dw = dlift * gr
        dsc = weigh * (dw - jnp.sum(weigh * dw, axis=1, keepdims=True))
        du = dsc * gr
        du_low = du.astype(bf16)
        da = (dot(du_low, sh, 1, 1) * (linked * scale)).astype(bf16)
        dsh = dsh + dot(aff, du_low, 0, 0)
        fdu = (du * (fresh * scale)).astype(bf16)
        right_all[5][0:n, hd] = (
            dot(da, kh)
            + jnp.concatenate([dot(fdu[rows_of(b)], states(h, b)[:, :head]) for b in range(blocks)], axis=0)
        ).astype(bf16)
        mdelta_ref[:, hd] = dot(da, qh, 0, 0)
        for stream in range(streams):
            pair = h * streams + stream
            total = None
            for b in reversed(range(stream * per, (stream + 1) * per)):
                at = pair * per + b % per
                own_k = dot(fdu[rows_of(b)], qh[rows_of(b)], 0, 0)
                own_v = dot(lifted[rows_of(b)], fdo[rows_of(b)], 0, 0)
                owed[at, :, :head] = own_k.astype(bf16)
                owed[at, :, head:] = own_v.astype(bf16)
                if total is not None:
                    factor = pass_ref[at][:, :1]
                    own_k, own_v = own_k + factor * total[0], own_v + factor * total[1]
                total = (own_k, own_v)
            at = slice(pair * slots, (pair + 1) * slots)
            going[at, :head] = total[0].astype(bf16)
            going[at, head:] = total[1].astype(bf16)
        da_acc[:, hs] = lifted.astype(f32) * dlift + du_low.astype(f32) * inner - dsh * sh.astype(f32)
        doma_acc[:, hs] = dsh * keep["inverse"][:, hs]

    def rows_for(place):
        return pl.ds(pl.multiple_of(place * share, 16), share)

    sources = [lax.rem(s + size - d, size) for d in range(1, size)]

    def first_hop():
        for d in range(1, size):
            to = others[d - 1]
            go(remote(going.at[rows_for(to[0])], gathered.at[s], (hop_send, hop_recv), (0, d - 1), to))
        gathered[s] = going[rows_for(s)]
        fetch_right(4)
        fetch_right(5)

    def second_hop():
        for d in range(1, size):
            part = gathered.at[sources[d - 1]]
            remote(part, part, (hop_send, hop_recv), (0, d - 1), sib).wait_recv()
        state = jnp.zeros((share, 2 * head), f32)
        for place in reversed(range(size)):
            prefix[place] = state.astype(bf16)
            state = have_ref["pass_all"][place][:, :1].astype(f32) * state + gathered[place].astype(f32)
        for d in range(1, size):
            to = others[d - 1]
            go(remote(prefix.at[to[0]], came.at[rows_for(s)], (hop_send, hop_recv), (1, d - 1), to))
        came[rows_for(s)] = prefix[s]

    def last_hop():
        for d in range(1, size):
            part = came.at[rows_for(sources[d - 1])]
            remote(part, part, (hop_send, hop_recv), (1, d - 1), sib).wait_recv()

    def end_head(h):
        kept, tail = keep["kept"], keep["tail"]
        row = lax.broadcasted_iota(jnp.int32, (BLOCK, 1), 0)
        hs, hd = slice(h * slots, (h + 1) * slots), slice(h * head, (h + 1) * head)
        for stream in range(streams):
            pair = h * streams + stream
            leaving = came[pair * slots : (pair + 1) * slots].astype(f32)
            for i in reversed(range(per)):
                at, rb = pair * per + i, rows_of(stream * per + i)
                low = leaving.astype(bf16)
                part = kept[rb, hs].astype(bf16)
                dkept = dot(k_ref[rb, hd], low[:, :head], 1, 1) + dot(v_ref[rb, hd], low[:, head:], 1, 1)
                right_all[6][rb, hd] = (mdelta_ref[rb, hd] + dot(part, low[:, :head])).astype(bf16)
                right_all[7][rb, hd] = (mixed_ref[rb, hd] + dot(part, low[:, head:])).astype(bf16)
                held = jnp.sum(low.astype(f32) * state_ref[pair, i + 1].astype(f32), axis=1, keepdims=True)
                da_acc[rb, hs] = (
                    da_acc[rb, hs] - dkept * part.astype(f32) + jnp.where(row == BLOCK - 1, to_row(held), 0.0)
                )
                doma_acc[rb, hs] = doma_acc[rb, hs] + dkept * tail[rb, hs]
                if i > 0:
                    leaving = owed[at].astype(f32) + pass_ref[at][:, :1] * leaving

    def end_gates():
        fetch_right(6)
        fetch_right(7)
        z, u = keep["z"], keep["u"]
        dg = dot(keep["lower"], da_acc[...], 0, 0, count=3) - doma_acc[...] * (1.0 - keep["oma"])
        sig = jnp.where(z >= 0.0, u / (1.0 + u), 1.0 / (1.0 + u))
        dpre = dg * sig * 0.125
        right_all[8][0:n] = dpre.astype(bf16)
        fetch_right(8)
        pltpu.make_async_copy(first_in, mdelta_ref, first_sem.at[0]).start()
        pltpu.make_async_copy(tokens_in, q_ref, first_sem.at[1]).start()
        vec_acc[0] = jnp.zeros(vec_acc.shape[1:], f32)
        vec_acc[0, 1:2, : dpre.shape[1]] = jnp.sum(dpre, axis=0, keepdims=True)
        vec_acc[0, 2:3, :head] = keep["gain"]
        vec_acc[0, 3:4, :] = postgain_ref[...]

    def strip_step(i):
        strip_copy(i).wait()
        w, at = strips[i]
        term = dot(right_all[(6, 7, 8, 5, 4)[w]][0:n, at : at + TILE], strip[i % STRIPS], 1, 1)
        logit_ref[...] = term if i == 0 else logit_ref[...] + term
        if i + STRIPS < len(strips):
            strip_copy(i + STRIPS).start()

    def end_norm():
        pltpu.make_async_copy(first_in, mdelta_ref, first_sem.at[0]).wait()
        pltpu.make_async_copy(tokens_in, q_ref, first_sem.at[1]).wait()
        inputs = q_ref[...].astype(f32)
        r = lax.rsqrt(jnp.mean(inputs * inputs, axis=1, keepdims=True) + norm_eps)
        unit = inputs * r
        delta = logit_ref[...]
        vec_acc[0, 0:1, :] = jnp.sum(delta * unit, axis=0, keepdims=True)
        delta = delta * pre_gain[...]
        input_grad[...] = (
            mdelta_ref[...] + r * (delta - unit * jnp.mean(unit * delta, axis=1, keepdims=True))
        ).astype(bf16)
        go(v_copy(0))

    def v_copy(i):
        return remote(vec_acc.at[i], vec_got.at[i], (v_send, v_recv), i, (sib, far, nx, nz, nzz)[i])

    def vector(i):
        v_copy(i).wait_recv()
        total = vec_acc[i] + vec_got[i]
        if i == 4:
            vec_out[...] = total
            return
        vec_acc[i + 1] = total
        go(v_copy(i + 1))

    steps = {"begin": begin}
    path = [("begin", 2.0, None, None, 0)]
    for h in range(heads):
        steps["head", h] = functools.partial(one_head, h)
        path.append((("head", h), 3.0, None, None, 0))
    steps.update({"first hop": first_hop, "second hop": second_hop, "last hop": last_hop})
    path.append(("first hop", 0.5, None, "first", 12.0))
    path.append(("second hop", 1.0, "first", "second", 12.0))
    path.append(("last hop", 0.1, "second", None, 0))
    for h in range(heads):
        steps["end", h] = functools.partial(end_head, h)
        path.append((("end", h), 1.2, None, None, 0))
    steps["gates"] = end_gates
    path.append(("gates", 1.0, None, None, 0))
    for i in range(len(strips)):
        steps["strip", i] = functools.partial(strip_step, i)
        path.append((("strip", i), 0.4, None, None, 0))
    steps["norm"] = end_norm
    path.append(("norm", 1.5, None, ("vector", 0), 3.0))
    for i in range(5):
        steps["vector", i] = functools.partial(vector, i)
        path.append((("vector", i), 0.1, ("vector", i), ("vector", i + 1), 4.0))
    held_back = {4: "first hop", 5: "first hop", 6: "gates", 7: "gates", 8: "gates"}
    for what, which, stage in in_order(chunks, path, held_back, LEAST, SHALLOW, DEEP):
        if what == "path":
            steps[which]()
        elif what == "produce":
            produce(which)
        else:
            advance(which, stage)
    for copy in started:
        copy.wait_send()


def back(size, heads, plan, lefts, rights, saved, weights, first, tokens, bias, flags, head_gain, pre_gain, postgain):
    n, width = saved["q"].shape
    head, slots = width // heads, bias.shape[1] // heads
    pairs, per = heads * 2, n // BLOCK // 2
    share = pairs * slots // size
    chunks = [(p[2],) + c for p in plan for c in p[4]]
    nc = len(chunks)
    dma = pltpu.SemaphoreType.DMA
    saved = [saved[name] for name in SAVED]
    scratch = [VMEM((a.shape[1], 2 * n), bf16) for a in lefts]
    scratch += [VMEM((2 * n, p[1]), bf16) for p in plan]
    scratch += [VMEM(a.shape, a.dtype) for a in saved]
    for lead in ((2, 2, 2, 2), (2, 2, 2), (2, 2), (2,), ()):
        scratch += [VMEM(lead + (r, w), bf16) for r, _, w, _ in chunks]
    scratch += [
        VMEM((pairs * per, slots, 2 * head), bf16),
        VMEM((n, heads * slots), f32),
        VMEM((n, heads * slots), f32),
        VMEM((STRIPS, width, TILE), bf16),
        VMEM((pairs * slots, 2 * head), bf16),
        VMEM((size, share, 2 * head), bf16),
        VMEM((size, share, 2 * head), bf16),
        VMEM((pairs * slots, 2 * head), bf16),
        VMEM((5, 8, width), f32),
        VMEM((5, 8, width), f32),
        dma((len(SAVED),)),
        dma((8,)),
        dma((13,)),
        dma((13,)),
        dma((STRIPS,)),
        dma((2,)),
        dma((2, size - 1)),
        dma((2, size - 1)),
        dma((4, nc)),
        dma((4, nc)),
        dma((5,)),
        dma((5,)),
    ]
    out = pl.pallas_call(
        functools.partial(back_kernel, size, heads, plan),
        name="back",
        out_shape=[jax.ShapeDtypeStruct((p[3], p[1]), f32) for p in plan]
        + [jax.ShapeDtypeStruct((8, width), f32), jax.ShapeDtypeStruct((n, width), bf16)],
        in_specs=[in_place()] * (8 + len(saved) + 7) + [in_vmem()] * 5,
        out_specs=[in_vmem()] * (len(plan) + 2),
        scratch_shapes=scratch,
        compiler_params=pltpu.CompilerParams(
            collective_id=2, has_side_effects=True, vmem_limit_bytes=BACK_LIMIT
        ),
    )(*lefts, *rights, *saved, *weights, first, tokens, bias, flags, head_gain, pre_gain, postgain)
    return out[: len(plan)], out[-2], out[-1]


def finish_kernel(count, *refs):
    vectors, outs = refs[count], refs[count + 1 :]
    for i in range(count):
        outs[i][...] = refs[i][...]
    for i, out in enumerate(outs[count:]):
        out[...] = vectors[i, : out.shape[0]]


def finish(arrays, vectors, sizes):
    count = len(arrays)
    return pl.pallas_call(
        functools.partial(finish_kernel, count),
        name="finish",
        out_shape=[jax.ShapeDtypeStruct(a.shape, a.dtype) for a in arrays]
        + [jax.ShapeDtypeStruct((size,), f32) for size in sizes],
        in_specs=[in_vmem()] * (count + 1),
        out_specs=[in_vmem()] * (count + len(sizes)),
        compiler_params=pltpu.CompilerParams(vmem_limit_bytes=LIMIT),
    )(*arrays, vectors)


def by_owner(a, hi, lo):
    features, tokens = a.shape
    r = features // (hi * lo * 4)
    t = a.reshape(hi, lo, 2, 2, r, tokens).transpose(3, 1, 2, 0, 4, 5).reshape(2, lo * 2, hi * r, tokens)
    pad = -(hi * r) % 16
    if pad:
        t = jnp.pad(t, ((0, 0), (0, 0), (0, pad), (0, 0)))
    return t.reshape(2, -1, tokens)


def body(
    size, tokens, resets, pre_gain, query_weight, key_weight, value_weight, forget_weight, forget_bias,
    outgate_weight, output_weight, head_gain, post_gain, gate_weight, up_weight, down_weight, cotangent,
):
    lo = 8
    hi = size // lo
    streams, length, width = tokens.shape
    n = streams * length
    head = head_gain.shape[0]
    heads = width // head
    shards = {
        "query": query_weight, "key": key_weight, "value": value_weight, "forget": forget_weight,
        "outgate": outgate_weight, "output": output_weight, "gate": gate_weight, "up": up_weight, "down": down_weight,
    }
    ff = gate_weight.shape[1]
    flat, cotan = tokens.reshape(n, width), cotangent.reshape(n, width)
    bias, gain = forget_bias[None], head_gain[None]
    (
        block_output, first_delta, attn_delta, merged_delta, postgain_grad,
        normed_t, merged_t, second_t, hidden_t, gate_delta, up_delta,
        q, k, v, pre, logits, mixed, aff, mixing, weights, inner, state, passed, pass_all, *wholes,
    ) = front(
        size, heads, hi == 1, shards, flat, cotan, pre_gain[None], post_gain[None],
        gain, bias, resets,
    )
    lefts = [hidden_t, second_t, merged_t, normed_t]
    if hi > 1:
        lefts = [by_owner(a, hi, lo) for a in lefts]
    rights = [cotan, gate_delta, up_delta, attn_delta]
    columns = (width, ff, ff, width, width, width, width, width, bias.shape[1])
    kept_rows = [(ff if i == 0 else width) // (lo * 4) for i in range(len(FORM))]
    padded = [-(-r // 16) * 16 for r in kept_rows]
    pieces = cut(tuple(zip(columns, padded)))
    plan = [(left, columns[i], padded[i], kept_rows[i], pieces[i]) for i, (_, left) in enumerate(FORM)]
    saved = dict(
        q=q, k=k, v=v, pre=pre, logits=logits, mixed=mixed, aff=aff, mixing=mixing, weights=weights, inner=inner,
        state=state, mdelta=merged_delta, pass_all=pass_all,
    )
    saved["pass"] = passed
    grads, vectors, input_grad = back(
        size, heads, tuple(plan), lefts, rights, saved, wholes, first_delta, flat, bias, resets, gain,
        pre_gain[None], postgain_grad,
    )
    if hi > 1:
        alike = [[a * lo + b for a in range(hi)] for b in range(lo)]
        grads = [
            lax.psum_scatter(g, "seq", scatter_dimension=0, axis_index_groups=alike, tiled=True)
            for g in grads
        ]
        vectors = lax.psum(vectors, "seq", axis_index_groups=alike)
    down_grad, gate_grad, up_grad, output_grad, outgate_grad, query_grad, key_grad, value_grad, forget_grad = grads
    shape = tokens.shape
    got = finish(
        (
            block_output, input_grad, query_grad, key_grad, value_grad, forget_grad, outgate_grad, output_grad,
            gate_grad, up_grad, down_grad,
        ), vectors, (width, bias.shape[1], head, width),
    )
    pregain, bias_total, headgain, postgain = got[11:]
    return (
        got[0].reshape(shape), got[1].reshape(shape), pregain, *got[2:6], bias_total, *got[6:8], headgain,
        postgain, *got[8:11],
    )


def solution(mesh):
    rows, whole, both = P("fsdp", None), P(), P(("seq", "fsdp"), None)
    return jax.shard_map(
        functools.partial(body, mesh.shape["seq"]),
        mesh=mesh,
        in_specs=(
            P("fsdp", "seq", None), P("fsdp", "seq"), whole, rows, rows, rows, rows, whole, rows, rows,
            whole, whole, rows, rows, rows, P("fsdp", "seq", None),
        ),
        out_specs=(
            P("fsdp", "seq", None), P("fsdp", "seq", None), whole, both, both, both, both, whole, both,
            both, whole, whole, both, both, both,
        ),
        check_vma=False,
    )
```

```python
import functools

import jax
import jax.numpy as jnp
from jax import lax
from jax.experimental import pallas as pl
from jax.experimental.pallas import tpu as pltpu
from jax.sharding import PartitionSpec as P

BLOCK = 64
TILE = 256
norm_eps = 1e-06
f32, bf16 = jnp.float32, jnp.bfloat16
MESH = pl.DeviceIdType.MESH
VMEM = pltpu.VMEM
ANY = pl.ANY
LIMIT = 60 * 2**20


def in_vmem():
    return pl.BlockSpec(memory_space=VMEM)


def in_place():
    return pl.BlockSpec(memory_space=ANY)


def greet(partners):
    barrier = pltpu.get_barrier_semaphore()
    for partner in partners:
        pl.semaphore_signal(barrier, inc=1, device_id=partner, device_id_type=MESH)
    pl.semaphore_wait(barrier, len(partners))


def remote(src, dst, sems, index, partner):
    return pltpu.make_async_remote_copy(
        src_ref=src,
        dst_ref=dst,
        send_sem=sems[0].at[index],
        recv_sem=sems[1].at[index],
        device_id=partner,
        device_id_type=MESH,
    )


def parts_of(a, count):
    if a.dtype == bf16:
        return [a]
    out = []
    for i in range(count):
        part = a.astype(bf16)
        out.append(part)
        if i + 1 < count:
            a = a - part.astype(f32)
    return out


def dot(a, b, ca=1, cb=0, count=1):
    total = None
    for right in reversed(parts_of(b, count)):
        term = lax.dot_general(
            a.astype(bf16), right, (((ca,), (cb,)), ((), ())), preferred_element_type=f32
        )
        total = term if total is None else total + term
    return total


def to_col(row):
    n = row.shape[1]
    i = lax.broadcasted_iota(jnp.int32, (n, n), 0)
    j = lax.broadcasted_iota(jnp.int32, (n, n), 1)
    return jnp.sum(jnp.where(i == j, jnp.broadcast_to(row, (n, n)), 0.0), axis=1, keepdims=True)


def mask_set(flags):
    row = jnp.concatenate([flags[i : i + 1].astype(f32) for i in range(flags.shape[0])], axis=1)
    n = row.shape[1]
    flags_row = jnp.broadcast_to(row, (8, n))
    i = lax.broadcasted_iota(jnp.int32, (n, n), 0)
    j = lax.broadcasted_iota(jnp.int32, (n, n), 1)
    same = (i // BLOCK) == (j // BLOCK)
    lower = jnp.where(same & (i >= j), 1.0, 0.0)
    block = jnp.where(same, 1.0, 0.0)
    seen_col = dot(lower, flags_row, 1, 1)[:, :1]
    all_col = dot(block, flags_row, 1, 1)[:, :1]
    seen_row = dot(flags_row, lower, 1, 1)[:1, :]
    linked = jnp.where(seen_col == seen_row, lower, 0.0)
    fresh = jnp.where(seen_col == 0.0, 1.0, 0.0)
    ending = jnp.where(seen_col == all_col, 1.0, 0.0)
    unbroken = jnp.where(all_col == 0.0, 1.0, 0.0)
    return lower, linked, fresh, ending, unbroken


def gate_set(pre, bias, lower, ending):
    z = pre + bias
    u = jnp.exp(-jnp.abs(z))
    lp = jnp.where(
        u < 0.02, u * (1.0 - u * (0.5 - u * (1.0 / 3.0 - 0.25 * u))), jnp.log(1.0 + u)
    )
    g = (jnp.minimum(z, 0.0) - lp) * 0.125
    series = 1.0 + g * (1.0 / 7.0)
    for order in (6, 5, 4, 3, 2):
        series = 1.0 + g * (1.0 / order) * series
    oma = jnp.where(g > -0.35, -g * series, 1.0 - jnp.exp(g))
    a = dot(lower, g, count=3)
    n, lanes = a.shape
    last = jnp.concatenate(
        [
            jnp.broadcast_to(a[b * BLOCK + BLOCK - 1 : b * BLOCK + BLOCK], (BLOCK, lanes))
            for b in range(n // BLOCK)
        ],
        axis=0,
    )
    tail = jnp.exp(last - a) * ending
    return z, u, oma, jnp.exp(a), jnp.exp(-a), tail


def rows_of(b):
    return slice(b * BLOCK, (b + 1) * BLOCK)


def passing(growth, unbroken, b, hs):
    last = b * BLOCK + BLOCK - 1
    return to_col(growth[last : last + 1, hs] * unbroken[last : last + 1])


def sigmoid(v):
    return 1.0 / (1.0 + jnp.exp(-v))


WEIGHTS = ("key", "value", "forget", "query", "outgate", "output", "gate", "up", "down")
TWICE = ("output", "gate", "up", "down", "rest")
PARTS = WEIGHTS + ("rest",)


RESULTS = (
    "block", "first", "attn", "mdelta", "postgain", "normed_t", "merged_t", "second_t", "hidden_t", "gate_delta",
    "up_delta", "q", "k", "v", "pre", "logits", "mixed", "aff", "mixing", "weights", "inner", "state", "pass", "pass_all",
)
SHARED = ("normed_t", "merged_t", "second_t", "hidden_t")


def front_kernel(size, heads, grouped, *refs):
    count = len(WEIGHTS)
    shards, refs = dict(zip(WEIGHTS, refs[:count])), refs[count:]
    (tok_ref, cot_ref, pre_gain, post_gain, head_gain, bias_ref, flag_ref), refs = refs[:7], refs[7:]
    results, refs = dict(zip(RESULTS, refs[: len(RESULTS)])), refs[len(RESULTS) :]
    passed, refs = dict(zip(WEIGHTS[:5], refs[:5])), refs[5:]
    held, refs = refs[: len(RESULTS)], refs[len(RESULTS) :]
    (
        out_ref, first_ref, attn_ref, mdelta_ref, postgain_grad,
        normed_t, merged_t, second_t, hidden_t, gate_delta, up_delta,
        q_ref, k_ref, v_ref, pre_ref, logit_ref,
        mixed_ref, aff_ref, mixing_ref, weight_ref, inner_ref, state_ref, pass_ref, pass_all,
    ) = held
    held = dict(zip(RESULTS, held))
    whole, refs = dict(zip(WEIGHTS, refs[:count])), refs[count:]
    (
        normed, merged, one_ref, second, block_acc, delta_acc, flat_t,
        ends, going, gathered, prefix, came,
        local, send_sem, recv_sem, away, st_send, st_recv, out_sem, share_send, share_recv,
    ) = refs
    sems = (send_sem, recv_sem)
    s, f = lax.axis_index("seq"), lax.axis_index("fsdp")
    q = lax.rem(s, 4)
    kind_bit = lax.rem(q + q // 2, 2)
    sib, far, nx, nz = (s, f ^ 1), (s, f ^ 2), (s ^ 1, f), (s ^ 2, f)
    fy, fs = f ^ 2, f ^ 3
    others = [(lax.rem(s + d, size), f) for d in range(1, size)]
    greet([sib, far] + others)
    started = []

    def go(copy):
        copy.start()
        started.append(copy)

    leaving = []

    def emit(*names):
        n = tok_ref.shape[0]
        for name in names:
            source, to, i = held[name], results[name], RESULTS.index(name)
            if grouped and name in SHARED:
                far_half = to.at[:, pl.ds(n, n)]
                core = lax.rem(f, 2)
                j = SHARED.index(name)
                copy = remote(source.at[1 - core], far_half, (share_send, share_recv), j, sib)
                copy.start()
                leaving.append(copy)
                source, to = source.at[core], to.at[:, pl.ds(0, n)]
            copy = pltpu.make_async_copy(source, to, out_sem.at[i])
            copy.start()
            leaving.append(copy)

    spot = {m: (m, 0, shards[m].shape[0]) for m in WEIGHTS}
    rows = shards["down"].shape[0]
    lead = rows // 2 // 64 * 64
    spot["down"], spot["rest"] = ("down", 0, lead), ("down", lead, rows - lead)

    def piece(m, owner, start, length):
        name, first, _ = spot[m]
        rows = shards[name].shape[0]
        return whole[name].at[pl.ds(pl.multiple_of(owner * rows + first + start, 16), length)]

    def quarter(m, owner, which, half=None):
        rows = spot[m][2] // 4
        first = (rows // 2 + 15) // 16 * 16
        start, length = (0, rows) if half is None else ((0, first), (first, rows - first))[half]
        return piece(m, owner, which * rows + start, length)

    def eighth(m, owner, bit, half):
        rows = spot[m][2] // 2
        return piece(m, owner, bit * rows + half * (rows // 2), rows // 2)

    def mine(m, owner):
        if m in TWICE:
            rows = spot[m][2] // 2
            return piece(m, owner, kind_bit * rows, rows)
        return quarter(m, owner, q)

    def from_x(m, owner):
        return eighth(m, owner, 1 - kind_bit, 0) if m in TWICE else quarter(m, owner, q ^ 1)

    def from_z(m, owner):
        return eighth(m, owner, 1 - kind_bit, 1) if m in TWICE else quarter(m, owner, q ^ 2)

    def send(kind, m, part, partner):
        go(remote(part, part, sems, (kind, PARTS.index(m)), partner))

    def arrived(kind, m, part):
        remote(part, part, sems, (kind, PARTS.index(m)), sib).wait_recv()

    for i, m in enumerate(PARTS):
        name, first, rows = spot[m]
        if m in TWICE:
            src = shards[name].at[pl.ds(pl.multiple_of(first + kind_bit * (rows // 2), 16), rows // 2)]
        else:
            src = shards[name].at[pl.ds(pl.multiple_of(first + q * (rows // 4), 16), rows // 4)]
        go(remote(src, mine(m, f), sems, (1, i), far))

    def own_rows(m, owner):
        rows = shards[m].shape[0]
        return whole[m].at[pl.ds(pl.multiple_of(owner * rows, 16), rows)]

    own = {}
    for i, m in enumerate(WEIGHTS):
        go(remote(shards[m], own_rows(m, f), sems, (0, i), sib))
        own[m] = pltpu.make_async_copy(shards[m], own_rows(m, f), local.at[i])
        own[m].start()

    def pass_first(m):
        part = mine(m, fy)
        arrived(1, m, part)
        if m in TWICE:
            send(2, m, eighth(m, fy, kind_bit, 0), nx)
            send(3, m, eighth(m, fy, kind_bit, 1), nz)
        else:
            send(2, m, part, nx)
            send(3, m, part, nz)
        send(6, m, part, sib)

    def pass_second(m):
        arrived(2, m, from_x(m, fy))
        if m not in TWICE:
            send(4, m, quarter(m, fy, q ^ 1, 0), nz)
        send(7, m, from_x(m, fy), sib)
        arrived(3, m, from_z(m, fy))
        if m not in TWICE:
            send(5, m, quarter(m, fy, q ^ 2, 1), nx)
        send(8, m, from_z(m, fy), sib)

    def pass_third(m):
        if m not in TWICE:
            for kind in (4, 5):
                part = quarter(m, fy, q ^ 3, kind - 4)
                arrived(kind, m, part)
                send(kind + 5, m, part, sib)

    def pump(step):
        for late, stage in enumerate((pass_first, pass_second, pass_third)):
            if 0 <= step - late < len(PARTS):
                stage(PARTS[step - late])

    def ready(m):
        own[m].wait()
        arrived(0, m, own_rows(m, f ^ 1))
        for part in ("down", "rest") if m == "down" else (m,):
            arrived(6, part, mine(part, fs))
            arrived(7, part, from_x(part, fs))
            arrived(8, part, from_z(part, fs))
            if part not in TWICE:
                arrived(9, part, quarter(part, fs, q ^ 3, 0))
                arrived(10, part, quarter(part, fs, q ^ 3, 1))

    n, width = tok_ref.shape
    head = width // heads
    slots = bias_ref.shape[1] // heads
    blocks = n // BLOCK
    streams = 2
    per = blocks // streams
    pairs = heads * streams
    scale = head ** (-0.5)

    def across(columns, step):
        def turn(i, carry):
            step(pl.ds(pl.multiple_of(i * TILE, TILE), TILE))
            return carry

        lax.fori_loop(0, columns // TILE, turn, 0)

    def project(m, to_ref):
        def step(at):
            to_ref[:, at] = dot(normed[...], whole[m][:, at]).astype(to_ref.dtype)

        across(whole[m].shape[1], step)

    def turn_over(source, to_ref, rows, padded):
        if not grouped:
            to_ref[...] = source[...].astype(bf16)
            return
        for group in range(16):
            for core in range(2):
                at = (group * 2 + core) * rows
                to_ref[core, group * padded : group * padded + rows] = source[at : at + rows].astype(bf16)

    inputs = tok_ref[...].astype(f32)
    unit = inputs * lax.rsqrt(jnp.mean(inputs * inputs, axis=1, keepdims=True) + norm_eps)
    scaled = unit * pre_gain[...]
    normed[...] = scaled.astype(bf16)
    turn_over(scaled.T, normed_t, width // 32, width // 32)
    emit("normed_t")
    for step in range(5):
        pump(step)
    for m, to_ref in (("key", k_ref), ("value", v_ref), ("forget", pre_ref)):
        ready(m)
        project(m, to_ref)
    emit("k", "v", "pre")
    lower, linked, fresh, ending, unbroken = mask_set(flag_ref[...])
    z, u, oma, growth, inverse, tail = gate_set(pre_ref[...], bias_ref[...], lower, ending)
    shrink, kept = inverse * oma, tail * oma
    for h in range(heads):
        hs, hd = slice(h * slots, (h + 1) * slots), slice(h * head, (h + 1) * head)
        for stream in range(streams):
            pair = h * streams + stream
            total, through = None, None
            for b in range(stream * per, (stream + 1) * per):
                part = kept[rows_of(b), hs].astype(bf16)
                at = pair * per + b % per
                end_k = dot(part, k_ref[rows_of(b), hd], 0, 0)
                end_v = dot(part, v_ref[rows_of(b), hd], 0, 0)
                ends[at, :, :head] = end_k
                ends[at, :, head:] = end_v
                factor = passing(growth, unbroken, b, hs)
                pass_ref[at] = jnp.broadcast_to(factor, pass_ref.shape[1:])
                if total is None:
                    total, through = (end_k, end_v), factor
                else:
                    total = (factor * total[0] + end_k, factor * total[1] + end_v)
                    through = through * factor
            at = slice(pair * slots, (pair + 1) * slots)
            going[at, :head] = total[0].astype(bf16)
            going[at, head : 2 * head] = total[1].astype(bf16)
            going[at, 2 * head :] = jnp.broadcast_to(through, (slots, going.shape[1] - 2 * head)).astype(bf16)

    share = pairs * slots // size

    def rows_for(place):
        return pl.ds(pl.multiple_of(place * share, 16), share)

    first_hop, second_hop = [], []
    for d in range(1, size):
        to = others[d - 1]
        copy = remote(going.at[rows_for(to[0])], gathered.at[s], (st_send, st_recv), (0, d - 1), to)
        go(copy)
        first_hop.append(lax.rem(s + size - d, size))
    gathered[s] = going[rows_for(s)]
    pump(5)
    pump(6)
    for m, to_ref in (("query", q_ref), ("outgate", logit_ref)):
        ready(m)
        project(m, to_ref)
    emit("q", "logits", "pass")
    for i, m in enumerate(WEIGHTS[:5]):
        copy = pltpu.make_async_copy(whole[m], passed[m], away.at[i])
        copy.start()
        own[m] = copy
    for d in range(1, size):
        source = first_hop[d - 1]
        remote(gathered.at[source], gathered.at[source], (st_send, st_recv), (0, d - 1), sib).wait_recv()
    state = jnp.zeros((share, 2 * head), f32)
    for place in range(size):
        prefix[place] = state.astype(bf16)
        entry = gathered[place].astype(f32)
        pass_all[place] = gathered[place][:, 2 * head :]
        state = entry[:, 2 * head : 2 * head + 1] * state + entry[:, : 2 * head]
    for d in range(1, size):
        to = others[d - 1]
        go(remote(prefix.at[to[0]], came.at[rows_for(s)], (st_send, st_recv), (1, d - 1), to))
    came[rows_for(s)] = prefix[s]
    emit("pass_all")
    pump(7)
    for h in range(heads):
        hd = slice(h * head, (h + 1) * head)
        aff_ref[h] = (dot(q_ref[:, hd], k_ref[:, hd], 1, 1) * (linked * scale)).astype(bf16)
    emit("aff")
    for d in range(1, size):
        part = came.at[rows_for(first_hop[d - 1])]
        remote(part, part, (st_send, st_recv), (1, d - 1), sib).wait_recv()
    for h in range(heads):
        hs, hd = slice(h * slots, (h + 1) * slots), slice(h * head, (h + 1) * head)
        for stream in range(streams):
            pair = h * streams + stream
            state = came[pair * slots : (pair + 1) * slots].astype(f32)
            for b in range(per):
                at = pair * per + b
                state_ref[pair, b] = state.astype(bf16)
                state = pass_ref[at][:, :1] * state + ends[at]
            state_ref[pair, per] = state.astype(bf16)
        gr, sh = growth[:, hs], shrink[:, hs]
        qh, vh = q_ref[:, hd], v_ref[:, hd]
        carried = jnp.concatenate(
            [
                dot(qh[rows_of(b)], state_ref[h * streams + b // per, b % per, :, :head], 1, 1)
                for b in range(blocks)
            ],
            axis=0,
        )
        inner = dot(aff_ref[h], sh) + carried * (scale * fresh)
        scores = gr * inner
        e = jnp.exp(scores - jnp.max(scores, axis=1, keepdims=True))
        weights = e / jnp.sum(e, axis=1, keepdims=True)
        weight_ref[:, hs] = weights
        inner_ref[:, hs] = inner
        lifted = weights * gr
        mixing = (dot(lifted, sh.astype(bf16), 1, 1) * linked).astype(bf16)
        mixing_ref[h] = mixing
        brought = jnp.concatenate(
            [
                dot(lifted[rows_of(b)], state_ref[h * streams + b // per, b % per, :, head:])
                for b in range(blocks)
            ],
            axis=0,
        )
        mixed = dot(mixing, vh) + brought * fresh
        mixed_ref[:, hd] = mixed
        r = lax.rsqrt(jnp.mean(mixed * mixed, axis=1, keepdims=True) + norm_eps)
        logits = logit_ref[:, hd]
        delta_acc[:, hd] = mixed * r * head_gain[...] * (logits * sigmoid(logits))
        merged[:, hd] = delta_acc[:, hd].astype(bf16)
    emit("mixed", "mixing", "weights", "inner", "state")
    pass_first("down")
    pass_second("up")
    ready("output")

    def join(at):
        one_ref[:, at] = tok_ref[:, at].astype(f32) + dot(merged[...], whole["output"][:, at])

    across(width, join)
    turn_over(delta_acc[...].T, merged_t, width // 32, width // 32)
    emit("merged_t")
    one = one_ref[...]
    scaled = one * lax.rsqrt(jnp.mean(one * one, axis=1, keepdims=True) + norm_eps) * post_gain[...]
    second[...] = scaled.astype(bf16)
    turn_over(scaled.T, second_t, width // 32, width // 32)
    emit("second_t")
    pass_first("rest")
    ready("gate")
    ready("up")
    block_acc[...] = one
    delta_acc[...] = jnp.zeros_like(delta_acc)

    def open_tile(i, carry):
        at = pl.ds(pl.multiple_of(i * TILE, TILE), TILE)
        gate_vals, up_vals = dot(second[...], whole["gate"][:, at]), dot(second[...], whole["up"][:, at])
        sig = sigmoid(gate_vals)
        silu = gate_vals * sig
        flat_t[at] = (silu * up_vals).T
        up_delta[:, at] = silu.astype(bf16)
        gate_delta[:, at] = (up_vals * (sig + silu * (1.0 - sig))).astype(bf16)
        return carry

    def unit_tile(i, carry):
        at = pl.ds(pl.multiple_of(i * TILE, TILE), TILE)
        w_gate, w_up, w_down = whole["gate"][:, at], whole["up"][:, at], whole["down"][at]
        hidden_delta = dot(cot_ref[...], w_down, 1, 1)
        d_up = (hidden_delta * up_delta[:, at].astype(f32)).astype(bf16)
        d_gate = (hidden_delta * gate_delta[:, at].astype(f32)).astype(bf16)
        gate_delta[:, at] = d_gate
        up_delta[:, at] = d_up
        block_acc[...] += dot(flat_t[at].astype(bf16), w_down, 0, 0)
        delta_acc[...] += dot(d_gate, w_gate, 1, 1) + dot(d_up, w_up, 1, 1)
        return carry

    ff = whole["gate"].shape[1]
    lax.fori_loop(0, ff // TILE, open_tile, 0)
    turn_over(flat_t, hidden_t, ff // 32, -(-(ff // 32) // 16) * 16)
    emit("hidden_t")
    pass_second("down")
    pass_second("rest")
    ready("down")
    lax.fori_loop(0, ff // TILE, unit_tile, 0)
    out_ref[...] = block_acc[...].astype(bf16)
    emit("block", "gate_delta", "up_delta")
    one = one_ref[...]
    r = lax.rsqrt(jnp.mean(one * one, axis=1, keepdims=True) + norm_eps)
    unit = one * r
    delta = delta_acc[...]
    postgain_grad[...] = jnp.sum(delta * unit, axis=0, keepdims=True)
    delta = delta * post_gain[...]
    first = cot_ref[...].astype(f32) + r * (delta - unit * jnp.mean(unit * delta, axis=1, keepdims=True))
    first_ref[...] = first
    attn_ref[...] = first.astype(bf16)
    emit("postgain", "first", "attn")

    def split(at):
        mdelta_ref[:, at] = dot(attn_ref[...], whole["output"][at], 1, 1)

    across(width, split)
    emit("mdelta")
    for copy in leaving:
        copy.wait()
    for m in WEIGHTS[:5]:
        own[m].wait()
    for copy in started:
        copy.wait_send()


def front(size, heads, grouped, shards, tokens, cotan, pre_gain, post_gain, head_gain, bias, flags):
    n, width = tokens.shape
    head, slots = width // heads, bias.shape[1] // heads
    pairs, per = heads * 2, n // BLOCK // 2
    ff = shards["gate"].shape[1]
    shards = [shards[m] for m in WEIGHTS]
    count = len(shards)
    padded = -(-(ff // 32) // 16) * 512

    def turned(rows, grouped_rows):
        return low(grouped_rows // 2, 2 * n) if grouped else low(rows, n)

    def low(*shape):
        return jax.ShapeDtypeStruct(shape, bf16)

    def full(*shape):
        return jax.ShapeDtypeStruct(shape, f32)

    outs = [
        low(n, width), full(n, width), low(n, width), full(n, width), full(1, width),
        turned(width, width), turned(width, width), turned(width, width), turned(ff, padded),
        low(n, ff), low(n, ff),
        low(n, width), low(n, width), low(n, width), full(n, heads * slots), full(n, width),
        full(n, width), low(heads, n, n), low(heads, n, n), full(n, heads * slots), full(n, heads * slots),
        low(pairs, per + 1, slots, 2 * head), full(pairs * per, slots, 128),
        low(size, pairs * slots // size, 128),
    ]
    wholes = [low(4 * w.shape[0], w.shape[1]) for w in shards]
    keeps = [
        (2, o.shape[0], n) if grouped and name in SHARED else o.shape for name, o in zip(RESULTS, outs)
    ]
    share = pairs * slots // size
    dma = pltpu.SemaphoreType.DMA
    got = pl.pallas_call(
        functools.partial(front_kernel, size, heads, grouped),
        name="front",
        out_shape=outs + wholes[:5],
        in_specs=[in_place()] * count + [in_vmem()] * 7,
        out_specs=[in_place()] * (len(outs) + 5),
        scratch_shapes=[VMEM(shape, o.dtype) for shape, o in zip(keeps, outs)]
        + [VMEM(w.shape, bf16) for w in wholes]
        + [
            VMEM((n, width), bf16),
            VMEM((n, width), bf16),
            VMEM((n, width), f32),
            VMEM((n, width), bf16),
            VMEM((n, width), f32),
            VMEM((n, width), f32),
            VMEM((ff, n), f32),
            VMEM((pairs * per, slots, 2 * head), f32),
            VMEM((pairs * slots, 2 * head + 128), bf16),
            VMEM((size, share, 2 * head + 128), bf16),
            VMEM((size, share, 2 * head), bf16),
            VMEM((pairs * slots, 2 * head), bf16),
            dma((count,)),
            dma((11, len(PARTS))),
            dma((11, len(PARTS))),
            dma((5,)),
            dma((2, size - 1)),
            dma((2, size - 1)),
            dma((len(RESULTS),)),
            dma((len(SHARED),)),
            dma((len(SHARED),)),
        ],
        compiler_params=pltpu.CompilerParams(
            collective_id=1, has_side_effects=True, vmem_limit_bytes=LIMIT
        ),
    )(*shards, tokens, cotan, pre_gain, post_gain, head_gain, bias, flags)
    return got


def to_row(col):
    n = col.shape[0]
    i = lax.broadcasted_iota(jnp.int32, (n, n), 0)
    j = lax.broadcasted_iota(jnp.int32, (n, n), 1)
    return jnp.sum(jnp.where(i == j, jnp.broadcast_to(col, (n, n)), 0.0), axis=0, keepdims=True)


LEAST, SHALLOW, DEEP = 4.0, 8.0, 10.0
STRIPS = 3
BACK_LIMIT = 63 * 2**20


ROUTES = (("y", "z", "x", "zz"), ("x", "z", "y", "zz"), ("y", "x", "z", "zz"), ("x", "y", "z", "zz"))
STATES = {"x": 1.15, "y": 0.0, "z": 1.75}


def cut(sizes):
    load, plan, last = dict(STATES), [], 1
    for columns, rows in sizes:
        tiles = columns // TILE
        pieces = min(4, 2 * tiles) if tiles <= 4 else 6
        width = columns // pieces if tiles <= 1 else TILE
        out, start = [], 0
        for i in range(pieces):
            count = 1 if tiles <= 1 else tiles // pieces + (1 if i < tiles % pieces else 0)
            size = 2 * 16 * rows * width * count * 2 / 1e6

            def after(route):
                new = dict(load)
                for stage, link in enumerate(ROUTES[route]):
                    new["z" if link == "zz" else link] += size / 2 ** (stage + 1)
                return new

            route = min((1 - last, 3 - last), key=lambda r: sum(v**4 for v in after(r).values()))
            load, last = after(route), route % 2
            out.append((start, width * count, route))
            start += width * count
        plan.append(tuple(out))
    return plan


def in_order(chunks, path, held_back, least, shallow, deep):
    now, free = 0.0, dict.fromkeys(("x", "y", "z", "zz"), 0.0)
    came, done, coming, out = {}, set(), [], []
    path, left = list(path), list(range(len(chunks)))
    rate, delay = 0.045, 2.0

    def leave(c, stage):
        rows, width, order = chunks[c][1], chunks[c][3], chunks[c][4]
        link = ROUTES[order][stage]
        size = 16 * rows * width * 2 / 1e6 / 2 ** (stage + 1)
        free[link] = max(now, free[link]) + size / rate * (2 if stage == 3 else 1)
        coming.append((free[link] + delay, c, stage))

    while left or path or coming:
        here = sorted(a for a in coming if a[0] <= now)
        open_ = [c for c in left if held_back.get(chunks[c][0], None) in done or chunks[c][0] not in held_back]
        depth = deep if "second hop" in done else shallow
        queue = free[ROUTES[chunks[open_[0]][4]][0]] - now if open_ else 0.0
        ready = path and came.get(path[0][2], 0.0 if path[0][2] is None else 1e9) <= now
        if here:
            _, c, stage = here[0]
            coming.remove(here[0])
            now += 0.1 + 0.1 * chunks[c][1] / 32 * chunks[c][3] / TILE / 2**stage
            out.append(("advance", c, stage))
            if stage < 3:
                leave(c, stage + 1)
        elif ready and not (open_ and queue < least):
            name, time, _, starts, takes = path.pop(0)
            now += time
            done.add(name)
            out.append(("path", name, None))
            if starts:
                came[starts] = now + takes
        elif open_ and queue < depth:
            c = open_[0]
            left.remove(c)
            now += 0.1 + 0.3 * chunks[c][1] / 32 * chunks[c][3] / TILE
            out.append(("produce", c, None))
            leave(c, 0)
        else:
            later = [a[0] for a in coming]
            if path and path[0][2] in came:
                later.append(came[path[0][2]])
            if open_:
                later.append(now + queue - depth)
            now = max(now + 0.05, min(later))
    return out


FORM = (("cotan", 0), ("gate", 1), ("up", 1), ("attn", 2), ("outgate", 3), ("query", 3), ("key", 3), ("value", 3), ("forget", 3))
SAVED = ("q", "k", "v", "pre", "logits", "mixed", "aff", "mixing", "weights", "inner", "state", "pass", "mdelta", "pass_all")


def back_kernel(size, heads, plan, *refs):
    def take(count):
        nonlocal refs
        got, refs = refs[:count], refs[count:]
        return got

    lefts, rights, saved = take(4), take(4), dict(zip(SAVED, take(len(SAVED))))
    weights, (first_in, tokens_in) = take(5), take(2)
    bias_ref, flag_ref, head_gain, pre_gain, postgain_ref = take(5)
    outs, (vec_out, input_grad) = take(9), take(2)
    left_all, right_all = take(4), take(9)
    have_ref = dict(zip(SAVED, take(len(SAVED))))
    chunks = [(g, p[2]) + c for g, p in enumerate(plan) for c in p[4]]
    nc = len(chunks)
    sums = take(nc)
    landed = [take(nc) for _ in range(4)]
    owed, da_acc, doma_acc, strip, going, gathered, prefix, came, vec_acc, vec_got = take(10)
    loads, in_local, in_send, in_recv, strip_sem, first_sem = take(6)
    hop_send, hop_recv, st_send, st_recv, v_send, v_recv = take(6)
    q_ref, k_ref, v_ref = have_ref["q"], have_ref["k"], have_ref["v"]
    logit_ref, mixed_ref, mdelta_ref = have_ref["logits"], have_ref["mixed"], have_ref["mdelta"]
    state_ref, pass_ref = have_ref["state"], have_ref["pass"]

    s, f = lax.axis_index("seq"), lax.axis_index("fsdp")
    core, y = lax.rem(f, 2), f // 2
    x, z_low, z_high = lax.rem(s, 2), lax.rem(s // 2, 2), lax.rem(s // 4, 2)
    sib, far, nx, nz, nzz = (s, f ^ 1), (s, f ^ 2), (s ^ 1, f), (s ^ 2, f), (s ^ 4, f)
    others = [(lax.rem(s + d, size), f) for d in range(1, size)]
    greet([sib, far] + others)
    started = []

    def go(copy):
        copy.start()
        started.append(copy)

    n, width = q_ref.shape
    head = width // heads
    slots = bias_ref.shape[1] // heads
    blocks = n // BLOCK
    streams = 2
    per = blocks // streams
    pairs = heads * streams
    scale = head ** (-0.5)
    share = pairs * slots // size

    waiting = {}

    def fetch_left(i):
        if len(lefts[i].shape) == 2:
            keep = pltpu.make_async_copy(lefts[i], left_all[i], in_local.at[i])
            keep.start()
            waiting["left", i] = [keep, None]
            return
        keep = pltpu.make_async_copy(lefts[i].at[core], left_all[i].at[:, pl.ds(0, n)], in_local.at[i])
        keep.start()
        copy = remote(lefts[i].at[1 - core], left_all[i].at[:, pl.ds(n, n)], (in_send, in_recv), i, sib)
        go(copy)
        waiting["left", i] = [keep, copy]

    def fetch_right(i):
        own, other = right_all[i].at[pl.ds(0, n)], right_all[i].at[pl.ds(n, n)]
        keep = None
        src = own
        if i < 4:
            src = rights[i]
            keep = pltpu.make_async_copy(src, own, in_local.at[4 + i])
            keep.start()
        copy = remote(src, other, (in_send, in_recv), 4 + i, sib)
        go(copy)
        waiting["right", i] = [keep, copy]

    def have(kind, i):
        pair = waiting[kind, i]
        if pair:
            if pair[0] is not None:
                pair[0].wait()
            if pair[1] is not None:
                pair[1].wait_recv()
            waiting[kind, i] = None

    fetch_left(0)
    fetch_right(0)
    loading = []
    for i, name in enumerate(SAVED):
        copy = pltpu.make_async_copy(saved[name], have_ref[name], loads.at[i])
        copy.start()
        loading.append(copy)
    for i in (1, 2, 3):
        fetch_right(i)
    for i in (1, 2, 3):
        fetch_left(i)

    strips = [(w, t * TILE) for w in range(5) for t in range(weights[w].shape[1] // TILE)]

    def strip_copy(i):
        w, at = strips[i]
        return pltpu.make_async_copy(weights[w].at[:, pl.ds(at, TILE)], strip.at[i % STRIPS], strip_sem.at[i % STRIPS])

    for i in range(STRIPS):
        strip_copy(i).start()

    def route(c):
        names = ROUTES[chunks[c][4]]
        places, partners = dict(x=x, y=y, z=z_low, zz=z_high), dict(x=nx, y=far, z=nz, zz=nzz)
        return tuple(places[i] for i in names), tuple(partners[i] for i in names)

    def stage_copy(c, stage):
        bits, partners = route(c)
        at = bits[:stage] + (1 - bits[stage],)
        return remote(sums[c].at[at], landed[stage][c], (st_send, st_recv), (stage, c), partners[stage])

    def produce(c):
        g, rows, start, wide, order = chunks[c]
        left = plan[g][0]
        have("left", left)
        have("right", g)
        tile = min(TILE, wide)

        def turn(i, carry):
            at = pl.multiple_of(start + i * tile, 128)
            to = pl.multiple_of(i * tile, 128)
            got = jnp.dot(
                left_all[left][...], right_all[g][:, pl.ds(at, tile)], preferred_element_type=f32
            ).astype(bf16)
            for group in range(16):
                bits = dict(zz=group >> 3 & 1, z=group >> 2 & 1, x=group >> 1 & 1, y=group & 1)
                place = tuple(bits[i] for i in ROUTES[order])
                sums[c][*place, :, pl.ds(to, tile)] = got[group * rows : (group + 1) * rows]
            return carry

        lax.fori_loop(0, wide // tile, turn, 0)
        go(stage_copy(c, 0))

    def advance(c, stage):
        stage_copy(c, stage).wait_recv()
        bits, _ = route(c)
        if stage == 3:
            g, rows, start, wide, _ = chunks[c]
            total = sums[c][bits].astype(f32) + landed[3][c][...].astype(f32)
            outs[g][:, start : start + wide] = total[: plan[g][3]]
            return
        for rest in range(1 << (3 - stage)):
            tail = tuple((rest >> k) & 1 for k in reversed(range(3 - stage)))
            at = bits[: stage + 1] + tail
            sums[c][at] = (sums[c][at].astype(f32) + landed[stage][c][tail].astype(f32)).astype(bf16)
        go(stage_copy(c, stage + 1))

    keep = {}

    def begin():
        for copy in loading:
            copy.wait()
        lower, linked, fresh, ending, unbroken = mask_set(flag_ref[...])
        z, u, oma, growth, inverse, tail = gate_set(have_ref["pre"][...], bias_ref[...], lower, ending)
        keep.update(lower=lower, linked=linked, fresh=fresh, z=z, u=u, oma=oma, growth=growth)
        keep.update(inverse=inverse, tail=tail, shrink=inverse * oma, kept=tail * oma)
        keep["gain"] = jnp.zeros((1, head), f32)

    def states(h, b):
        return state_ref.at[h * streams + b // per, b % per]

    def one_head(h):
        linked, fresh, growth, shrink = keep["linked"], keep["fresh"], keep["growth"], keep["shrink"]
        hs, hd = slice(h * slots, (h + 1) * slots), slice(h * head, (h + 1) * head)
        mixed, logits, delta = mixed_ref[:, hd], logit_ref[:, hd], mdelta_ref[:, hd]
        r = lax.rsqrt(jnp.mean(mixed * mixed, axis=1, keepdims=True) + norm_eps)
        sig = sigmoid(logits)
        silu = logits * sig
        unit = mixed * r
        dy = delta * silu
        right_all[4][0:n, hd] = (delta * unit * head_gain[...] * (sig + silu * (1.0 - sig))).astype(bf16)
        keep["gain"] = keep["gain"] + jnp.sum(dy * unit, axis=0, keepdims=True)
        dy = dy * head_gain[...]
        dmixed = r * (dy - unit * jnp.mean(unit * dy, axis=1, keepdims=True))
        gr, sh = growth[:, hs], shrink[:, hs].astype(bf16)
        weigh, inner = have_ref["weights"][:, hs], have_ref["inner"][:, hs]
        aff, mixing = have_ref["aff"][h], have_ref["mixing"][h]
        qh, kh, vh = q_ref[:, hd], k_ref[:, hd], v_ref[:, hd]
        do = dmixed.astype(bf16)
        lifted = (weigh * gr).astype(bf16)
        dm = (dot(do, vh, 1, 1) * linked).astype(bf16)
        mixed_ref[:, hd] = dot(mixing, do, 0, 0)
        fdo = (dmixed * fresh).astype(bf16)
        dlift = dot(dm, sh) + jnp.concatenate(
            [dot(fdo[rows_of(b)], states(h, b)[:, head:], 1, 1) for b in range(blocks)], axis=0
        )
        dsh = dot(dm, lifted, 0, 0)
        dw = dlift * gr
        dsc = weigh * (dw - jnp.sum(weigh * dw, axis=1, keepdims=True))
        du = dsc * gr
        du_low = du.astype(bf16)
        da = (dot(du_low, sh, 1, 1) * (linked * scale)).astype(bf16)
        dsh = dsh + dot(aff, du_low, 0, 0)
        fdu = (du * (fresh * scale)).astype(bf16)
        right_all[5][0:n, hd] = (
            dot(da, kh)
            + jnp.concatenate([dot(fdu[rows_of(b)], states(h, b)[:, :head]) for b in range(blocks)], axis=0)
        ).astype(bf16)
        mdelta_ref[:, hd] = dot(da, qh, 0, 0)
        for stream in range(streams):
            pair = h * streams + stream
            total = None
            for b in reversed(range(stream * per, (stream + 1) * per)):
                at = pair * per + b % per
                own_k = dot(fdu[rows_of(b)], qh[rows_of(b)], 0, 0)
                own_v = dot(lifted[rows_of(b)], fdo[rows_of(b)], 0, 0)
                owed[at, :, :head] = own_k.astype(bf16)
                owed[at, :, head:] = own_v.astype(bf16)
                if total is not None:
                    factor = pass_ref[at][:, :1]
                    own_k, own_v = own_k + factor * total[0], own_v + factor * total[1]
                total = (own_k, own_v)
            at = slice(pair * slots, (pair + 1) * slots)
            going[at, :head] = total[0].astype(bf16)
            going[at, head:] = total[1].astype(bf16)
        da_acc[:, hs] = lifted.astype(f32) * dlift + du_low.astype(f32) * inner - dsh * sh.astype(f32)
        doma_acc[:, hs] = dsh * keep["inverse"][:, hs]

    def rows_for(place):
        return pl.ds(pl.multiple_of(place * share, 16), share)

    sources = [lax.rem(s + size - d, size) for d in range(1, size)]

    def first_hop():
        for d in range(1, size):
            to = others[d - 1]
            go(remote(going.at[rows_for(to[0])], gathered.at[s], (hop_send, hop_recv), (0, d - 1), to))
        gathered[s] = going[rows_for(s)]
        fetch_right(4)
        fetch_right(5)

    def second_hop():
        for d in range(1, size):
            part = gathered.at[sources[d - 1]]
            remote(part, part, (hop_send, hop_recv), (0, d - 1), sib).wait_recv()
        state = jnp.zeros((share, 2 * head), f32)
        for place in reversed(range(size)):
            prefix[place] = state.astype(bf16)
            state = have_ref["pass_all"][place][:, :1].astype(f32) * state + gathered[place].astype(f32)
        for d in range(1, size):
            to = others[d - 1]
            go(remote(prefix.at[to[0]], came.at[rows_for(s)], (hop_send, hop_recv), (1, d - 1), to))
        came[rows_for(s)] = prefix[s]

    def last_hop():
        for d in range(1, size):
            part = came.at[rows_for(sources[d - 1])]
            remote(part, part, (hop_send, hop_recv), (1, d - 1), sib).wait_recv()

    def end_head(h):
        kept, tail = keep["kept"], keep["tail"]
        row = lax.broadcasted_iota(jnp.int32, (BLOCK, 1), 0)
        hs, hd = slice(h * slots, (h + 1) * slots), slice(h * head, (h + 1) * head)
        for stream in range(streams):
            pair = h * streams + stream
            leaving = came[pair * slots : (pair + 1) * slots].astype(f32)
            for i in reversed(range(per)):
                at, rb = pair * per + i, rows_of(stream * per + i)
                low = leaving.astype(bf16)
                part = kept[rb, hs].astype(bf16)
                dkept = dot(k_ref[rb, hd], low[:, :head], 1, 1) + dot(v_ref[rb, hd], low[:, head:], 1, 1)
                right_all[6][rb, hd] = (mdelta_ref[rb, hd] + dot(part, low[:, :head])).astype(bf16)
                right_all[7][rb, hd] = (mixed_ref[rb, hd] + dot(part, low[:, head:])).astype(bf16)
                held = jnp.sum(low.astype(f32) * state_ref[pair, i + 1].astype(f32), axis=1, keepdims=True)
                da_acc[rb, hs] = (
                    da_acc[rb, hs] - dkept * part.astype(f32) + jnp.where(row == BLOCK - 1, to_row(held), 0.0)
                )
                doma_acc[rb, hs] = doma_acc[rb, hs] + dkept * tail[rb, hs]
                if i > 0:
                    leaving = owed[at].astype(f32) + pass_ref[at][:, :1] * leaving

    def end_gates():
        fetch_right(6)
        fetch_right(7)
        z, u = keep["z"], keep["u"]
        dg = dot(keep["lower"], da_acc[...], 0, 0, count=3) - doma_acc[...] * (1.0 - keep["oma"])
        sig = jnp.where(z >= 0.0, u / (1.0 + u), 1.0 / (1.0 + u))
        dpre = dg * sig * 0.125
        right_all[8][0:n] = dpre.astype(bf16)
        fetch_right(8)
        pltpu.make_async_copy(first_in, mdelta_ref, first_sem.at[0]).start()
        pltpu.make_async_copy(tokens_in, q_ref, first_sem.at[1]).start()
        vec_acc[0] = jnp.zeros(vec_acc.shape[1:], f32)
        vec_acc[0, 1:2, : dpre.shape[1]] = jnp.sum(dpre, axis=0, keepdims=True)
        vec_acc[0, 2:3, :head] = keep["gain"]
        vec_acc[0, 3:4, :] = postgain_ref[...]

    def strip_step(i):
        strip_copy(i).wait()
        w, at = strips[i]
        term = dot(right_all[(6, 7, 8, 5, 4)[w]][0:n, at : at + TILE], strip[i % STRIPS], 1, 1)
        logit_ref[...] = term if i == 0 else logit_ref[...] + term
        if i + STRIPS < len(strips):
            strip_copy(i + STRIPS).start()

    def end_norm():
        pltpu.make_async_copy(first_in, mdelta_ref, first_sem.at[0]).wait()
        pltpu.make_async_copy(tokens_in, q_ref, first_sem.at[1]).wait()
        inputs = q_ref[...].astype(f32)
        r = lax.rsqrt(jnp.mean(inputs * inputs, axis=1, keepdims=True) + norm_eps)
        unit = inputs * r
        delta = logit_ref[...]
        vec_acc[0, 0:1, :] = jnp.sum(delta * unit, axis=0, keepdims=True)
        delta = delta * pre_gain[...]
        input_grad[...] = (
            mdelta_ref[...] + r * (delta - unit * jnp.mean(unit * delta, axis=1, keepdims=True))
        ).astype(bf16)
        go(v_copy(0))

    def v_copy(i):
        return remote(vec_acc.at[i], vec_got.at[i], (v_send, v_recv), i, (sib, far, nx, nz, nzz)[i])

    def vector(i):
        v_copy(i).wait_recv()
        total = vec_acc[i] + vec_got[i]
        if i == 4:
            vec_out[...] = total
            return
        vec_acc[i + 1] = total
        go(v_copy(i + 1))

    steps = {"begin": begin}
    path = [("begin", 2.0, None, None, 0)]
    for h in range(heads):
        steps["head", h] = functools.partial(one_head, h)
        path.append((("head", h), 3.0, None, None, 0))
    steps.update({"first hop": first_hop, "second hop": second_hop, "last hop": last_hop})
    path.append(("first hop", 0.5, None, "first", 12.0))
    path.append(("second hop", 1.0, "first", "second", 12.0))
    path.append(("last hop", 0.1, "second", None, 0))
    for h in range(heads):
        steps["end", h] = functools.partial(end_head, h)
        path.append((("end", h), 1.2, None, None, 0))
    steps["gates"] = end_gates
    path.append(("gates", 1.0, None, None, 0))
    for i in range(len(strips)):
        steps["strip", i] = functools.partial(strip_step, i)
        path.append((("strip", i), 0.4, None, None, 0))
    steps["norm"] = end_norm
    path.append(("norm", 1.5, None, ("vector", 0), 3.0))
    for i in range(5):
        steps["vector", i] = functools.partial(vector, i)
        path.append((("vector", i), 0.1, ("vector", i), ("vector", i + 1), 4.0))
    held_back = {4: "first hop", 5: "first hop", 6: "gates", 7: "gates", 8: "gates"}
    for what, which, stage in in_order(chunks, path, held_back, LEAST, SHALLOW, DEEP):
        if what == "path":
            steps[which]()
        elif what == "produce":
            produce(which)
        else:
            advance(which, stage)
    for copy in started:
        copy.wait_send()


def back(size, heads, plan, lefts, rights, saved, weights, first, tokens, bias, flags, head_gain, pre_gain, postgain):
    n, width = saved["q"].shape
    head, slots = width // heads, bias.shape[1] // heads
    pairs, per = heads * 2, n // BLOCK // 2
    share = pairs * slots // size
    chunks = [(p[2],) + c for p in plan for c in p[4]]
    nc = len(chunks)
    dma = pltpu.SemaphoreType.DMA
    saved = [saved[name] for name in SAVED]
    scratch = [VMEM((a.shape[-2], 2 * n), bf16) for a in lefts]
    scratch += [VMEM((2 * n, p[1]), bf16) for p in plan]
    scratch += [VMEM(a.shape, a.dtype) for a in saved]
    for lead in ((2, 2, 2, 2), (2, 2, 2), (2, 2), (2,), ()):
        scratch += [VMEM(lead + (r, w), bf16) for r, _, w, _ in chunks]
    scratch += [
        VMEM((pairs * per, slots, 2 * head), bf16),
        VMEM((n, heads * slots), f32),
        VMEM((n, heads * slots), f32),
        VMEM((STRIPS, width, TILE), bf16),
        VMEM((pairs * slots, 2 * head), bf16),
        VMEM((size, share, 2 * head), bf16),
        VMEM((size, share, 2 * head), bf16),
        VMEM((pairs * slots, 2 * head), bf16),
        VMEM((5, 8, width), f32),
        VMEM((5, 8, width), f32),
        dma((len(SAVED),)),
        dma((8,)),
        dma((13,)),
        dma((13,)),
        dma((STRIPS,)),
        dma((2,)),
        dma((2, size - 1)),
        dma((2, size - 1)),
        dma((4, nc)),
        dma((4, nc)),
        dma((5,)),
        dma((5,)),
    ]
    out = pl.pallas_call(
        functools.partial(back_kernel, size, heads, plan),
        name="back",
        out_shape=[jax.ShapeDtypeStruct((p[3], p[1]), f32) for p in plan]
        + [jax.ShapeDtypeStruct((8, width), f32), jax.ShapeDtypeStruct((n, width), bf16)],
        in_specs=[in_place()] * (8 + len(saved) + 7) + [in_vmem()] * 5,
        out_specs=[in_vmem()] * (len(plan) + 2),
        scratch_shapes=scratch,
        compiler_params=pltpu.CompilerParams(
            collective_id=2, has_side_effects=True, vmem_limit_bytes=BACK_LIMIT
        ),
    )(*lefts, *rights, *saved, *weights, first, tokens, bias, flags, head_gain, pre_gain, postgain)
    return out[: len(plan)], out[-2], out[-1]


def finish_kernel(count, *refs):
    vectors, outs = refs[count], refs[count + 1 :]
    for i in range(count):
        outs[i][...] = refs[i][...]
    for i, out in enumerate(outs[count:]):
        out[...] = vectors[i, : out.shape[0]]


def finish(arrays, vectors, sizes):
    count = len(arrays)
    return pl.pallas_call(
        functools.partial(finish_kernel, count),
        name="finish",
        out_shape=[jax.ShapeDtypeStruct(a.shape, a.dtype) for a in arrays]
        + [jax.ShapeDtypeStruct((size,), f32) for size in sizes],
        in_specs=[in_vmem()] * (count + 1),
        out_specs=[in_vmem()] * (count + len(sizes)),
        compiler_params=pltpu.CompilerParams(vmem_limit_bytes=LIMIT),
    )(*arrays, vectors)


def by_owner(a, hi, lo):
    features, tokens = a.shape
    r = features // (hi * lo * 4)
    t = a.reshape(hi, lo, 2, 2, r, tokens).transpose(3, 1, 2, 0, 4, 5).reshape(2, lo * 2, hi * r, tokens)
    pad = -(hi * r) % 16
    if pad:
        t = jnp.pad(t, ((0, 0), (0, 0), (0, pad), (0, 0)))
    return t.reshape(2, -1, tokens)


def body(
    size, tokens, resets, pre_gain, query_weight, key_weight, value_weight, forget_weight, forget_bias,
    outgate_weight, output_weight, head_gain, post_gain, gate_weight, up_weight, down_weight, cotangent,
):
    lo = 8
    hi = size // lo
    streams, length, width = tokens.shape
    n = streams * length
    head = head_gain.shape[0]
    heads = width // head
    shards = {
        "query": query_weight, "key": key_weight, "value": value_weight, "forget": forget_weight,
        "outgate": outgate_weight, "output": output_weight, "gate": gate_weight, "up": up_weight, "down": down_weight,
    }
    ff = gate_weight.shape[1]
    flat, cotan = tokens.reshape(n, width), cotangent.reshape(n, width)
    bias, gain = forget_bias[None], head_gain[None]
    (
        block_output, first_delta, attn_delta, merged_delta, postgain_grad,
        normed_t, merged_t, second_t, hidden_t, gate_delta, up_delta,
        q, k, v, pre, logits, mixed, aff, mixing, weights, inner, state, passed, pass_all, *wholes,
    ) = front(
        size, heads, hi == 1, shards, flat, cotan, pre_gain[None], post_gain[None],
        gain, bias, resets,
    )
    lefts = [hidden_t, second_t, merged_t, normed_t]
    if hi > 1:
        lefts = [by_owner(a, hi, lo) for a in lefts]
    rights = [cotan, gate_delta, up_delta, attn_delta]
    columns = (width, ff, ff, width, width, width, width, width, bias.shape[1])
    kept_rows = [(ff if i == 0 else width) // (lo * 4) for i in range(len(FORM))]
    padded = [-(-r // 16) * 16 for r in kept_rows]
    pieces = cut(tuple(zip(columns, padded)))
    plan = [(left, columns[i], padded[i], kept_rows[i], pieces[i]) for i, (_, left) in enumerate(FORM)]
    saved = dict(
        q=q, k=k, v=v, pre=pre, logits=logits, mixed=mixed, aff=aff, mixing=mixing, weights=weights, inner=inner,
        state=state, mdelta=merged_delta, pass_all=pass_all,
    )
    saved["pass"] = passed
    grads, vectors, input_grad = back(
        size, heads, tuple(plan), lefts, rights, saved, wholes, first_delta, flat, bias, resets, gain,
        pre_gain[None], postgain_grad,
    )
    if hi > 1:
        alike = [[a * lo + b for a in range(hi)] for b in range(lo)]
        grads = [
            lax.psum_scatter(g, "seq", scatter_dimension=0, axis_index_groups=alike, tiled=True)
            for g in grads
        ]
        vectors = lax.psum(vectors, "seq", axis_index_groups=alike)
    down_grad, gate_grad, up_grad, output_grad, outgate_grad, query_grad, key_grad, value_grad, forget_grad = grads
    shape = tokens.shape
    got = finish(
        (
            block_output, input_grad, query_grad, key_grad, value_grad, forget_grad, outgate_grad, output_grad,
            gate_grad, up_grad, down_grad,
        ), vectors, (width, bias.shape[1], head, width),
    )
    pregain, bias_total, headgain, postgain = got[11:]
    return (
        got[0].reshape(shape), got[1].reshape(shape), pregain, *got[2:6], bias_total, *got[6:8], headgain,
        postgain, *got[8:11],
    )


def solution(mesh):
    rows, whole, both = P("fsdp", None), P(), P(("seq", "fsdp"), None)
    return jax.shard_map(
        functools.partial(body, mesh.shape["seq"]),
        mesh=mesh,
        in_specs=(
            P("fsdp", "seq", None), P("fsdp", "seq"), whole, rows, rows, rows, rows, whole, rows, rows,
            whole, whole, rows, rows, rows, P("fsdp", "seq", None),
        ),
        out_specs=(
            P("fsdp", "seq", None), P("fsdp", "seq", None), whole, both, both, both, both, whole, both,
            both, whole, whole, both, both, both,
        ),
        check_vma=False,
    )
```

```python
import functools

import jax
import jax.numpy as jnp
from jax import lax
from jax.experimental import pallas as pl
from jax.experimental.pallas import tpu as pltpu
from jax.sharding import PartitionSpec as P

BLOCK = 64
TILE = 256
norm_eps = 1e-06
f32, bf16 = jnp.float32, jnp.bfloat16
MESH = pl.DeviceIdType.MESH
VMEM = pltpu.VMEM
ANY = pl.ANY
LIMIT = 60 * 2**20


def in_vmem():
    return pl.BlockSpec(memory_space=VMEM)


def in_place():
    return pl.BlockSpec(memory_space=ANY)


def greet(partners):
    barrier = pltpu.get_barrier_semaphore()
    for partner in partners:
        pl.semaphore_signal(barrier, inc=1, device_id=partner, device_id_type=MESH)
    pl.semaphore_wait(barrier, len(partners))


def remote(src, dst, sems, index, partner):
    return pltpu.make_async_remote_copy(
        src_ref=src,
        dst_ref=dst,
        send_sem=sems[0].at[index],
        recv_sem=sems[1].at[index],
        device_id=partner,
        device_id_type=MESH,
    )


def parts_of(a, count):
    if a.dtype == bf16:
        return [a]
    out = []
    for i in range(count):
        part = a.astype(bf16)
        out.append(part)
        if i + 1 < count:
            a = a - part.astype(f32)
    return out


def dot(a, b, ca=1, cb=0, count=1):
    total = None
    for right in reversed(parts_of(b, count)):
        term = lax.dot_general(
            a.astype(bf16), right, (((ca,), (cb,)), ((), ())), preferred_element_type=f32
        )
        total = term if total is None else total + term
    return total


def to_col(row):
    n = row.shape[1]
    i = lax.broadcasted_iota(jnp.int32, (n, n), 0)
    j = lax.broadcasted_iota(jnp.int32, (n, n), 1)
    return jnp.sum(jnp.where(i == j, jnp.broadcast_to(row, (n, n)), 0.0), axis=1, keepdims=True)


def mask_set(flags):
    row = jnp.concatenate([flags[i : i + 1].astype(f32) for i in range(flags.shape[0])], axis=1)
    n = row.shape[1]
    flags_row = jnp.broadcast_to(row, (8, n))
    i = lax.broadcasted_iota(jnp.int32, (n, n), 0)
    j = lax.broadcasted_iota(jnp.int32, (n, n), 1)
    same = (i // BLOCK) == (j // BLOCK)
    lower = jnp.where(same & (i >= j), 1.0, 0.0)
    block = jnp.where(same, 1.0, 0.0)
    seen_col = dot(lower, flags_row, 1, 1)[:, :1]
    all_col = dot(block, flags_row, 1, 1)[:, :1]
    seen_row = dot(flags_row, lower, 1, 1)[:1, :]
    linked = jnp.where(seen_col == seen_row, lower, 0.0)
    fresh = jnp.where(seen_col == 0.0, 1.0, 0.0)
    ending = jnp.where(seen_col == all_col, 1.0, 0.0)
    unbroken = jnp.where(all_col == 0.0, 1.0, 0.0)
    return lower, linked, fresh, ending, unbroken


def gate_set(pre, bias, lower, ending):
    z = pre + bias
    u = jnp.exp(-jnp.abs(z))
    lp = jnp.where(
        u < 0.02, u * (1.0 - u * (0.5 - u * (1.0 / 3.0 - 0.25 * u))), jnp.log(1.0 + u)
    )
    g = (jnp.minimum(z, 0.0) - lp) * 0.125
    series = 1.0 + g * (1.0 / 7.0)
    for order in (6, 5, 4, 3, 2):
        series = 1.0 + g * (1.0 / order) * series
    oma = jnp.where(g > -0.35, -g * series, 1.0 - jnp.exp(g))
    a = dot(lower, g, count=3)
    n, lanes = a.shape
    last = jnp.concatenate(
        [
            jnp.broadcast_to(a[b * BLOCK + BLOCK - 1 : b * BLOCK + BLOCK], (BLOCK, lanes))
            for b in range(n // BLOCK)
        ],
        axis=0,
    )
    tail = jnp.exp(last - a) * ending
    return z, u, oma, jnp.exp(a), jnp.exp(-a), tail


def rows_of(b):
    return slice(b * BLOCK, (b + 1) * BLOCK)


def passing(growth, unbroken, b, hs):
    last = b * BLOCK + BLOCK - 1
    return to_col(growth[last : last + 1, hs] * unbroken[last : last + 1])


def sigmoid(v):
    return 1.0 / (1.0 + jnp.exp(-v))


WEIGHTS = ("key", "value", "forget", "query", "outgate", "output", "gate", "up", "down")
TWICE = ("output", "gate", "up", "down", "rest")
PARTS = WEIGHTS + ("rest",)


RESULTS, SHARED = 24, (5, 6, 7, 8)


def front_kernel(size, heads, grouped, *refs):
    count = len(WEIGHTS)
    shards, refs = dict(zip(WEIGHTS, refs[:count])), refs[count:]
    (tok_ref, cot_ref, pre_gain, post_gain, head_gain, bias_ref, flag_ref), refs = refs[:7], refs[7:]
    results, refs = refs[:RESULTS], refs[RESULTS:]
    passed, refs = dict(zip(WEIGHTS[:5], refs[:5])), refs[5:]
    held, refs = refs[:RESULTS], refs[RESULTS:]
    (
        out_ref, first_ref, attn_ref, mdelta_ref, postgain_grad,
        normed_t, merged_t, second_t, hidden_t, gate_delta, up_delta,
        q_ref, k_ref, v_ref, pre_ref, logit_ref,
        mixed_ref, aff_ref, mixing_ref, weight_ref, inner_ref, state_ref, pass_ref, pass_all,
    ) = held
    whole, refs = dict(zip(WEIGHTS, refs[:count])), refs[count:]
    (
        normed, merged, one_ref, second, block_acc, delta_acc, flat_t,
        ends, going, gathered, prefix, came,
        local, send_sem, recv_sem, away, st_send, st_recv, out_sem, share_send, share_recv,
    ) = refs
    sems = (send_sem, recv_sem)
    s, f = lax.axis_index("seq"), lax.axis_index("fsdp")
    q = lax.rem(s, 4)
    kind_bit = lax.rem(q + q // 2, 2)
    sib, far, nx, nz = (s, f ^ 1), (s, f ^ 2), (s ^ 1, f), (s ^ 2, f)
    fy, fs = f ^ 2, f ^ 3
    others = [(lax.rem(s + d, size), f) for d in range(1, size)]
    greet([sib, far] + others)
    started = []

    def go(copy):
        copy.start()
        started.append(copy)

    leaving = []

    def emit(*sources):
        n = tok_ref.shape[0]
        for source in sources:
            i = next(k for k, ref in enumerate(held) if ref is source)
            to = results[i]
            if grouped and i in SHARED:
                far_half = to.at[:, pl.ds(n, n)]
                core = lax.rem(f, 2)
                j = SHARED.index(i)
                copy = remote(source.at[1 - core], far_half, (share_send, share_recv), j, sib)
                copy.start()
                leaving.append(copy)
                source, to = source.at[core], to.at[:, pl.ds(0, n)]
            copy = pltpu.make_async_copy(source, to, out_sem.at[i])
            copy.start()
            leaving.append(copy)

    spot = {m: (m, 0, shards[m].shape[0]) for m in WEIGHTS}
    rows = shards["down"].shape[0]
    lead = rows // 2 // 64 * 64
    spot["down"], spot["rest"] = ("down", 0, lead), ("down", lead, rows - lead)

    def piece(m, owner, start, length):
        name, first, _ = spot[m]
        rows = shards[name].shape[0]
        return whole[name].at[pl.ds(pl.multiple_of(owner * rows + first + start, 16), length)]

    def quarter(m, owner, which, half=None):
        rows = spot[m][2] // 4
        first = (rows // 2 + 15) // 16 * 16
        start, length = (0, rows) if half is None else ((0, first), (first, rows - first))[half]
        return piece(m, owner, which * rows + start, length)

    def eighth(m, owner, bit, half):
        rows = spot[m][2] // 2
        return piece(m, owner, bit * rows + half * (rows // 2), rows // 2)

    def mine(m, owner):
        if m in TWICE:
            rows = spot[m][2] // 2
            return piece(m, owner, kind_bit * rows, rows)
        return quarter(m, owner, q)

    def from_x(m, owner):
        return eighth(m, owner, 1 - kind_bit, 0) if m in TWICE else quarter(m, owner, q ^ 1)

    def from_z(m, owner):
        return eighth(m, owner, 1 - kind_bit, 1) if m in TWICE else quarter(m, owner, q ^ 2)

    def send(kind, m, part, partner):
        go(remote(part, part, sems, (kind, PARTS.index(m)), partner))

    def arrived(kind, m, part):
        remote(part, part, sems, (kind, PARTS.index(m)), sib).wait_recv()

    for i, m in enumerate(PARTS):
        name, first, rows = spot[m]
        if m in TWICE:
            src = shards[name].at[pl.ds(pl.multiple_of(first + kind_bit * (rows // 2), 16), rows // 2)]
        else:
            src = shards[name].at[pl.ds(pl.multiple_of(first + q * (rows // 4), 16), rows // 4)]
        go(remote(src, mine(m, f), sems, (1, i), far))

    def own_rows(m, owner):
        rows = shards[m].shape[0]
        return whole[m].at[pl.ds(pl.multiple_of(owner * rows, 16), rows)]

    own = {}
    for i, m in enumerate(WEIGHTS):
        go(remote(shards[m], own_rows(m, f), sems, (0, i), sib))
        own[m] = pltpu.make_async_copy(shards[m], own_rows(m, f), local.at[i])
        own[m].start()

    def pass_first(m):
        part = mine(m, fy)
        arrived(1, m, part)
        if m in TWICE:
            send(2, m, eighth(m, fy, kind_bit, 0), nx)
            send(3, m, eighth(m, fy, kind_bit, 1), nz)
        else:
            send(2, m, part, nx)
            send(3, m, part, nz)
        send(6, m, part, sib)

    def pass_second(m):
        arrived(2, m, from_x(m, fy))
        if m not in TWICE:
            send(4, m, quarter(m, fy, q ^ 1, 0), nz)
        send(7, m, from_x(m, fy), sib)
        arrived(3, m, from_z(m, fy))
        if m not in TWICE:
            send(5, m, quarter(m, fy, q ^ 2, 1), nx)
        send(8, m, from_z(m, fy), sib)

    def pass_third(m):
        if m not in TWICE:
            for kind in (4, 5):
                part = quarter(m, fy, q ^ 3, kind - 4)
                arrived(kind, m, part)
                send(kind + 5, m, part, sib)

    def pump(step):
        for late, stage in enumerate((pass_first, pass_second, pass_third)):
            if 0 <= step - late < len(PARTS):
                stage(PARTS[step - late])

    def ready(m):
        own[m].wait()
        arrived(0, m, own_rows(m, f ^ 1))
        for part in ("down", "rest") if m == "down" else (m,):
            arrived(6, part, mine(part, fs))
            arrived(7, part, from_x(part, fs))
            arrived(8, part, from_z(part, fs))
            if part not in TWICE:
                arrived(9, part, quarter(part, fs, q ^ 3, 0))
                arrived(10, part, quarter(part, fs, q ^ 3, 1))

    n, width = tok_ref.shape
    head = width // heads
    slots = bias_ref.shape[1] // heads
    blocks = n // BLOCK
    streams = 2
    per = blocks // streams
    pairs = heads * streams
    scale = head ** (-0.5)

    def across(columns, step):
        def turn(i, carry):
            step(pl.ds(pl.multiple_of(i * TILE, TILE), TILE))
            return carry

        lax.fori_loop(0, columns // TILE, turn, 0)

    def project(m, to_ref):
        def step(at):
            to_ref[:, at] = dot(normed[...], whole[m][:, at]).astype(to_ref.dtype)

        across(whole[m].shape[1], step)

    def turn_over(source, to_ref, rows, padded):
        if not grouped:
            to_ref[...] = source[...].astype(bf16)
            return
        for group in range(16):
            for core in range(2):
                at = (group * 2 + core) * rows
                to_ref[core, group * padded : group * padded + rows] = source[at : at + rows].astype(bf16)

    inputs = tok_ref[...].astype(f32)
    unit = inputs * lax.rsqrt(jnp.mean(inputs * inputs, axis=1, keepdims=True) + norm_eps)
    scaled = unit * pre_gain[...]
    normed[...] = scaled.astype(bf16)
    turn_over(scaled.T, normed_t, width // 32, width // 32)
    emit(normed_t)
    for step in range(5):
        pump(step)
    for m, to_ref in (("key", k_ref), ("value", v_ref), ("forget", pre_ref)):
        ready(m)
        project(m, to_ref)
    emit(k_ref, v_ref, pre_ref)
    lower, linked, fresh, ending, unbroken = mask_set(flag_ref[...])
    z, u, oma, growth, inverse, tail = gate_set(pre_ref[...], bias_ref[...], lower, ending)
    shrink, kept = inverse * oma, tail * oma
    for h in range(heads):
        hs, hd = slice(h * slots, (h + 1) * slots), slice(h * head, (h + 1) * head)
        for stream in range(streams):
            pair = h * streams + stream
            total, through = None, None
            for b in range(stream * per, (stream + 1) * per):
                part = kept[rows_of(b), hs].astype(bf16)
                at = pair * per + b % per
                end_k = dot(part, k_ref[rows_of(b), hd], 0, 0)
                end_v = dot(part, v_ref[rows_of(b), hd], 0, 0)
                ends[at, :, :head] = end_k
                ends[at, :, head:] = end_v
                factor = passing(growth, unbroken, b, hs)
                pass_ref[at] = jnp.broadcast_to(factor, pass_ref.shape[1:])
                if total is None:
                    total, through = (end_k, end_v), factor
                else:
                    total = (factor * total[0] + end_k, factor * total[1] + end_v)
                    through = through * factor
            at = slice(pair * slots, (pair + 1) * slots)
            going[at, :head] = total[0].astype(bf16)
            going[at, head : 2 * head] = total[1].astype(bf16)
            going[at, 2 * head :] = jnp.broadcast_to(through, (slots, going.shape[1] - 2 * head)).astype(bf16)

    share = pairs * slots // size

    def rows_for(place):
        return pl.ds(pl.multiple_of(place * share, 16), share)

    first_hop, second_hop = [], []
    for d in range(1, size):
        to = others[d - 1]
        copy = remote(going.at[rows_for(to[0])], gathered.at[s], (st_send, st_recv), (0, d - 1), to)
        go(copy)
        first_hop.append(lax.rem(s + size - d, size))
    gathered[s] = going[rows_for(s)]
    pump(5)
    pump(6)
    for m, to_ref in (("query", q_ref), ("outgate", logit_ref)):
        ready(m)
        project(m, to_ref)
    emit(q_ref, logit_ref, pass_ref)
    for i, m in enumerate(WEIGHTS[:5]):
        copy = pltpu.make_async_copy(whole[m], passed[m], away.at[i])
        copy.start()
        own[m] = copy
    for d in range(1, size):
        source = first_hop[d - 1]
        remote(gathered.at[source], gathered.at[source], (st_send, st_recv), (0, d - 1), sib).wait_recv()
    state = jnp.zeros((share, 2 * head), f32)
    for place in range(size):
        prefix[place] = state.astype(bf16)
        entry = gathered[place].astype(f32)
        pass_all[place] = gathered[place][:, 2 * head :]
        state = entry[:, 2 * head : 2 * head + 1] * state + entry[:, : 2 * head]
    for d in range(1, size):
        to = others[d - 1]
        go(remote(prefix.at[to[0]], came.at[rows_for(s)], (st_send, st_recv), (1, d - 1), to))
    came[rows_for(s)] = prefix[s]
    emit(pass_all)
    pump(7)
    for h in range(heads):
        hd = slice(h * head, (h + 1) * head)
        aff_ref[h] = (dot(q_ref[:, hd], k_ref[:, hd], 1, 1) * (linked * scale)).astype(bf16)
    emit(aff_ref)
    for d in range(1, size):
        part = came.at[rows_for(first_hop[d - 1])]
        remote(part, part, (st_send, st_recv), (1, d - 1), sib).wait_recv()
    for h in range(heads):
        hs, hd = slice(h * slots, (h + 1) * slots), slice(h * head, (h + 1) * head)
        for stream in range(streams):
            pair = h * streams + stream
            state = came[pair * slots : (pair + 1) * slots].astype(f32)
            for b in range(per):
                at = pair * per + b
                state_ref[pair, b] = state.astype(bf16)
                state = pass_ref[at][:, :1] * state + ends[at]
            state_ref[pair, per] = state.astype(bf16)
        gr, sh = growth[:, hs], shrink[:, hs]
        qh, vh = q_ref[:, hd], v_ref[:, hd]
        carried = jnp.concatenate(
            [
                dot(qh[rows_of(b)], state_ref[h * streams + b // per, b % per, :, :head], 1, 1)
                for b in range(blocks)
            ],
            axis=0,
        )
        inner = dot(aff_ref[h], sh) + carried * (scale * fresh)
        scores = gr * inner
        e = jnp.exp(scores - jnp.max(scores, axis=1, keepdims=True))
        weights = e / jnp.sum(e, axis=1, keepdims=True)
        weight_ref[:, hs] = weights
        inner_ref[:, hs] = inner
        lifted = weights * gr
        mixing = (dot(lifted, sh.astype(bf16), 1, 1) * linked).astype(bf16)
        mixing_ref[h] = mixing
        brought = jnp.concatenate(
            [
                dot(lifted[rows_of(b)], state_ref[h * streams + b // per, b % per, :, head:])
                for b in range(blocks)
            ],
            axis=0,
        )
        mixed = dot(mixing, vh) + brought * fresh
        mixed_ref[:, hd] = mixed
        r = lax.rsqrt(jnp.mean(mixed * mixed, axis=1, keepdims=True) + norm_eps)
        logits = logit_ref[:, hd]
        delta_acc[:, hd] = mixed * r * head_gain[...] * (logits * sigmoid(logits))
        merged[:, hd] = delta_acc[:, hd].astype(bf16)
    emit(mixed_ref, mixing_ref, weight_ref, inner_ref, state_ref)
    pass_first("down")
    pass_second("up")
    ready("output")

    def join(at):
        one_ref[:, at] = tok_ref[:, at].astype(f32) + dot(merged[...], whole["output"][:, at])

    across(width, join)
    turn_over(delta_acc[...].T, merged_t, width // 32, width // 32)
    emit(merged_t)
    one = one_ref[...]
    scaled = one * lax.rsqrt(jnp.mean(one * one, axis=1, keepdims=True) + norm_eps) * post_gain[...]
    second[...] = scaled.astype(bf16)
    turn_over(scaled.T, second_t, width // 32, width // 32)
    emit(second_t)
    pass_first("rest")
    ready("gate")
    ready("up")
    block_acc[...] = one
    delta_acc[...] = jnp.zeros_like(delta_acc)

    def open_tile(i, carry):
        at = pl.ds(pl.multiple_of(i * TILE, TILE), TILE)
        gate_vals, up_vals = dot(second[...], whole["gate"][:, at]), dot(second[...], whole["up"][:, at])
        sig = sigmoid(gate_vals)
        silu = gate_vals * sig
        flat_t[at] = (silu * up_vals).T
        up_delta[:, at] = silu.astype(bf16)
        gate_delta[:, at] = (up_vals * (sig + silu * (1.0 - sig))).astype(bf16)
        return carry

    def unit_tile(i, carry):
        at = pl.ds(pl.multiple_of(i * TILE, TILE), TILE)
        w_gate, w_up, w_down = whole["gate"][:, at], whole["up"][:, at], whole["down"][at]
        hidden_delta = dot(cot_ref[...], w_down, 1, 1)
        d_up = (hidden_delta * up_delta[:, at].astype(f32)).astype(bf16)
        d_gate = (hidden_delta * gate_delta[:, at].astype(f32)).astype(bf16)
        gate_delta[:, at] = d_gate
        up_delta[:, at] = d_up
        block_acc[...] += dot(flat_t[at].astype(bf16), w_down, 0, 0)
        delta_acc[...] += dot(d_gate, w_gate, 1, 1) + dot(d_up, w_up, 1, 1)
        return carry

    ff = whole["gate"].shape[1]
    lax.fori_loop(0, ff // TILE, open_tile, 0)
    turn_over(flat_t, hidden_t, ff // 32, -(-(ff // 32) // 16) * 16)
    emit(hidden_t)
    pass_second("down")
    pass_second("rest")
    ready("down")
    lax.fori_loop(0, ff // TILE, unit_tile, 0)
    out_ref[...] = block_acc[...].astype(bf16)
    emit(out_ref, gate_delta, up_delta)
    one = one_ref[...]
    r = lax.rsqrt(jnp.mean(one * one, axis=1, keepdims=True) + norm_eps)
    unit = one * r
    delta = delta_acc[...]
    postgain_grad[...] = jnp.sum(delta * unit, axis=0, keepdims=True)
    delta = delta * post_gain[...]
    first = cot_ref[...].astype(f32) + r * (delta - unit * jnp.mean(unit * delta, axis=1, keepdims=True))
    first_ref[...] = first
    attn_ref[...] = first.astype(bf16)
    emit(postgain_grad, first_ref, attn_ref)

    def split(at):
        mdelta_ref[:, at] = dot(attn_ref[...], whole["output"][at], 1, 1)

    across(width, split)
    emit(mdelta_ref)
    for copy in leaving:
        copy.wait()
    for m in WEIGHTS[:5]:
        own[m].wait()
    for copy in started:
        copy.wait_send()


def front(size, heads, grouped, shards, tokens, cotan, pre_gain, post_gain, head_gain, bias, flags):
    n, width = tokens.shape
    head, slots = width // heads, bias.shape[1] // heads
    pairs, per = heads * 2, n // BLOCK // 2
    ff = shards["gate"].shape[1]
    shards = [shards[m] for m in WEIGHTS]
    count = len(shards)
    padded = -(-(ff // 32) // 16) * 512

    def turned(rows, grouped_rows):
        return low(grouped_rows // 2, 2 * n) if grouped else low(rows, n)

    def low(*shape):
        return jax.ShapeDtypeStruct(shape, bf16)

    def full(*shape):
        return jax.ShapeDtypeStruct(shape, f32)

    outs = [
        low(n, width), full(n, width), low(n, width), full(n, width), full(1, width),
        turned(width, width), turned(width, width), turned(width, width), turned(ff, padded),
        low(n, ff), low(n, ff),
        low(n, width), low(n, width), low(n, width), full(n, heads * slots), full(n, width),
        full(n, width), low(heads, n, n), low(heads, n, n), full(n, heads * slots), full(n, heads * slots),
        low(pairs, per + 1, slots, 2 * head), full(pairs * per, slots, 128),
        low(size, pairs * slots // size, 128),
    ]
    wholes = [low(4 * w.shape[0], w.shape[1]) for w in shards]
    keeps = [
        (2, o.shape[0], n) if grouped and i in SHARED else o.shape for i, o in enumerate(outs)
    ]
    share = pairs * slots // size
    dma = pltpu.SemaphoreType.DMA
    got = pl.pallas_call(
        functools.partial(front_kernel, size, heads, grouped),
        name="front",
        out_shape=outs + wholes[:5],
        in_specs=[in_place()] * count + [in_vmem()] * 7,
        out_specs=[in_place()] * (len(outs) + 5),
        scratch_shapes=[VMEM(shape, o.dtype) for shape, o in zip(keeps, outs)]
        + [VMEM(w.shape, bf16) for w in wholes]
        + [
            VMEM((n, width), bf16),
            VMEM((n, width), bf16),
            VMEM((n, width), f32),
            VMEM((n, width), bf16),
            VMEM((n, width), f32),
            VMEM((n, width), f32),
            VMEM((ff, n), f32),
            VMEM((pairs * per, slots, 2 * head), f32),
            VMEM((pairs * slots, 2 * head + 128), bf16),
            VMEM((size, share, 2 * head + 128), bf16),
            VMEM((size, share, 2 * head), bf16),
            VMEM((pairs * slots, 2 * head), bf16),
            dma((count,)),
            dma((11, len(PARTS))),
            dma((11, len(PARTS))),
            dma((5,)),
            dma((2, size - 1)),
            dma((2, size - 1)),
            dma((RESULTS,)),
            dma((len(SHARED),)),
            dma((len(SHARED),)),
        ],
        compiler_params=pltpu.CompilerParams(
            collective_id=1, has_side_effects=True, vmem_limit_bytes=LIMIT
        ),
    )(*shards, tokens, cotan, pre_gain, post_gain, head_gain, bias, flags)
    return got


def to_row(col):
    n = col.shape[0]
    i = lax.broadcasted_iota(jnp.int32, (n, n), 0)
    j = lax.broadcasted_iota(jnp.int32, (n, n), 1)
    return jnp.sum(jnp.where(i == j, jnp.broadcast_to(col, (n, n)), 0.0), axis=0, keepdims=True)


LEAST, SHALLOW, DEEP = 4.0, 8.0, 12.0
STRIPS = 3
BACK_LIMIT = 63 * 2**20


ROUTES = (("y", "z", "x", "zz"), ("x", "z", "y", "zz"), ("y", "x", "z", "zz"), ("x", "y", "z", "zz"))
STATES = {"x": 1.15, "y": 0.0, "z": 1.75}


def cut(sizes):
    load, plan, last = dict(STATES), [], 1
    for columns, rows in sizes:
        tiles = columns // TILE
        pieces = min(4, 2 * tiles) if tiles <= 4 else 6
        width = columns // pieces if tiles <= 1 else TILE
        out, start = [], 0
        for i in range(pieces):
            count = 1 if tiles <= 1 else tiles // pieces + (1 if i < tiles % pieces else 0)
            size = 2 * 16 * rows * width * count * 2 / 1e6

            def after(route):
                new = dict(load)
                for stage, link in enumerate(ROUTES[route]):
                    new["z" if link == "zz" else link] += size / 2 ** (stage + 1)
                return new

            route = min((1 - last, 3 - last), key=lambda r: sum(v**4 for v in after(r).values()))
            load, last = after(route), route % 2
            out.append((start, width * count, route))
            start += width * count
        plan.append(tuple(out))
    return plan


def in_order(chunks, path, held_back, least, shallow, deep):
    now, free = 0.0, dict.fromkeys(("x", "y", "z", "zz"), 0.0)
    came, done, coming, out = {}, set(), [], []
    path, left = list(path), list(range(len(chunks)))
    rate, delay = 0.04, 4.0

    def leave(c, stage):
        rows, width, order = chunks[c][1], chunks[c][3], chunks[c][4]
        link = ROUTES[order][stage]
        size = 16 * rows * width * 2 / 1e6 / 2 ** (stage + 1)
        free[link] = max(now, free[link]) + size / rate * (2 if stage == 3 else 1)
        coming.append((free[link] + delay, c, stage))

    while left or path or coming:
        here = sorted(a for a in coming if a[0] <= now)
        open_ = [c for c in left if held_back.get(chunks[c][0], None) in done or chunks[c][0] not in held_back]
        depth = deep if "second hop" in done else shallow
        queue = free[ROUTES[chunks[open_[0]][4]][0]] - now if open_ else 0.0
        ready = path and came.get(path[0][2], 0.0 if path[0][2] is None else 1e9) <= now
        if here:
            _, c, stage = here[0]
            coming.remove(here[0])
            now += 0.1 + 0.1 * chunks[c][1] / 32 * chunks[c][3] / TILE / 2**stage
            out.append(("advance", c, stage))
            if stage < 3:
                leave(c, stage + 1)
        elif ready and not (open_ and queue < least):
            name, time, _, starts, takes = path.pop(0)
            now += time
            done.add(name)
            out.append(("path", name, None))
            if starts:
                came[starts] = now + takes
        elif open_ and queue < depth:
            c = open_[0]
            left.remove(c)
            now += 0.1 + 0.3 * chunks[c][1] / 32 * chunks[c][3] / TILE
            out.append(("produce", c, None))
            leave(c, 0)
        else:
            later = [a[0] for a in coming]
            if path and path[0][2] in came:
                later.append(came[path[0][2]])
            if open_:
                later.append(now + queue - depth)
            now = max(now + 0.05, min(later))
    return out


FORM = (("cotan", 0), ("gate", 1), ("up", 1), ("attn", 2), ("outgate", 3), ("query", 3), ("key", 3), ("value", 3), ("forget", 3))
SAVED = ("q", "k", "v", "pre", "logits", "mixed", "aff", "mixing", "weights", "inner", "state", "pass", "mdelta", "pass_all")


def back_kernel(size, heads, plan, *refs):
    def take(count):
        nonlocal refs
        got, refs = refs[:count], refs[count:]
        return got

    lefts, rights, saved = take(4), take(4), dict(zip(SAVED, take(len(SAVED))))
    weights, (first_in, tokens_in) = take(5), take(2)
    bias_ref, flag_ref, head_gain, pre_gain, postgain_ref = take(5)
    outs, (vec_out, input_grad) = take(9), take(2)
    left_all, right_all = take(4), take(9)
    have_ref = dict(zip(SAVED, take(len(SAVED))))
    chunks = [(g, p[2]) + c for g, p in enumerate(plan) for c in p[4]]
    nc = len(chunks)
    sums = take(nc)
    landed = [take(nc) for _ in range(4)]
    owed, da_acc, doma_acc, strip, going, gathered, prefix, came, vec_acc, vec_got = take(10)
    loads, in_local, in_send, in_recv, strip_sem, first_sem = take(6)
    hop_send, hop_recv, st_send, st_recv, v_send, v_recv = take(6)
    q_ref, k_ref, v_ref = have_ref["q"], have_ref["k"], have_ref["v"]
    logit_ref, mixed_ref, mdelta_ref = have_ref["logits"], have_ref["mixed"], have_ref["mdelta"]
    state_ref, pass_ref = have_ref["state"], have_ref["pass"]

    s, f = lax.axis_index("seq"), lax.axis_index("fsdp")
    core, y = lax.rem(f, 2), f // 2
    x, z_low, z_high = lax.rem(s, 2), lax.rem(s // 2, 2), lax.rem(s // 4, 2)
    sib, far, nx, nz, nzz = (s, f ^ 1), (s, f ^ 2), (s ^ 1, f), (s ^ 2, f), (s ^ 4, f)
    others = [(lax.rem(s + d, size), f) for d in range(1, size)]
    greet([sib, far] + others)
    started = []

    def go(copy):
        copy.start()
        started.append(copy)

    n, width = q_ref.shape
    head = width // heads
    slots = bias_ref.shape[1] // heads
    blocks = n // BLOCK
    streams = 2
    per = blocks // streams
    pairs = heads * streams
    scale = head ** (-0.5)
    share = pairs * slots // size

    waiting = {}

    def fetch_left(i):
        if len(lefts[i].shape) == 2:
            keep = pltpu.make_async_copy(lefts[i], left_all[i], in_local.at[i])
            keep.start()
            waiting["left", i] = [keep, None]
            return
        keep = pltpu.make_async_copy(lefts[i].at[core], left_all[i].at[:, pl.ds(0, n)], in_local.at[i])
        keep.start()
        copy = remote(lefts[i].at[1 - core], left_all[i].at[:, pl.ds(n, n)], (in_send, in_recv), i, sib)
        go(copy)
        waiting["left", i] = [keep, copy]

    def fetch_right(i):
        own, other = right_all[i].at[pl.ds(0, n)], right_all[i].at[pl.ds(n, n)]
        keep = None
        src = own
        if i < 4:
            src = rights[i]
            keep = pltpu.make_async_copy(src, own, in_local.at[4 + i])
            keep.start()
        copy = remote(src, other, (in_send, in_recv), 4 + i, sib)
        go(copy)
        waiting["right", i] = [keep, copy]

    def have(kind, i):
        pair = waiting[kind, i]
        if pair:
            if pair[0] is not None:
                pair[0].wait()
            if pair[1] is not None:
                pair[1].wait_recv()
            waiting[kind, i] = None

    fetch_left(0)
    fetch_right(0)
    loading = []
    for i, name in enumerate(SAVED):
        copy = pltpu.make_async_copy(saved[name], have_ref[name], loads.at[i])
        copy.start()
        loading.append(copy)
    for i in (1, 2, 3):
        fetch_right(i)
    for i in (1, 2, 3):
        fetch_left(i)

    strips = [(w, t * TILE) for w in range(5) for t in range(weights[w].shape[1] // TILE)]

    def strip_copy(i):
        w, at = strips[i]
        return pltpu.make_async_copy(weights[w].at[:, pl.ds(at, TILE)], strip.at[i % STRIPS], strip_sem.at[i % STRIPS])

    for i in range(STRIPS):
        strip_copy(i).start()

    def route(c):
        names = ROUTES[chunks[c][4]]
        places, partners = dict(x=x, y=y, z=z_low, zz=z_high), dict(x=nx, y=far, z=nz, zz=nzz)
        return tuple(places[i] for i in names), tuple(partners[i] for i in names)

    def stage_copy(c, stage):
        bits, partners = route(c)
        at = bits[:stage] + (1 - bits[stage],)
        return remote(sums[c].at[at], landed[stage][c], (st_send, st_recv), (stage, c), partners[stage])

    def produce(c):
        g, rows, start, wide, order = chunks[c]
        left = plan[g][0]
        have("left", left)
        have("right", g)
        tile = min(TILE, wide)

        def turn(i, carry):
            at = pl.multiple_of(start + i * tile, 128)
            to = pl.multiple_of(i * tile, 128)
            got = jnp.dot(
                left_all[left][...], right_all[g][:, pl.ds(at, tile)], preferred_element_type=f32
            ).astype(bf16)
            for group in range(16):
                bits = dict(zz=group >> 3 & 1, z=group >> 2 & 1, x=group >> 1 & 1, y=group & 1)
                place = tuple(bits[i] for i in ROUTES[order])
                sums[c][*place, :, pl.ds(to, tile)] = got[group * rows : (group + 1) * rows]
            return carry

        lax.fori_loop(0, wide // tile, turn, 0)
        go(stage_copy(c, 0))

    def advance(c, stage):
        stage_copy(c, stage).wait_recv()
        bits, _ = route(c)
        if stage == 3:
            g, rows, start, wide, _ = chunks[c]
            total = sums[c][bits].astype(f32) + landed[3][c][...].astype(f32)
            outs[g][:, start : start + wide] = total[: plan[g][3]]
            return
        for rest in range(1 << (3 - stage)):
            tail = tuple((rest >> k) & 1 for k in reversed(range(3 - stage)))
            at = bits[: stage + 1] + tail
            sums[c][at] = (sums[c][at].astype(f32) + landed[stage][c][tail].astype(f32)).astype(bf16)
        go(stage_copy(c, stage + 1))

    keep = {}

    def begin():
        for copy in loading:
            copy.wait()
        lower, linked, fresh, ending, unbroken = mask_set(flag_ref[...])
        z, u, oma, growth, inverse, tail = gate_set(have_ref["pre"][...], bias_ref[...], lower, ending)
        keep.update(lower=lower, linked=linked, fresh=fresh, z=z, u=u, oma=oma, growth=growth)
        keep.update(inverse=inverse, tail=tail, shrink=inverse * oma, kept=tail * oma)
        keep["gain"] = jnp.zeros((1, head), f32)

    def states(h, b):
        return state_ref.at[h * streams + b // per, b % per]

    def one_head(h):
        linked, fresh, growth, shrink = keep["linked"], keep["fresh"], keep["growth"], keep["shrink"]
        hs, hd = slice(h * slots, (h + 1) * slots), slice(h * head, (h + 1) * head)
        mixed, logits, delta = mixed_ref[:, hd], logit_ref[:, hd], mdelta_ref[:, hd]
        r = lax.rsqrt(jnp.mean(mixed * mixed, axis=1, keepdims=True) + norm_eps)
        sig = sigmoid(logits)
        silu = logits * sig
        unit = mixed * r
        dy = delta * silu
        right_all[4][0:n, hd] = (delta * unit * head_gain[...] * (sig + silu * (1.0 - sig))).astype(bf16)
        keep["gain"] = keep["gain"] + jnp.sum(dy * unit, axis=0, keepdims=True)
        dy = dy * head_gain[...]
        dmixed = r * (dy - unit * jnp.mean(unit * dy, axis=1, keepdims=True))
        gr, sh = growth[:, hs], shrink[:, hs].astype(bf16)
        weigh, inner = have_ref["weights"][:, hs], have_ref["inner"][:, hs]
        aff, mixing = have_ref["aff"][h], have_ref["mixing"][h]
        qh, kh, vh = q_ref[:, hd], k_ref[:, hd], v_ref[:, hd]
        do = dmixed.astype(bf16)
        lifted = (weigh * gr).astype(bf16)
        dm = (dot(do, vh, 1, 1) * linked).astype(bf16)
        mixed_ref[:, hd] = dot(mixing, do, 0, 0)
        fdo = (dmixed * fresh).astype(bf16)
        dlift = dot(dm, sh) + jnp.concatenate(
            [dot(fdo[rows_of(b)], states(h, b)[:, head:], 1, 1) for b in range(blocks)], axis=0
        )
        dsh = dot(dm, lifted, 0, 0)
        dw = dlift * gr
        dsc = weigh * (dw - jnp.sum(weigh * dw, axis=1, keepdims=True))
        du = dsc * gr
        du_low = du.astype(bf16)
        da = (dot(du_low, sh, 1, 1) * (linked * scale)).astype(bf16)
        dsh = dsh + dot(aff, du_low, 0, 0)
        fdu = (du * (fresh * scale)).astype(bf16)
        right_all[5][0:n, hd] = (
            dot(da, kh)
            + jnp.concatenate([dot(fdu[rows_of(b)], states(h, b)[:, :head]) for b in range(blocks)], axis=0)
        ).astype(bf16)
        mdelta_ref[:, hd] = dot(da, qh, 0, 0)
        for stream in range(streams):
            pair = h * streams + stream
            total = None
            for b in reversed(range(stream * per, (stream + 1) * per)):
                at = pair * per + b % per
                own_k = dot(fdu[rows_of(b)], qh[rows_of(b)], 0, 0)
                own_v = dot(lifted[rows_of(b)], fdo[rows_of(b)], 0, 0)
                owed[at, :, :head] = own_k.astype(bf16)
                owed[at, :, head:] = own_v.astype(bf16)
                if total is not None:
                    factor = pass_ref[at][:, :1]
                    own_k, own_v = own_k + factor * total[0], own_v + factor * total[1]
                total = (own_k, own_v)
            at = slice(pair * slots, (pair + 1) * slots)
            going[at, :head] = total[0].astype(bf16)
            going[at, head:] = total[1].astype(bf16)
        da_acc[:, hs] = lifted.astype(f32) * dlift + du_low.astype(f32) * inner - dsh * sh.astype(f32)
        doma_acc[:, hs] = dsh * keep["inverse"][:, hs]

    def rows_for(place):
        return pl.ds(pl.multiple_of(place * share, 16), share)

    sources = [lax.rem(s + size - d, size) for d in range(1, size)]

    def first_hop():
        for d in range(1, size):
            to = others[d - 1]
            go(remote(going.at[rows_for(to[0])], gathered.at[s], (hop_send, hop_recv), (0, d - 1), to))
        gathered[s] = going[rows_for(s)]
        fetch_right(4)
        fetch_right(5)

    def second_hop():
        for d in range(1, size):
            part = gathered.at[sources[d - 1]]
            remote(part, part, (hop_send, hop_recv), (0, d - 1), sib).wait_recv()
        state = jnp.zeros((share, 2 * head), f32)
        for place in reversed(range(size)):
            prefix[place] = state.astype(bf16)
            state = have_ref["pass_all"][place][:, :1].astype(f32) * state + gathered[place].astype(f32)
        for d in range(1, size):
            to = others[d - 1]
            go(remote(prefix.at[to[0]], came.at[rows_for(s)], (hop_send, hop_recv), (1, d - 1), to))
        came[rows_for(s)] = prefix[s]

    def last_hop():
        for d in range(1, size):
            part = came.at[rows_for(sources[d - 1])]
            remote(part, part, (hop_send, hop_recv), (1, d - 1), sib).wait_recv()

    def end_head(h):
        kept, tail = keep["kept"], keep["tail"]
        row = lax.broadcasted_iota(jnp.int32, (BLOCK, 1), 0)
        hs, hd = slice(h * slots, (h + 1) * slots), slice(h * head, (h + 1) * head)
        for stream in range(streams):
            pair = h * streams + stream
            leaving = came[pair * slots : (pair + 1) * slots].astype(f32)
            for i in reversed(range(per)):
                at, rb = pair * per + i, rows_of(stream * per + i)
                low = leaving.astype(bf16)
                part = kept[rb, hs].astype(bf16)
                dkept = dot(k_ref[rb, hd], low[:, :head], 1, 1) + dot(v_ref[rb, hd], low[:, head:], 1, 1)
                right_all[6][rb, hd] = (mdelta_ref[rb, hd] + dot(part, low[:, :head])).astype(bf16)
                right_all[7][rb, hd] = (mixed_ref[rb, hd] + dot(part, low[:, head:])).astype(bf16)
                held = jnp.sum(low.astype(f32) * state_ref[pair, i + 1].astype(f32), axis=1, keepdims=True)
                da_acc[rb, hs] = (
                    da_acc[rb, hs] - dkept * part.astype(f32) + jnp.where(row == BLOCK - 1, to_row(held), 0.0)
                )
                doma_acc[rb, hs] = doma_acc[rb, hs] + dkept * tail[rb, hs]
                if i > 0:
                    leaving = owed[at].astype(f32) + pass_ref[at][:, :1] * leaving

    def end_gates():
        fetch_right(6)
        fetch_right(7)
        z, u = keep["z"], keep["u"]
        dg = dot(keep["lower"], da_acc[...], 0, 0, count=3) - doma_acc[...] * (1.0 - keep["oma"])
        sig = jnp.where(z >= 0.0, u / (1.0 + u), 1.0 / (1.0 + u))
        dpre = dg * sig * 0.125
        right_all[8][0:n] = dpre.astype(bf16)
        fetch_right(8)
        pltpu.make_async_copy(first_in, mdelta_ref, first_sem.at[0]).start()
        pltpu.make_async_copy(tokens_in, q_ref, first_sem.at[1]).start()
        vec_acc[0] = jnp.zeros(vec_acc.shape[1:], f32)
        vec_acc[0, 1:2, : dpre.shape[1]] = jnp.sum(dpre, axis=0, keepdims=True)
        vec_acc[0, 2:3, :head] = keep["gain"]
        vec_acc[0, 3:4, :] = postgain_ref[...]

    def strip_step(i):
        strip_copy(i).wait()
        w, at = strips[i]
        term = dot(right_all[(6, 7, 8, 5, 4)[w]][0:n, at : at + TILE], strip[i % STRIPS], 1, 1)
        logit_ref[...] = term if i == 0 else logit_ref[...] + term
        if i + STRIPS < len(strips):
            strip_copy(i + STRIPS).start()

    def end_norm():
        pltpu.make_async_copy(first_in, mdelta_ref, first_sem.at[0]).wait()
        pltpu.make_async_copy(tokens_in, q_ref, first_sem.at[1]).wait()
        inputs = q_ref[...].astype(f32)
        r = lax.rsqrt(jnp.mean(inputs * inputs, axis=1, keepdims=True) + norm_eps)
        unit = inputs * r
        delta = logit_ref[...]
        vec_acc[0, 0:1, :] = jnp.sum(delta * unit, axis=0, keepdims=True)
        delta = delta * pre_gain[...]
        input_grad[...] = (
            mdelta_ref[...] + r * (delta - unit * jnp.mean(unit * delta, axis=1, keepdims=True))
        ).astype(bf16)
        go(v_copy(0))

    def v_copy(i):
        return remote(vec_acc.at[i], vec_got.at[i], (v_send, v_recv), i, (sib, far, nx, nz, nzz)[i])

    def vector(i):
        v_copy(i).wait_recv()
        total = vec_acc[i] + vec_got[i]
        if i == 4:
            vec_out[...] = total
            return
        vec_acc[i + 1] = total
        go(v_copy(i + 1))

    steps = {"begin": begin}
    path = [("begin", 2.0, None, None, 0)]
    for h in range(heads):
        steps["head", h] = functools.partial(one_head, h)
        path.append((("head", h), 3.0, None, None, 0))
    steps.update({"first hop": first_hop, "second hop": second_hop, "last hop": last_hop})
    path.append(("first hop", 0.5, None, "first", 12.0))
    path.append(("second hop", 1.0, "first", "second", 12.0))
    path.append(("last hop", 0.1, "second", None, 0))
    for h in range(heads):
        steps["end", h] = functools.partial(end_head, h)
        path.append((("end", h), 1.2, None, None, 0))
    steps["gates"] = end_gates
    path.append(("gates", 1.0, None, None, 0))
    for i in range(len(strips)):
        steps["strip", i] = functools.partial(strip_step, i)
        path.append((("strip", i), 0.4, None, None, 0))
    steps["norm"] = end_norm
    path.append(("norm", 1.5, None, ("vector", 0), 3.0))
    for i in range(5):
        steps["vector", i] = functools.partial(vector, i)
        path.append((("vector", i), 0.1, ("vector", i), ("vector", i + 1), 4.0))
    held_back = {4: "first hop", 5: "first hop", 6: "gates", 7: "gates", 8: "gates"}
    for what, which, stage in in_order(chunks, path, held_back, LEAST, SHALLOW, DEEP):
        if what == "path":
            steps[which]()
        elif what == "produce":
            produce(which)
        else:
            advance(which, stage)
    for copy in started:
        copy.wait_send()


def back(size, heads, plan, lefts, rights, saved, weights, first, tokens, bias, flags, head_gain, pre_gain, postgain):
    n, width = saved["q"].shape
    head, slots = width // heads, bias.shape[1] // heads
    pairs, per = heads * 2, n // BLOCK // 2
    share = pairs * slots // size
    chunks = [(p[2],) + c for p in plan for c in p[4]]
    nc = len(chunks)
    dma = pltpu.SemaphoreType.DMA
    saved = [saved[name] for name in SAVED]
    scratch = [VMEM((a.shape[-2], 2 * n), bf16) for a in lefts]
    scratch += [VMEM((2 * n, p[1]), bf16) for p in plan]
    scratch += [VMEM(a.shape, a.dtype) for a in saved]
    for lead in ((2, 2, 2, 2), (2, 2, 2), (2, 2), (2,), ()):
        scratch += [VMEM(lead + (r, w), bf16) for r, _, w, _ in chunks]
    scratch += [
        VMEM((pairs * per, slots, 2 * head), bf16),
        VMEM((n, heads * slots), f32),
        VMEM((n, heads * slots), f32),
        VMEM((STRIPS, width, TILE), bf16),
        VMEM((pairs * slots, 2 * head), bf16),
        VMEM((size, share, 2 * head), bf16),
        VMEM((size, share, 2 * head), bf16),
        VMEM((pairs * slots, 2 * head), bf16),
        VMEM((5, 8, width), f32),
        VMEM((5, 8, width), f32),
        dma((len(SAVED),)),
        dma((8,)),
        dma((13,)),
        dma((13,)),
        dma((STRIPS,)),
        dma((2,)),
        dma((2, size - 1)),
        dma((2, size - 1)),
        dma((4, nc)),
        dma((4, nc)),
        dma((5,)),
        dma((5,)),
    ]
    out = pl.pallas_call(
        functools.partial(back_kernel, size, heads, plan),
        name="back",
        out_shape=[jax.ShapeDtypeStruct((p[3], p[1]), f32) for p in plan]
        + [jax.ShapeDtypeStruct((8, width), f32), jax.ShapeDtypeStruct((n, width), bf16)],
        in_specs=[in_place()] * (8 + len(saved) + 7) + [in_vmem()] * 5,
        out_specs=[in_vmem()] * (len(plan) + 2),
        scratch_shapes=scratch,
        compiler_params=pltpu.CompilerParams(
            collective_id=2, has_side_effects=True, vmem_limit_bytes=BACK_LIMIT
        ),
    )(*lefts, *rights, *saved, *weights, first, tokens, bias, flags, head_gain, pre_gain, postgain)
    return out[: len(plan)], out[-2], out[-1]


def finish_kernel(count, *refs):
    vectors, outs = refs[count], refs[count + 1 :]
    for i in range(count):
        outs[i][...] = refs[i][...]
    for i, out in enumerate(outs[count:]):
        out[...] = vectors[i, : out.shape[0]]


def finish(arrays, vectors, sizes):
    count = len(arrays)
    return pl.pallas_call(
        functools.partial(finish_kernel, count),
        name="finish",
        out_shape=[jax.ShapeDtypeStruct(a.shape, a.dtype) for a in arrays]
        + [jax.ShapeDtypeStruct((size,), f32) for size in sizes],
        in_specs=[in_vmem()] * (count + 1),
        out_specs=[in_vmem()] * (count + len(sizes)),
        compiler_params=pltpu.CompilerParams(vmem_limit_bytes=LIMIT),
    )(*arrays, vectors)


def by_owner(a, hi, lo):
    features, tokens = a.shape
    r = features // (hi * lo * 4)
    t = a.reshape(hi, lo, 2, 2, r, tokens).transpose(3, 1, 2, 0, 4, 5).reshape(2, lo * 2, hi * r, tokens)
    pad = -(hi * r) % 16
    if pad:
        t = jnp.pad(t, ((0, 0), (0, 0), (0, pad), (0, 0)))
    return t.reshape(2, -1, tokens)


def body(
    size, tokens, resets, pre_gain, query_weight, key_weight, value_weight, forget_weight, forget_bias,
    outgate_weight, output_weight, head_gain, post_gain, gate_weight, up_weight, down_weight, cotangent,
):
    lo = 8
    hi = size // lo
    streams, length, width = tokens.shape
    n = streams * length
    head = head_gain.shape[0]
    heads = width // head
    shards = {
        "query": query_weight, "key": key_weight, "value": value_weight, "forget": forget_weight,
        "outgate": outgate_weight, "output": output_weight, "gate": gate_weight, "up": up_weight, "down": down_weight,
    }
    ff = gate_weight.shape[1]
    flat, cotan = tokens.reshape(n, width), cotangent.reshape(n, width)
    bias, gain = forget_bias[None], head_gain[None]
    (
        block_output, first_delta, attn_delta, merged_delta, postgain_grad,
        normed_t, merged_t, second_t, hidden_t, gate_delta, up_delta,
        q, k, v, pre, logits, mixed, aff, mixing, weights, inner, state, passed, pass_all, *wholes,
    ) = front(
        size, heads, hi == 1, shards, flat, cotan, pre_gain[None], post_gain[None],
        gain, bias, resets,
    )
    lefts = [hidden_t, second_t, merged_t, normed_t]
    if hi > 1:
        lefts = [by_owner(a, hi, lo) for a in lefts]
    rights = [cotan, gate_delta, up_delta, attn_delta]
    columns = (width, ff, ff, width, width, width, width, width, bias.shape[1])
    kept_rows = [(ff if i == 0 else width) // (lo * 4) for i in range(len(FORM))]
    padded = [-(-r // 16) * 16 for r in kept_rows]
    pieces = cut(tuple(zip(columns, padded)))
    plan = [(left, columns[i], padded[i], kept_rows[i], pieces[i]) for i, (_, left) in enumerate(FORM)]
    saved = dict(
        q=q, k=k, v=v, pre=pre, logits=logits, mixed=mixed, aff=aff, mixing=mixing, weights=weights, inner=inner,
        state=state, mdelta=merged_delta, pass_all=pass_all,
    )
    saved["pass"] = passed
    grads, vectors, input_grad = back(
        size, heads, tuple(plan), lefts, rights, saved, wholes, first_delta, flat, bias, resets, gain,
        pre_gain[None], postgain_grad,
    )
    if hi > 1:
        alike = [[a * lo + b for a in range(hi)] for b in range(lo)]
        grads = [
            lax.psum_scatter(g, "seq", scatter_dimension=0, axis_index_groups=alike, tiled=True)
            for g in grads
        ]
        vectors = lax.psum(vectors, "seq", axis_index_groups=alike)
    down_grad, gate_grad, up_grad, output_grad, outgate_grad, query_grad, key_grad, value_grad, forget_grad = grads
    shape = tokens.shape
    got = finish(
        (
            block_output, input_grad, query_grad, key_grad, value_grad, forget_grad, outgate_grad, output_grad,
            gate_grad, up_grad, down_grad,
        ), vectors, (width, bias.shape[1], head, width),
    )
    pregain, bias_total, headgain, postgain = got[11:]
    return (
        got[0].reshape(shape), got[1].reshape(shape), pregain, *got[2:6], bias_total, *got[6:8], headgain,
        postgain, *got[8:11],
    )


def solution(mesh):
    rows, whole, both = P("fsdp", None), P(), P(("seq", "fsdp"), None)
    return jax.shard_map(
        functools.partial(body, mesh.shape["seq"]),
        mesh=mesh,
        in_specs=(
            P("fsdp", "seq", None), P("fsdp", "seq"), whole, rows, rows, rows, rows, whole, rows, rows,
            whole, whole, rows, rows, rows, P("fsdp", "seq", None),
        ),
        out_specs=(
            P("fsdp", "seq", None), P("fsdp", "seq", None), whole, both, both, both, both, whole, both,
            both, whole, whole, both, both, both,
        ),
        check_vma=False,
    )
```

```python
import functools

import jax
import jax.numpy as jnp
from jax import lax
from jax.experimental import pallas as pl
from jax.experimental.pallas import tpu as pltpu
from jax.sharding import PartitionSpec as P

BLOCK = 64
TILE = 256
norm_eps = 1e-06
f32, bf16 = jnp.float32, jnp.bfloat16
MESH = pl.DeviceIdType.MESH
VMEM = pltpu.VMEM
ANY = pl.ANY
LIMIT = 60 * 2**20


def in_vmem():
    return pl.BlockSpec(memory_space=VMEM)


def in_place():
    return pl.BlockSpec(memory_space=ANY)


def greet(partners):
    barrier = pltpu.get_barrier_semaphore()
    for partner in partners:
        pl.semaphore_signal(barrier, inc=1, device_id=partner, device_id_type=MESH)
    pl.semaphore_wait(barrier, len(partners))


def remote(src, dst, sems, index, partner):
    return pltpu.make_async_remote_copy(
        src_ref=src,
        dst_ref=dst,
        send_sem=sems[0].at[index],
        recv_sem=sems[1].at[index],
        device_id=partner,
        device_id_type=MESH,
    )


def parts_of(a, count):
    if a.dtype == bf16:
        return [a]
    out = []
    for i in range(count):
        part = a.astype(bf16)
        out.append(part)
        if i + 1 < count:
            a = a - part.astype(f32)
    return out


def dot(a, b, ca=1, cb=0, count=1):
    total = None
    for right in reversed(parts_of(b, count)):
        term = lax.dot_general(
            a.astype(bf16), right, (((ca,), (cb,)), ((), ())), preferred_element_type=f32
        )
        total = term if total is None else total + term
    return total


def to_col(row):
    n = row.shape[1]
    i = lax.broadcasted_iota(jnp.int32, (n, n), 0)
    j = lax.broadcasted_iota(jnp.int32, (n, n), 1)
    return jnp.sum(jnp.where(i == j, jnp.broadcast_to(row, (n, n)), 0.0), axis=1, keepdims=True)


def mask_set(flags):
    row = jnp.concatenate([flags[i : i + 1].astype(f32) for i in range(flags.shape[0])], axis=1)
    n = row.shape[1]
    flags_row = jnp.broadcast_to(row, (8, n))
    i = lax.broadcasted_iota(jnp.int32, (n, n), 0)
    j = lax.broadcasted_iota(jnp.int32, (n, n), 1)
    same = (i // BLOCK) == (j // BLOCK)
    lower = jnp.where(same & (i >= j), 1.0, 0.0)
    block = jnp.where(same, 1.0, 0.0)
    seen_col = dot(lower, flags_row, 1, 1)[:, :1]
    all_col = dot(block, flags_row, 1, 1)[:, :1]
    seen_row = dot(flags_row, lower, 1, 1)[:1, :]
    linked = jnp.where(seen_col == seen_row, lower, 0.0)
    fresh = jnp.where(seen_col == 0.0, 1.0, 0.0)
    ending = jnp.where(seen_col == all_col, 1.0, 0.0)
    unbroken = jnp.where(all_col == 0.0, 1.0, 0.0)
    return lower, linked, fresh, ending, unbroken


def gate_set(pre, bias, lower, ending):
    z = pre + bias
    u = jnp.exp(-jnp.abs(z))
    lp = jnp.where(
        u < 0.02, u * (1.0 - u * (0.5 - u * (1.0 / 3.0 - 0.25 * u))), jnp.log(1.0 + u)
    )
    g = (jnp.minimum(z, 0.0) - lp) * 0.125
    series = 1.0 + g * (1.0 / 7.0)
    for order in (6, 5, 4, 3, 2):
        series = 1.0 + g * (1.0 / order) * series
    oma = jnp.where(g > -0.35, -g * series, 1.0 - jnp.exp(g))
    a = dot(lower, g, count=3)
    n, lanes = a.shape
    last = jnp.concatenate(
        [
            jnp.broadcast_to(a[b * BLOCK + BLOCK - 1 : b * BLOCK + BLOCK], (BLOCK, lanes))
            for b in range(n // BLOCK)
        ],
        axis=0,
    )
    tail = jnp.exp(last - a) * ending
    return z, u, oma, jnp.exp(a), jnp.exp(-a), tail


def rows_of(b):
    return slice(b * BLOCK, (b + 1) * BLOCK)


def passing(growth, unbroken, b, hs):
    last = b * BLOCK + BLOCK - 1
    return to_col(growth[last : last + 1, hs] * unbroken[last : last + 1])


def sigmoid(v):
    return 1.0 / (1.0 + jnp.exp(-v))


WEIGHTS = ("key", "value", "forget", "query", "outgate", "output", "gate", "up", "down")
TWICE = ("output", "gate", "up", "down", "rest")
PARTS = WEIGHTS + ("rest",)


RESULTS, SHARED = 24, (5, 6, 7, 8)


def front_kernel(size, heads, grouped, *refs):
    count = len(WEIGHTS)
    shards, refs = dict(zip(WEIGHTS, refs[:count])), refs[count:]
    (tok_ref, cot_ref, pre_gain, post_gain, head_gain, bias_ref, flag_ref), refs = refs[:7], refs[7:]
    results, refs = refs[:RESULTS], refs[RESULTS:]
    passed, refs = dict(zip(WEIGHTS[:5], refs[:5])), refs[5:]
    held, refs = refs[:RESULTS], refs[RESULTS:]
    (
        out_ref, first_ref, attn_ref, mdelta_ref, postgain_grad,
        normed_t, merged_t, second_t, hidden_t, gate_delta, up_delta,
        q_ref, k_ref, v_ref, pre_ref, logit_ref,
        mixed_ref, aff_ref, mixing_ref, weight_ref, inner_ref, state_ref, pass_ref, pass_all,
    ) = held
    whole, refs = dict(zip(WEIGHTS, refs[:count])), refs[count:]
    (
        normed, merged, one_ref, second, block_acc, delta_acc, flat_t,
        ends, going, gathered, prefix, came,
        local, send_sem, recv_sem, away, st_send, st_recv, out_sem, share_send, share_recv,
    ) = refs
    sems = (send_sem, recv_sem)
    s, f = lax.axis_index("seq"), lax.axis_index("fsdp")
    q = lax.rem(s, 4)
    kind_bit = lax.rem(q + q // 2, 2)
    sib, far, nx, nz = (s, f ^ 1), (s, f ^ 2), (s ^ 1, f), (s ^ 2, f)
    fy, fs = f ^ 2, f ^ 3
    others = [(lax.rem(s + d, size), f) for d in range(1, size)]
    greet([sib, far] + others)
    started = []

    def go(copy):
        copy.start()
        started.append(copy)

    leaving = []

    def emit(*sources):
        n = tok_ref.shape[0]
        for source in sources:
            i = next(k for k, ref in enumerate(held) if ref is source)
            to = results[i]
            if grouped and i in SHARED:
                far_half = to.at[:, pl.ds(n, n)]
                core = lax.rem(f, 2)
                j = SHARED.index(i)
                copy = remote(source.at[1 - core], far_half, (share_send, share_recv), j, sib)
                copy.start()
                leaving.append(copy)
                source, to = source.at[core], to.at[:, pl.ds(0, n)]
            copy = pltpu.make_async_copy(source, to, out_sem.at[i])
            copy.start()
            leaving.append(copy)

    spot = {m: (m, 0, shards[m].shape[0]) for m in WEIGHTS}
    rows = shards["down"].shape[0]
    lead = rows // 2 // 64 * 64
    spot["down"], spot["rest"] = ("down", 0, lead), ("down", lead, rows - lead)

    def piece(m, owner, start, length):
        name, first, _ = spot[m]
        rows = shards[name].shape[0]
        return whole[name].at[pl.ds(pl.multiple_of(owner * rows + first + start, 16), length)]

    def quarter(m, owner, which, half=None):
        rows = spot[m][2] // 4
        first = (rows // 2 + 15) // 16 * 16
        start, length = (0, rows) if half is None else ((0, first), (first, rows - first))[half]
        return piece(m, owner, which * rows + start, length)

    def eighth(m, owner, bit, half):
        rows = spot[m][2] // 2
        return piece(m, owner, bit * rows + half * (rows // 2), rows // 2)

    def mine(m, owner):
        if m in TWICE:
            rows = spot[m][2] // 2
            return piece(m, owner, kind_bit * rows, rows)
        return quarter(m, owner, q)

    def from_x(m, owner):
        return eighth(m, owner, 1 - kind_bit, 0) if m in TWICE else quarter(m, owner, q ^ 1)

    def from_z(m, owner):
        return eighth(m, owner, 1 - kind_bit, 1) if m in TWICE else quarter(m, owner, q ^ 2)

    def send(kind, m, part, partner):
        go(remote(part, part, sems, (kind, PARTS.index(m)), partner))

    def arrived(kind, m, part):
        remote(part, part, sems, (kind, PARTS.index(m)), sib).wait_recv()

    for i, m in enumerate(PARTS):
        name, first, rows = spot[m]
        if m in TWICE:
            src = shards[name].at[pl.ds(pl.multiple_of(first + kind_bit * (rows // 2), 16), rows // 2)]
        else:
            src = shards[name].at[pl.ds(pl.multiple_of(first + q * (rows // 4), 16), rows // 4)]
        go(remote(src, mine(m, f), sems, (1, i), far))

    def own_rows(m, owner):
        rows = shards[m].shape[0]
        return whole[m].at[pl.ds(pl.multiple_of(owner * rows, 16), rows)]

    own = {}
    for i, m in enumerate(WEIGHTS):
        go(remote(shards[m], own_rows(m, f), sems, (0, i), sib))
        own[m] = pltpu.make_async_copy(shards[m], own_rows(m, f), local.at[i])
        own[m].start()

    def pass_first(m):
        part = mine(m, fy)
        arrived(1, m, part)
        if m in TWICE:
            send(2, m, eighth(m, fy, kind_bit, 0), nx)
            send(3, m, eighth(m, fy, kind_bit, 1), nz)
        else:
            send(2, m, part, nx)
            send(3, m, part, nz)
        send(6, m, part, sib)

    def pass_second(m):
        arrived(2, m, from_x(m, fy))
        if m not in TWICE:
            send(4, m, quarter(m, fy, q ^ 1, 0), nz)
        send(7, m, from_x(m, fy), sib)
        arrived(3, m, from_z(m, fy))
        if m not in TWICE:
            send(5, m, quarter(m, fy, q ^ 2, 1), nx)
        send(8, m, from_z(m, fy), sib)

    def pass_third(m):
        if m not in TWICE:
            for kind in (4, 5):
                part = quarter(m, fy, q ^ 3, kind - 4)
                arrived(kind, m, part)
                send(kind + 5, m, part, sib)

    def pump(step):
        for late, stage in enumerate((pass_first, pass_second, pass_third)):
            if 0 <= step - late < len(PARTS):
                stage(PARTS[step - late])

    def ready(m):
        own[m].wait()
        arrived(0, m, own_rows(m, f ^ 1))
        for part in ("down", "rest") if m == "down" else (m,):
            arrived(6, part, mine(part, fs))
            arrived(7, part, from_x(part, fs))
            arrived(8, part, from_z(part, fs))
            if part not in TWICE:
                arrived(9, part, quarter(part, fs, q ^ 3, 0))
                arrived(10, part, quarter(part, fs, q ^ 3, 1))

    n, width = tok_ref.shape
    head = width // heads
    slots = bias_ref.shape[1] // heads
    blocks = n // BLOCK
    streams = 2
    per = blocks // streams
    pairs = heads * streams
    scale = head ** (-0.5)

    def across(columns, step):
        def turn(i, carry):
            step(pl.ds(pl.multiple_of(i * TILE, TILE), TILE))
            return carry

        lax.fori_loop(0, columns // TILE, turn, 0)

    def project(m, to_ref):
        def step(at):
            to_ref[:, at] = dot(normed[...], whole[m][:, at]).astype(to_ref.dtype)

        across(whole[m].shape[1], step)

    def turn_over(source, to_ref, rows, padded):
        if not grouped:
            to_ref[...] = source[...].astype(bf16)
            return
        for group in range(16):
            for core in range(2):
                at = (group * 2 + core) * rows
                to_ref[core, group * padded : group * padded + rows] = source[at : at + rows].astype(bf16)

    inputs = tok_ref[...].astype(f32)
    unit = inputs * lax.rsqrt(jnp.mean(inputs * inputs, axis=1, keepdims=True) + norm_eps)
    scaled = unit * pre_gain[...]
    normed[...] = scaled.astype(bf16)
    turn_over(scaled.T, normed_t, width // 32, width // 32)
    emit(normed_t)
    for step in range(5):
        pump(step)
    for m, to_ref in (("key", k_ref), ("value", v_ref), ("forget", pre_ref)):
        ready(m)
        project(m, to_ref)
    emit(k_ref, v_ref, pre_ref)
    lower, linked, fresh, ending, unbroken = mask_set(flag_ref[...])
    z, u, oma, growth, inverse, tail = gate_set(pre_ref[...], bias_ref[...], lower, ending)
    shrink, kept = inverse * oma, tail * oma
    for h in range(heads):
        hs, hd = slice(h * slots, (h + 1) * slots), slice(h * head, (h + 1) * head)
        for stream in range(streams):
            pair = h * streams + stream
            total, through = None, None
            for b in range(stream * per, (stream + 1) * per):
                part = kept[rows_of(b), hs].astype(bf16)
                at = pair * per + b % per
                end_k = dot(part, k_ref[rows_of(b), hd], 0, 0)
                end_v = dot(part, v_ref[rows_of(b), hd], 0, 0)
                ends[at, :, :head] = end_k
                ends[at, :, head:] = end_v
                factor = passing(growth, unbroken, b, hs)
                pass_ref[at] = jnp.broadcast_to(factor, pass_ref.shape[1:])
                if total is None:
                    total, through = (end_k, end_v), factor
                else:
                    total = (factor * total[0] + end_k, factor * total[1] + end_v)
                    through = through * factor
            at = slice(pair * slots, (pair + 1) * slots)
            going[at, :head] = total[0].astype(bf16)
            going[at, head : 2 * head] = total[1].astype(bf16)
            going[at, 2 * head :] = jnp.broadcast_to(through, (slots, going.shape[1] - 2 * head)).astype(bf16)

    share = pairs * slots // size

    def rows_for(place):
        return pl.ds(pl.multiple_of(place * share, 16), share)

    first_hop, second_hop = [], []
    for d in range(1, size):
        to = others[d - 1]
        copy = remote(going.at[rows_for(to[0])], gathered.at[s], (st_send, st_recv), (0, d - 1), to)
        go(copy)
        first_hop.append(lax.rem(s + size - d, size))
    gathered[s] = going[rows_for(s)]
    pump(5)
    pump(6)
    for m, to_ref in (("query", q_ref), ("outgate", logit_ref)):
        ready(m)
        project(m, to_ref)
    emit(q_ref, logit_ref, pass_ref)
    for i, m in enumerate(WEIGHTS[:5]):
        copy = pltpu.make_async_copy(whole[m], passed[m], away.at[i])
        copy.start()
        own[m] = copy
    for d in range(1, size):
        source = first_hop[d - 1]
        remote(gathered.at[source], gathered.at[source], (st_send, st_recv), (0, d - 1), sib).wait_recv()
    state = jnp.zeros((share, 2 * head), f32)
    for place in range(size):
        prefix[place] = state.astype(bf16)
        entry = gathered[place].astype(f32)
        pass_all[place] = gathered[place][:, 2 * head :]
        state = entry[:, 2 * head : 2 * head + 1] * state + entry[:, : 2 * head]
    for d in range(1, size):
        to = others[d - 1]
        go(remote(prefix.at[to[0]], came.at[rows_for(s)], (st_send, st_recv), (1, d - 1), to))
    came[rows_for(s)] = prefix[s]
    emit(pass_all)
    pump(7)
    for h in range(heads):
        hd = slice(h * head, (h + 1) * head)
        aff_ref[h] = (dot(q_ref[:, hd], k_ref[:, hd], 1, 1) * (linked * scale)).astype(bf16)
    emit(aff_ref)
    for d in range(1, size):
        part = came.at[rows_for(first_hop[d - 1])]
        remote(part, part, (st_send, st_recv), (1, d - 1), sib).wait_recv()
    for h in range(heads):
        hs, hd = slice(h * slots, (h + 1) * slots), slice(h * head, (h + 1) * head)
        for stream in range(streams):
            pair = h * streams + stream
            state = came[pair * slots : (pair + 1) * slots].astype(f32)
            for b in range(per):
                at = pair * per + b
                state_ref[pair, b] = state.astype(bf16)
                state = pass_ref[at][:, :1] * state + ends[at]
            state_ref[pair, per] = state.astype(bf16)
        gr, sh = growth[:, hs], shrink[:, hs]
        qh, vh = q_ref[:, hd], v_ref[:, hd]
        carried = jnp.concatenate(
            [
                dot(qh[rows_of(b)], state_ref[h * streams + b // per, b % per, :, :head], 1, 1)
                for b in range(blocks)
            ],
            axis=0,
        )
        inner = dot(aff_ref[h], sh) + carried * (scale * fresh)
        scores = gr * inner
        e = jnp.exp(scores - jnp.max(scores, axis=1, keepdims=True))
        weights = e / jnp.sum(e, axis=1, keepdims=True)
        weight_ref[:, hs] = weights
        inner_ref[:, hs] = inner
        lifted = weights * gr
        mixing = (dot(lifted, sh.astype(bf16), 1, 1) * linked).astype(bf16)
        mixing_ref[h] = mixing
        brought = jnp.concatenate(
            [
                dot(lifted[rows_of(b)], state_ref[h * streams + b // per, b % per, :, head:])
                for b in range(blocks)
            ],
            axis=0,
        )
        mixed = dot(mixing, vh) + brought * fresh
        mixed_ref[:, hd] = mixed
        r = lax.rsqrt(jnp.mean(mixed * mixed, axis=1, keepdims=True) + norm_eps)
        logits = logit_ref[:, hd]
        delta_acc[:, hd] = mixed * r * head_gain[...] * (logits * sigmoid(logits))
        merged[:, hd] = delta_acc[:, hd].astype(bf16)
    emit(mixed_ref, mixing_ref, weight_ref, inner_ref, state_ref)
    pass_first("down")
    pass_second("up")
    ready("output")

    def join(at):
        one_ref[:, at] = tok_ref[:, at].astype(f32) + dot(merged[...], whole["output"][:, at])

    across(width, join)
    turn_over(delta_acc[...].T, merged_t, width // 32, width // 32)
    emit(merged_t)
    one = one_ref[...]
    scaled = one * lax.rsqrt(jnp.mean(one * one, axis=1, keepdims=True) + norm_eps) * post_gain[...]
    second[...] = scaled.astype(bf16)
    turn_over(scaled.T, second_t, width // 32, width // 32)
    emit(second_t)
    pass_first("rest")
    ready("gate")
    ready("up")
    block_acc[...] = one
    delta_acc[...] = jnp.zeros_like(delta_acc)

    def open_tile(i, carry):
        at = pl.ds(pl.multiple_of(i * TILE, TILE), TILE)
        gate_vals, up_vals = dot(second[...], whole["gate"][:, at]), dot(second[...], whole["up"][:, at])
        sig = sigmoid(gate_vals)
        silu = gate_vals * sig
        flat_t[at] = (silu * up_vals).T
        up_delta[:, at] = silu.astype(bf16)
        gate_delta[:, at] = (up_vals * (sig + silu * (1.0 - sig))).astype(bf16)
        return carry

    def unit_tile(i, carry):
        at = pl.ds(pl.multiple_of(i * TILE, TILE), TILE)
        w_gate, w_up, w_down = whole["gate"][:, at], whole["up"][:, at], whole["down"][at]
        hidden_delta = dot(cot_ref[...], w_down, 1, 1)
        d_up = (hidden_delta * up_delta[:, at].astype(f32)).astype(bf16)
        d_gate = (hidden_delta * gate_delta[:, at].astype(f32)).astype(bf16)
        gate_delta[:, at] = d_gate
        up_delta[:, at] = d_up
        block_acc[...] += dot(flat_t[at].astype(bf16), w_down, 0, 0)
        delta_acc[...] += dot(d_gate, w_gate, 1, 1) + dot(d_up, w_up, 1, 1)
        return carry

    ff = whole["gate"].shape[1]
    lax.fori_loop(0, ff // TILE, open_tile, 0)
    turn_over(flat_t, hidden_t, ff // 32, -(-(ff // 32) // 16) * 16)
    emit(hidden_t)
    pass_second("down")
    pass_second("rest")
    ready("down")
    lax.fori_loop(0, ff // TILE, unit_tile, 0)
    out_ref[...] = block_acc[...].astype(bf16)
    emit(out_ref, gate_delta, up_delta)
    one = one_ref[...]
    r = lax.rsqrt(jnp.mean(one * one, axis=1, keepdims=True) + norm_eps)
    unit = one * r
    delta = delta_acc[...]
    postgain_grad[...] = jnp.sum(delta * unit, axis=0, keepdims=True)
    delta = delta * post_gain[...]
    first = cot_ref[...].astype(f32) + r * (delta - unit * jnp.mean(unit * delta, axis=1, keepdims=True))
    first_ref[...] = first
    attn_ref[...] = first.astype(bf16)
    emit(postgain_grad, first_ref, attn_ref)

    def split(at):
        mdelta_ref[:, at] = dot(attn_ref[...], whole["output"][at], 1, 1)

    across(width, split)
    emit(mdelta_ref)
    for copy in leaving:
        copy.wait()
    for m in WEIGHTS[:5]:
        own[m].wait()
    for copy in started:
        copy.wait_send()


def front(size, heads, grouped, shards, tokens, cotan, pre_gain, post_gain, head_gain, bias, flags):
    n, width = tokens.shape
    head, slots = width // heads, bias.shape[1] // heads
    pairs, per = heads * 2, n // BLOCK // 2
    ff = shards["gate"].shape[1]
    shards = [shards[m] for m in WEIGHTS]
    count = len(shards)
    padded = -(-(ff // 32) // 16) * 512

    def turned(rows, grouped_rows):
        return low(grouped_rows // 2, 2 * n) if grouped else low(rows, n)

    def low(*shape):
        return jax.ShapeDtypeStruct(shape, bf16)

    def full(*shape):
        return jax.ShapeDtypeStruct(shape, f32)

    outs = [
        low(n, width), full(n, width), low(n, width), full(n, width), full(1, width),
        turned(width, width), turned(width, width), turned(width, width), turned(ff, padded),
        low(n, ff), low(n, ff),
        low(n, width), low(n, width), low(n, width), full(n, heads * slots), full(n, width),
        full(n, width), low(heads, n, n), low(heads, n, n), full(n, heads * slots), full(n, heads * slots),
        low(pairs, per + 1, slots, 2 * head), full(pairs * per, slots, 128),
        low(size, pairs * slots // size, 128),
    ]
    wholes = [low(4 * w.shape[0], w.shape[1]) for w in shards]
    keeps = [
        (2, o.shape[0], n) if grouped and i in SHARED else o.shape for i, o in enumerate(outs)
    ]
    share = pairs * slots // size
    dma = pltpu.SemaphoreType.DMA
    got = pl.pallas_call(
        functools.partial(front_kernel, size, heads, grouped),
        name="front",
        out_shape=outs + wholes[:5],
        in_specs=[in_place()] * count + [in_vmem()] * 7,
        out_specs=[in_place()] * (len(outs) + 5),
        scratch_shapes=[VMEM(shape, o.dtype) for shape, o in zip(keeps, outs)]
        + [VMEM(w.shape, bf16) for w in wholes]
        + [
            VMEM((n, width), bf16),
            VMEM((n, width), bf16),
            VMEM((n, width), f32),
            VMEM((n, width), bf16),
            VMEM((n, width), f32),
            VMEM((n, width), f32),
            VMEM((ff, n), f32),
            VMEM((pairs * per, slots, 2 * head), f32),
            VMEM((pairs * slots, 2 * head + 128), bf16),
            VMEM((size, share, 2 * head + 128), bf16),
            VMEM((size, share, 2 * head), bf16),
            VMEM((pairs * slots, 2 * head), bf16),
            dma((count,)),
            dma((11, len(PARTS))),
            dma((11, len(PARTS))),
            dma((5,)),
            dma((2, size - 1)),
            dma((2, size - 1)),
            dma((RESULTS,)),
            dma((len(SHARED),)),
            dma((len(SHARED),)),
        ],
        compiler_params=pltpu.CompilerParams(
            collective_id=1, has_side_effects=True, vmem_limit_bytes=LIMIT
        ),
    )(*shards, tokens, cotan, pre_gain, post_gain, head_gain, bias, flags)
    return got


def to_row(col):
    n = col.shape[0]
    i = lax.broadcasted_iota(jnp.int32, (n, n), 0)
    j = lax.broadcasted_iota(jnp.int32, (n, n), 1)
    return jnp.sum(jnp.where(i == j, jnp.broadcast_to(col, (n, n)), 0.0), axis=0, keepdims=True)


LEAST, SHALLOW, DEEP = 4.0, 8.0, 12.0
STRIPS = 3
BACK_LIMIT = 63 * 2**20


ROUTES = (("y", "z", "x", "zz"), ("x", "z", "y", "zz"), ("y", "x", "z", "zz"), ("x", "y", "z", "zz"))
STATES = {"x": 1.15, "y": 0.0, "z": 0.5}


def cut(sizes):
    load, plan, last = dict(STATES), [], 1
    for columns, rows in sizes:
        tiles = columns // TILE
        pieces = min(4, 2 * tiles) if tiles <= 4 else 6
        width = columns // pieces if tiles <= 1 else TILE
        out, start = [], 0
        for i in range(pieces):
            count = 1 if tiles <= 1 else tiles // pieces + (1 if i < tiles % pieces else 0)
            size = 2 * 16 * rows * width * count * 2 / 1e6

            def after(route):
                new = dict(load)
                for stage, link in enumerate(ROUTES[route]):
                    new["z" if link == "zz" else link] += size / 2 ** (stage + 1)
                return new

            route = min((1 - last, 3 - last), key=lambda r: sum(v**4 for v in after(r).values()))
            load, last = after(route), route % 2
            out.append((start, width * count, route))
            start += width * count
        plan.append(tuple(out))
    return plan


def in_order(chunks, path, held_back, least, shallow, deep):
    now, free = 0.0, dict.fromkeys(("x", "y", "z", "zz"), 0.0)
    came, done, coming, out = {}, set(), [], []
    path, left = list(path), list(range(len(chunks)))
    rate, delay = 0.04, 4.0

    def leave(c, stage):
        rows, width, order = chunks[c][1], chunks[c][3], chunks[c][4]
        link = ROUTES[order][stage]
        size = 16 * rows * width * 2 / 1e6 / 2 ** (stage + 1)
        free[link] = max(now, free[link]) + size / rate * (2 if stage == 3 else 1)
        coming.append((free[link] + delay, c, stage))

    while left or path or coming:
        here = sorted(a for a in coming if a[0] <= now)
        open_ = [c for c in left if held_back.get(chunks[c][0], None) in done or chunks[c][0] not in held_back]
        depth = deep if "second hop" in done else shallow
        queue = free[ROUTES[chunks[open_[0]][4]][0]] - now if open_ else 0.0
        ready = path and came.get(path[0][2], 0.0 if path[0][2] is None else 1e9) <= now
        if here:
            _, c, stage = here[0]
            coming.remove(here[0])
            now += 0.1 + 0.1 * chunks[c][1] / 32 * chunks[c][3] / TILE / 2**stage
            out.append(("advance", c, stage))
            if stage < 3:
                leave(c, stage + 1)
        elif ready and not (open_ and queue < least):
            name, time, _, starts, takes = path.pop(0)
            now += time
            done.add(name)
            out.append(("path", name, None))
            if starts:
                came[starts] = now + takes
        elif open_ and queue < depth:
            c = open_[0]
            left.remove(c)
            now += 0.1 + 0.3 * chunks[c][1] / 32 * chunks[c][3] / TILE
            out.append(("produce", c, None))
            leave(c, 0)
        else:
            later = [a[0] for a in coming]
            if path and path[0][2] in came:
                later.append(came[path[0][2]])
            if open_:
                later.append(now + queue - depth)
            now = max(now + 0.05, min(later))
    return out


FORM = (("cotan", 0), ("gate", 1), ("up", 1), ("attn", 2), ("outgate", 3), ("query", 3), ("key", 3), ("value", 3), ("forget", 3))
SAVED = ("q", "k", "v", "pre", "logits", "mixed", "aff", "mixing", "weights", "inner", "state", "pass", "mdelta", "pass_all")


def back_kernel(size, heads, plan, *refs):
    def take(count):
        nonlocal refs
        got, refs = refs[:count], refs[count:]
        return got

    lefts, rights, saved = take(4), take(4), dict(zip(SAVED, take(len(SAVED))))
    weights, (first_in, tokens_in) = take(5), take(2)
    bias_ref, flag_ref, head_gain, pre_gain, postgain_ref = take(5)
    outs, (vec_out, input_grad) = take(9), take(2)
    left_all, right_all = take(4), take(9)
    have_ref = dict(zip(SAVED, take(len(SAVED))))
    chunks = [(g, p[2]) + c for g, p in enumerate(plan) for c in p[4]]
    nc = len(chunks)
    sums = take(nc)
    landed = [take(nc) for _ in range(4)]
    owed, da_acc, doma_acc, strip, going, gathered, prefix, came, vec_acc, vec_got = take(10)
    loads, in_local, in_send, in_recv, strip_sem, first_sem = take(6)
    hop_send, hop_recv, st_send, st_recv, v_send, v_recv = take(6)
    q_ref, k_ref, v_ref = have_ref["q"], have_ref["k"], have_ref["v"]
    logit_ref, mixed_ref, mdelta_ref = have_ref["logits"], have_ref["mixed"], have_ref["mdelta"]
    state_ref, pass_ref = have_ref["state"], have_ref["pass"]

    s, f = lax.axis_index("seq"), lax.axis_index("fsdp")
    core, y = lax.rem(f, 2), f // 2
    x, z_low, z_high = lax.rem(s, 2), lax.rem(s // 2, 2), lax.rem(s // 4, 2)
    sib, far, nx, nz, nzz = (s, f ^ 1), (s, f ^ 2), (s ^ 1, f), (s ^ 2, f), (s ^ 4, f)
    others = [(lax.rem(s + d, size), f) for d in range(1, size)]
    greet([sib, far] + others)
    started = []

    def go(copy):
        copy.start()
        started.append(copy)

    n, width = q_ref.shape
    head = width // heads
    slots = bias_ref.shape[1] // heads
    blocks = n // BLOCK
    streams = 2
    per = blocks // streams
    pairs = heads * streams
    scale = head ** (-0.5)
    share = pairs * slots // size

    waiting = {}

    def fetch_left(i):
        if len(lefts[i].shape) == 2:
            keep = pltpu.make_async_copy(lefts[i], left_all[i], in_local.at[i])
            keep.start()
            waiting["left", i] = [keep, None]
            return
        keep = pltpu.make_async_copy(lefts[i].at[core], left_all[i].at[:, pl.ds(0, n)], in_local.at[i])
        keep.start()
        copy = remote(lefts[i].at[1 - core], left_all[i].at[:, pl.ds(n, n)], (in_send, in_recv), i, sib)
        go(copy)
        waiting["left", i] = [keep, copy]

    def fetch_right(i):
        own, other = right_all[i].at[pl.ds(0, n)], right_all[i].at[pl.ds(n, n)]
        keep = None
        src = own
        if i < 4:
            src = rights[i]
            keep = pltpu.make_async_copy(src, own, in_local.at[4 + i])
            keep.start()
        copy = remote(src, other, (in_send, in_recv), 4 + i, sib)
        go(copy)
        waiting["right", i] = [keep, copy]

    def have(kind, i):
        pair = waiting[kind, i]
        if pair:
            if pair[0] is not None:
                pair[0].wait()
            if pair[1] is not None:
                pair[1].wait_recv()
            waiting[kind, i] = None

    fetch_left(0)
    fetch_right(0)
    loading = []
    for i, name in enumerate(SAVED):
        copy = pltpu.make_async_copy(saved[name], have_ref[name], loads.at[i])
        copy.start()
        loading.append(copy)
    for i in (1, 2, 3):
        fetch_right(i)
    for i in (1, 2, 3):
        fetch_left(i)

    strips = [(w, t * TILE) for w in range(5) for t in range(weights[w].shape[1] // TILE)]

    def strip_copy(i):
        w, at = strips[i]
        return pltpu.make_async_copy(weights[w].at[:, pl.ds(at, TILE)], strip.at[i % STRIPS], strip_sem.at[i % STRIPS])

    for i in range(STRIPS):
        strip_copy(i).start()

    def route(c):
        names = ROUTES[chunks[c][4]]
        places, partners = dict(x=x, y=y, z=z_low, zz=z_high), dict(x=nx, y=far, z=nz, zz=nzz)
        return tuple(places[i] for i in names), tuple(partners[i] for i in names)

    def stage_copy(c, stage):
        bits, partners = route(c)
        at = bits[:stage] + (1 - bits[stage],)
        return remote(sums[c].at[at], landed[stage][c], (st_send, st_recv), (stage, c), partners[stage])

    def produce(c):
        g, rows, start, wide, order = chunks[c]
        left = plan[g][0]
        have("left", left)
        have("right", g)
        tile = min(TILE, wide)

        def turn(i, carry):
            at = pl.multiple_of(start + i * tile, 128)
            to = pl.multiple_of(i * tile, 128)
            got = jnp.dot(
                left_all[left][...], right_all[g][:, pl.ds(at, tile)], preferred_element_type=f32
            ).astype(bf16)
            for group in range(16):
                bits = dict(zz=group >> 3 & 1, z=group >> 2 & 1, x=group >> 1 & 1, y=group & 1)
                place = tuple(bits[i] for i in ROUTES[order])
                sums[c][*place, :, pl.ds(to, tile)] = got[group * rows : (group + 1) * rows]
            return carry

        lax.fori_loop(0, wide // tile, turn, 0)
        go(stage_copy(c, 0))

    def advance(c, stage):
        stage_copy(c, stage).wait_recv()
        bits, _ = route(c)
        if stage == 3:
            g, rows, start, wide, _ = chunks[c]
            total = sums[c][bits].astype(f32) + landed[3][c][...].astype(f32)
            outs[g][:, start : start + wide] = total[: plan[g][3]]
            return
        for rest in range(1 << (3 - stage)):
            tail = tuple((rest >> k) & 1 for k in reversed(range(3 - stage)))
            at = bits[: stage + 1] + tail
            sums[c][at] = (sums[c][at].astype(f32) + landed[stage][c][tail].astype(f32)).astype(bf16)
        go(stage_copy(c, stage + 1))

    keep = {}

    def begin():
        for copy in loading:
            copy.wait()
        lower, linked, fresh, ending, unbroken = mask_set(flag_ref[...])
        z, u, oma, growth, inverse, tail = gate_set(have_ref["pre"][...], bias_ref[...], lower, ending)
        keep.update(lower=lower, linked=linked, fresh=fresh, z=z, u=u, oma=oma, growth=growth)
        keep.update(inverse=inverse, tail=tail, shrink=inverse * oma, kept=tail * oma)
        keep["gain"] = jnp.zeros((1, head), f32)

    def states(h, b):
        return state_ref.at[h * streams + b // per, b % per]

    def one_head(h):
        linked, fresh, growth, shrink = keep["linked"], keep["fresh"], keep["growth"], keep["shrink"]
        hs, hd = slice(h * slots, (h + 1) * slots), slice(h * head, (h + 1) * head)
        mixed, logits, delta = mixed_ref[:, hd], logit_ref[:, hd], mdelta_ref[:, hd]
        r = lax.rsqrt(jnp.mean(mixed * mixed, axis=1, keepdims=True) + norm_eps)
        sig = sigmoid(logits)
        silu = logits * sig
        unit = mixed * r
        dy = delta * silu
        right_all[4][0:n, hd] = (delta * unit * head_gain[...] * (sig + silu * (1.0 - sig))).astype(bf16)
        keep["gain"] = keep["gain"] + jnp.sum(dy * unit, axis=0, keepdims=True)
        dy = dy * head_gain[...]
        dmixed = r * (dy - unit * jnp.mean(unit * dy, axis=1, keepdims=True))
        gr, sh = growth[:, hs], shrink[:, hs].astype(bf16)
        weigh, inner = have_ref["weights"][:, hs], have_ref["inner"][:, hs]
        aff, mixing = have_ref["aff"][h], have_ref["mixing"][h]
        qh, kh, vh = q_ref[:, hd], k_ref[:, hd], v_ref[:, hd]
        do = dmixed.astype(bf16)
        lifted = (weigh * gr).astype(bf16)
        dm = (dot(do, vh, 1, 1) * linked).astype(bf16)
        mixed_ref[:, hd] = dot(mixing, do, 0, 0)
        fdo = (dmixed * fresh).astype(bf16)
        dlift = dot(dm, sh) + jnp.concatenate(
            [dot(fdo[rows_of(b)], states(h, b)[:, head:], 1, 1) for b in range(blocks)], axis=0
        )
        dsh = dot(dm, lifted, 0, 0)
        dw = dlift * gr
        dsc = weigh * (dw - jnp.sum(weigh * dw, axis=1, keepdims=True))
        du = dsc * gr
        du_low = du.astype(bf16)
        da = (dot(du_low, sh, 1, 1) * (linked * scale)).astype(bf16)
        dsh = dsh + dot(aff, du_low, 0, 0)
        fdu = (du * (fresh * scale)).astype(bf16)
        right_all[5][0:n, hd] = (
            dot(da, kh)
            + jnp.concatenate([dot(fdu[rows_of(b)], states(h, b)[:, :head]) for b in range(blocks)], axis=0)
        ).astype(bf16)
        mdelta_ref[:, hd] = dot(da, qh, 0, 0)
        for stream in range(streams):
            pair = h * streams + stream
            total = None
            for b in reversed(range(stream * per, (stream + 1) * per)):
                at = pair * per + b % per
                own_k = dot(fdu[rows_of(b)], qh[rows_of(b)], 0, 0)
                own_v = dot(lifted[rows_of(b)], fdo[rows_of(b)], 0, 0)
                owed[at, :, :head] = own_k.astype(bf16)
                owed[at, :, head:] = own_v.astype(bf16)
                if total is not None:
                    factor = pass_ref[at][:, :1]
                    own_k, own_v = own_k + factor * total[0], own_v + factor * total[1]
                total = (own_k, own_v)
            at = slice(pair * slots, (pair + 1) * slots)
            going[at, :head] = total[0].astype(bf16)
            going[at, head:] = total[1].astype(bf16)
        da_acc[:, hs] = lifted.astype(f32) * dlift + du_low.astype(f32) * inner - dsh * sh.astype(f32)
        doma_acc[:, hs] = dsh * keep["inverse"][:, hs]

    def rows_for(place):
        return pl.ds(pl.multiple_of(place * share, 16), share)

    sources = [lax.rem(s + size - d, size) for d in range(1, size)]

    def first_hop():
        for d in range(1, size):
            to = others[d - 1]
            go(remote(going.at[rows_for(to[0])], gathered.at[s], (hop_send, hop_recv), (0, d - 1), to))
        gathered[s] = going[rows_for(s)]
        fetch_right(4)
        fetch_right(5)

    def second_hop():
        for d in range(1, size):
            part = gathered.at[sources[d - 1]]
            remote(part, part, (hop_send, hop_recv), (0, d - 1), sib).wait_recv()
        state = jnp.zeros((share, 2 * head), f32)
        for place in reversed(range(size)):
            prefix[place] = state.astype(bf16)
            state = have_ref["pass_all"][place][:, :1].astype(f32) * state + gathered[place].astype(f32)
        for d in range(1, size):
            to = others[d - 1]
            go(remote(prefix.at[to[0]], came.at[rows_for(s)], (hop_send, hop_recv), (1, d - 1), to))
        came[rows_for(s)] = prefix[s]

    def last_hop():
        for d in range(1, size):
            part = came.at[rows_for(sources[d - 1])]
            remote(part, part, (hop_send, hop_recv), (1, d - 1), sib).wait_recv()

    def end_head(h):
        kept, tail = keep["kept"], keep["tail"]
        row = lax.broadcasted_iota(jnp.int32, (BLOCK, 1), 0)
        hs, hd = slice(h * slots, (h + 1) * slots), slice(h * head, (h + 1) * head)
        for stream in range(streams):
            pair = h * streams + stream
            leaving = came[pair * slots : (pair + 1) * slots].astype(f32)
            for i in reversed(range(per)):
                at, rb = pair * per + i, rows_of(stream * per + i)
                low = leaving.astype(bf16)
                part = kept[rb, hs].astype(bf16)
                dkept = dot(k_ref[rb, hd], low[:, :head], 1, 1) + dot(v_ref[rb, hd], low[:, head:], 1, 1)
                right_all[6][rb, hd] = (mdelta_ref[rb, hd] + dot(part, low[:, :head])).astype(bf16)
                right_all[7][rb, hd] = (mixed_ref[rb, hd] + dot(part, low[:, head:])).astype(bf16)
                held = jnp.sum(low.astype(f32) * state_ref[pair, i + 1].astype(f32), axis=1, keepdims=True)
                da_acc[rb, hs] = (
                    da_acc[rb, hs] - dkept * part.astype(f32) + jnp.where(row == BLOCK - 1, to_row(held), 0.0)
                )
                doma_acc[rb, hs] = doma_acc[rb, hs] + dkept * tail[rb, hs]
                if i > 0:
                    leaving = owed[at].astype(f32) + pass_ref[at][:, :1] * leaving

    def end_gates():
        fetch_right(6)
        fetch_right(7)
        z, u = keep["z"], keep["u"]
        dg = dot(keep["lower"], da_acc[...], 0, 0, count=3) - doma_acc[...] * (1.0 - keep["oma"])
        sig = jnp.where(z >= 0.0, u / (1.0 + u), 1.0 / (1.0 + u))
        dpre = dg * sig * 0.125
        right_all[8][0:n] = dpre.astype(bf16)
        fetch_right(8)
        pltpu.make_async_copy(first_in, mdelta_ref, first_sem.at[0]).start()
        pltpu.make_async_copy(tokens_in, q_ref, first_sem.at[1]).start()
        vec_acc[0] = jnp.zeros(vec_acc.shape[1:], f32)
        vec_acc[0, 1:2, : dpre.shape[1]] = jnp.sum(dpre, axis=0, keepdims=True)
        vec_acc[0, 2:3, :head] = keep["gain"]
        vec_acc[0, 3:4, :] = postgain_ref[...]

    def strip_step(i):
        strip_copy(i).wait()
        w, at = strips[i]
        term = dot(right_all[(6, 7, 8, 5, 4)[w]][0:n, at : at + TILE], strip[i % STRIPS], 1, 1)
        logit_ref[...] = term if i == 0 else logit_ref[...] + term
        if i + STRIPS < len(strips):
            strip_copy(i + STRIPS).start()

    def end_norm():
        pltpu.make_async_copy(first_in, mdelta_ref, first_sem.at[0]).wait()
        pltpu.make_async_copy(tokens_in, q_ref, first_sem.at[1]).wait()
        inputs = q_ref[...].astype(f32)
        r = lax.rsqrt(jnp.mean(inputs * inputs, axis=1, keepdims=True) + norm_eps)
        unit = inputs * r
        delta = logit_ref[...]
        vec_acc[0, 0:1, :] = jnp.sum(delta * unit, axis=0, keepdims=True)
        delta = delta * pre_gain[...]
        input_grad[...] = (
            mdelta_ref[...] + r * (delta - unit * jnp.mean(unit * delta, axis=1, keepdims=True))
        ).astype(bf16)
        go(v_copy(0))

    def v_copy(i):
        return remote(vec_acc.at[i], vec_got.at[i], (v_send, v_recv), i, (sib, far, nx, nz, nzz)[i])

    def vector(i):
        v_copy(i).wait_recv()
        total = vec_acc[i] + vec_got[i]
        if i == 4:
            vec_out[...] = total
            return
        vec_acc[i + 1] = total
        go(v_copy(i + 1))

    steps = {"begin": begin}
    path = [("begin", 2.0, None, None, 0)]
    for h in range(heads):
        steps["head", h] = functools.partial(one_head, h)
        path.append((("head", h), 3.0, None, None, 0))
    steps.update({"first hop": first_hop, "second hop": second_hop, "last hop": last_hop})
    path.append(("first hop", 0.5, None, "first", 12.0))
    path.append(("second hop", 1.0, "first", "second", 12.0))
    path.append(("last hop", 0.1, "second", None, 0))
    for h in range(heads):
        steps["end", h] = functools.partial(end_head, h)
        path.append((("end", h), 1.2, None, None, 0))
    steps["gates"] = end_gates
    path.append(("gates", 1.0, None, None, 0))
    for i in range(len(strips)):
        steps["strip", i] = functools.partial(strip_step, i)
        path.append((("strip", i), 0.4, None, None, 0))
    steps["norm"] = end_norm
    path.append(("norm", 1.5, None, ("vector", 0), 3.0))
    for i in range(5):
        steps["vector", i] = functools.partial(vector, i)
        path.append((("vector", i), 0.1, ("vector", i), ("vector", i + 1), 4.0))
    held_back = {4: "first hop", 5: "first hop", 6: "gates", 7: "gates", 8: "gates"}
    for what, which, stage in in_order(chunks, path, held_back, LEAST, SHALLOW, DEEP):
        if what == "path":
            steps[which]()
        elif what == "produce":
            produce(which)
        else:
            advance(which, stage)
    for copy in started:
        copy.wait_send()


def back(size, heads, plan, lefts, rights, saved, weights, first, tokens, bias, flags, head_gain, pre_gain, postgain):
    n, width = saved["q"].shape
    head, slots = width // heads, bias.shape[1] // heads
    pairs, per = heads * 2, n // BLOCK // 2
    share = pairs * slots // size
    chunks = [(p[2],) + c for p in plan for c in p[4]]
    nc = len(chunks)
    dma = pltpu.SemaphoreType.DMA
    saved = [saved[name] for name in SAVED]
    scratch = [VMEM((a.shape[-2], 2 * n), bf16) for a in lefts]
    scratch += [VMEM((2 * n, p[1]), bf16) for p in plan]
    scratch += [VMEM(a.shape, a.dtype) for a in saved]
    for lead in ((2, 2, 2, 2), (2, 2, 2), (2, 2), (2,), ()):
        scratch += [VMEM(lead + (r, w), bf16) for r, _, w, _ in chunks]
    scratch += [
        VMEM((pairs * per, slots, 2 * head), bf16),
        VMEM((n, heads * slots), f32),
        VMEM((n, heads * slots), f32),
        VMEM((STRIPS, width, TILE), bf16),
        VMEM((pairs * slots, 2 * head), bf16),
        VMEM((size, share, 2 * head), bf16),
        VMEM((size, share, 2 * head), bf16),
        VMEM((pairs * slots, 2 * head), bf16),
        VMEM((5, 8, width), f32),
        VMEM((5, 8, width), f32),
        dma((len(SAVED),)),
        dma((8,)),
        dma((13,)),
        dma((13,)),
        dma((STRIPS,)),
        dma((2,)),
        dma((2, size - 1)),
        dma((2, size - 1)),
        dma((4, nc)),
        dma((4, nc)),
        dma((5,)),
        dma((5,)),
    ]
    out = pl.pallas_call(
        functools.partial(back_kernel, size, heads, plan),
        name="back",
        out_shape=[jax.ShapeDtypeStruct((p[3], p[1]), f32) for p in plan]
        + [jax.ShapeDtypeStruct((8, width), f32), jax.ShapeDtypeStruct((n, width), bf16)],
        in_specs=[in_place()] * (8 + len(saved) + 7) + [in_vmem()] * 5,
        out_specs=[in_vmem()] * (len(plan) + 2),
        scratch_shapes=scratch,
        compiler_params=pltpu.CompilerParams(
            collective_id=2, has_side_effects=True, vmem_limit_bytes=BACK_LIMIT
        ),
    )(*lefts, *rights, *saved, *weights, first, tokens, bias, flags, head_gain, pre_gain, postgain)
    return out[: len(plan)], out[-2], out[-1]


def finish_kernel(count, *refs):
    vectors, outs = refs[count], refs[count + 1 :]
    for i in range(count):
        outs[i][...] = refs[i][...]
    for i, out in enumerate(outs[count:]):
        out[...] = vectors[i, : out.shape[0]]


def finish(arrays, vectors, sizes):
    count = len(arrays)
    return pl.pallas_call(
        functools.partial(finish_kernel, count),
        name="finish",
        out_shape=[jax.ShapeDtypeStruct(a.shape, a.dtype) for a in arrays]
        + [jax.ShapeDtypeStruct((size,), f32) for size in sizes],
        in_specs=[in_vmem()] * (count + 1),
        out_specs=[in_vmem()] * (count + len(sizes)),
        compiler_params=pltpu.CompilerParams(vmem_limit_bytes=LIMIT),
    )(*arrays, vectors)


def by_owner(a, hi, lo):
    features, tokens = a.shape
    r = features // (hi * lo * 4)
    t = a.reshape(hi, lo, 2, 2, r, tokens).transpose(3, 1, 2, 0, 4, 5).reshape(2, lo * 2, hi * r, tokens)
    pad = -(hi * r) % 16
    if pad:
        t = jnp.pad(t, ((0, 0), (0, 0), (0, pad), (0, 0)))
    return t.reshape(2, -1, tokens)


def body(
    size, tokens, resets, pre_gain, query_weight, key_weight, value_weight, forget_weight, forget_bias,
    outgate_weight, output_weight, head_gain, post_gain, gate_weight, up_weight, down_weight, cotangent,
):
    lo = 8
    hi = size // lo
    streams, length, width = tokens.shape
    n = streams * length
    head = head_gain.shape[0]
    heads = width // head
    shards = {
        "query": query_weight, "key": key_weight, "value": value_weight, "forget": forget_weight,
        "outgate": outgate_weight, "output": output_weight, "gate": gate_weight, "up": up_weight, "down": down_weight,
    }
    ff = gate_weight.shape[1]
    flat, cotan = tokens.reshape(n, width), cotangent.reshape(n, width)
    bias, gain = forget_bias[None], head_gain[None]
    (
        block_output, first_delta, attn_delta, merged_delta, postgain_grad,
        normed_t, merged_t, second_t, hidden_t, gate_delta, up_delta,
        q, k, v, pre, logits, mixed, aff, mixing, weights, inner, state, passed, pass_all, *wholes,
    ) = front(
        size, heads, hi == 1, shards, flat, cotan, pre_gain[None], post_gain[None],
        gain, bias, resets,
    )
    lefts = [hidden_t, second_t, merged_t, normed_t]
    if hi > 1:
        lefts = [by_owner(a, hi, lo) for a in lefts]
    rights = [cotan, gate_delta, up_delta, attn_delta]
    columns = (width, ff, ff, width, width, width, width, width, bias.shape[1])
    kept_rows = [(ff if i == 0 else width) // (lo * 4) for i in range(len(FORM))]
    padded = [-(-r // 16) * 16 for r in kept_rows]
    pieces = cut(tuple(zip(columns, padded)))
    plan = [(left, columns[i], padded[i], kept_rows[i], pieces[i]) for i, (_, left) in enumerate(FORM)]
    saved = dict(
        q=q, k=k, v=v, pre=pre, logits=logits, mixed=mixed, aff=aff, mixing=mixing, weights=weights, inner=inner,
        state=state, mdelta=merged_delta, pass_all=pass_all,
    )
    saved["pass"] = passed
    grads, vectors, input_grad = back(
        size, heads, tuple(plan), lefts, rights, saved, wholes, first_delta, flat, bias, resets, gain,
        pre_gain[None], postgain_grad,
    )
    if hi > 1:
        alike = [[a * lo + b for a in range(hi)] for b in range(lo)]
        grads = [
            lax.psum_scatter(g, "seq", scatter_dimension=0, axis_index_groups=alike, tiled=True)
            for g in grads
        ]
        vectors = lax.psum(vectors, "seq", axis_index_groups=alike)
    down_grad, gate_grad, up_grad, output_grad, outgate_grad, query_grad, key_grad, value_grad, forget_grad = grads
    shape = tokens.shape
    got = finish(
        (
            block_output, input_grad, query_grad, key_grad, value_grad, forget_grad, outgate_grad, output_grad,
            gate_grad, up_grad, down_grad,
        ), vectors, (width, bias.shape[1], head, width),
    )
    pregain, bias_total, headgain, postgain = got[11:]
    return (
        got[0].reshape(shape), got[1].reshape(shape), pregain, *got[2:6], bias_total, *got[6:8], headgain,
        postgain, *got[8:11],
    )


def solution(mesh):
    rows, whole, both = P("fsdp", None), P(), P(("seq", "fsdp"), None)
    return jax.shard_map(
        functools.partial(body, mesh.shape["seq"]),
        mesh=mesh,
        in_specs=(
            P("fsdp", "seq", None), P("fsdp", "seq"), whole, rows, rows, rows, rows, whole, rows, rows,
            whole, whole, rows, rows, rows, P("fsdp", "seq", None),
        ),
        out_specs=(
            P("fsdp", "seq", None), P("fsdp", "seq", None), whole, both, both, both, both, whole, both,
            both, whole, whole, both, both, both,
        ),
        check_vma=False,
    )
```
